256 devices in a mesh: dp: 64 (over x, z, core), tensor: 4 (over y).
Axes of the slice: x: 4, y: 4, z: 8, core: 2. Of those that a mesh axis runs over, the one named last changes fastest.
Arguments:
- patches: bfloat16 [24576, 1408], P('dp', 'tensor'), may hold values from -6 to 6
- seg_ids: int32 [16384], P('dp'), may hold values from 0 to 16383, as said below
- cut: int32 [64, 2], P('dp'), may hold values from -64 to 64, as said below
- w_qkv: bfloat16 [3, 704, 1408], P(None, 'tensor'), may hold values from -0.15625 to 0.15625
- w_out: bfloat16 [704, 1408], P('tensor'), may hold values from -0.21875 to 0.21875
- grad_out: bfloat16 [16384, 1408], P('dp', 'tensor'), may hold values from -6 to 6
Outputs:
- mixed: bfloat16 [16384, 1408], P('dp', 'tensor')
- grad_patches: bfloat16 [24576, 1408], P('dp', 'tensor')
- grad_w_qkv: float32 [3, 704, 1408], P(None, 'tensor', 'dp')
- grad_w_out: float32 [704, 1408], P('tensor', 'dp')
The draws below stay inside these ranges and needn't reach their ends.
Inputs may be any that keep to these rules, and one draw needn't show every extreme that they name: Source block i holds, from its row 0 and in order, the packed rows 256 i + cut[i,0] up to 256 (i + 1) + cut[i,1] - 1. cut[i,1] equals cut[i+1,0]; the first block's cut[.,0] and the last block's cut[.,1] are 0. In every draw one sequence takes 64 rows from each of its two neighbouring blocks. seg_ids[r] is the packed index of the first row of r's image; an image lies within one sequence and within one source block, and seg_ids never falls. The last packed row is an image of its own.
All inputs are finite; a program needn't handle non-finite values.
Results may differ from the reference program's by a relative error of at most 0.0093.
Values may be sent and summed in bfloat16 or wider, within the bound.
A program may use at most 64 MiB of HBM per device.

```python
import math
import jax
import jax.numpy as jnp
from jax import lax

D = 1408
HD = 88
HEADS = 8
SEQ = 256
SPILL = 64
QD = 704
TOKENS = 16384
SOURCE_ROWS = 24576
N_TENSOR = 4


def shared_edges(key):
    seq_count = TOKENS // SEQ
    edge_key = jax.random.fold_in(key, 71)
    first_key, second_key, sign_key = jax.random.split(edge_key, 3)
    magnitude = jax.random.randint(first_key, (seq_count + 1,), 3 * SPILL // 4, SPILL + 1, dtype=jnp.int32)
    flips = jax.random.randint(sign_key, (seq_count + 1,), 0, 2, dtype=jnp.int32)
    edges = jnp.where(flips == 1, magnitude, -magnitude)
    place = jnp.arange(seq_count + 1, dtype=jnp.int32)
    chosen = jax.random.randint(second_key, (), 1, seq_count - 1, dtype=jnp.int32)
    edges = jnp.where((place == 0) | (place == seq_count), 0, edges)
    edges = jnp.where(place == chosen, SPILL, jnp.where(place == chosen + 1, -SPILL, edges))
    return edges.astype(jnp.int32)


def draw_cut(key, part):
    edges = shared_edges(key)
    return jnp.stack([edges[:-1], edges[1:]], axis=1).astype(jnp.int32)


def draw_seg_ids(key, part):
    edges = shared_edges(key)
    key = jax.random.fold_in(key, 9)
    packed_index = jnp.arange(TOKENS, dtype=jnp.int32)
    local_row = packed_index % SEQ
    owner = packed_index // SEQ
    head_rows = jnp.maximum(edges[owner], 0)
    tail_rows = jnp.maximum(-edges[owner + 1], 0)
    chance = jax.random.randint(key, (TOKENS,), 0, 96, dtype=jnp.int32)
    begins = (local_row == 0) | (local_row == head_rows) | (local_row == SEQ - tail_rows) | (chance == 0) | (packed_index == TOKENS - 1)
    marks = jnp.where(begins, packed_index, 0)
    return lax.cummax(marks, axis=0).astype(jnp.int32)


def steps_of(own_key, extent, pieces, low, largest):
    gain, own = 1.0, jax.random.fold_in(own_key, 6)
    for position, parts in pieces:
        draws = jnp.exp(jax.random.uniform(jax.random.fold_in(own, position), (parts,), jnp.float32, low / len(pieces), largest / len(pieces)))
        gain = gain * jnp.repeat(draws, extent[position] // parts).reshape([-1 if axis == position else 1 for axis in range(len(extent))])
    return gain


def scatter_about(rng, dims, scale, bound, cuts=(), kind=jnp.bfloat16):
    entries = jax.random.normal(rng, dims, jnp.float32) * scale
    if len(cuts) > 0:
        entries = steps_of(rng, dims, cuts, -0.22, 0.18) * entries
    return jnp.clip(entries, min=-bound, max=bound).astype(kind)


def setup_inputs(seed: int = 0) -> dict:
    seeds = jax.random.split(jax.random.key(seed), 7)
    return {
        "patches": scatter_about(seeds[0], (SOURCE_ROWS, D), 1.0, 6.0, ((0, 64), (1, 4))),
        "seg_ids": draw_seg_ids(jax.random.fold_in(seeds[6], 71), 0),
        "cut": draw_cut(jax.random.fold_in(seeds[6], 71), 0),
        "w_qkv": scatter_about(seeds[3], (3, QD, D), D ** -0.5, 0.15625, ((1, 4),)),
        "w_out": scatter_about(seeds[4], (QD, D), QD ** -0.5, 0.21875, ((0, 4),)),
        "grad_out": scatter_about(seeds[5], (TOKENS, D), 1.0, 6.0, ((0, 64), (1, 4))),
    }


norm_eps = 1e-06

def row_norm(values):
    center = values - lax.optimization_barrier(jnp.mean(values, axis=-1, keepdims=True))
    spread = lax.optimization_barrier(jnp.mean(center * center, axis=-1, keepdims=True))
    inverse = lax.rsqrt(spread + norm_eps)
    return (center * inverse, inverse)

def norm_back(upstream, normed, inverse):
    first_mean = lax.optimization_barrier(jnp.mean(upstream, axis=-1, keepdims=True))
    second_mean = lax.optimization_barrier(jnp.mean(upstream * normed, axis=-1, keepdims=True))
    return inverse * (upstream - first_mean - normed * second_mean)

def rounded(values):
    return lax.optimization_barrier(values.astype(jnp.bfloat16)).astype(jnp.float32)

def reference(patches, seg_ids, cut, w_qkv, w_out, grad_out):
    seq_count = TOKENS // SEQ
    src_rows = SEQ + 2 * SPILL
    group_count = N_TENSOR
    score_scale = HD ** (-0.5)
    starts = SEQ * jnp.arange(seq_count, dtype=jnp.int32) + cut[:, 0]
    lengths = SEQ + cut[:, 1] - cut[:, 0]
    packed_index = jnp.arange(TOKENS, dtype=jnp.int32)
    owner = (jnp.searchsorted(starts, packed_index, side='right') - 1).astype(jnp.int32)
    source_index = owner * src_rows + packed_index - starts[owner]
    packed_rows = patches[source_index]
    qkv_flat = w_qkv.reshape(3 * QD, D)

    def sequence_pass(totals, block_args):
        qkv_total, out_total = totals
        patch_rows, image_ids, grad_rows = block_args
        normed, inverse = row_norm(patch_rows.astype(jnp.float32))
        normed_low = normed.astype(jnp.bfloat16)
        projected = jnp.dot(normed_low, qkv_flat.T, preferred_element_type=jnp.float32).reshape(SEQ, 3, HEADS, HD)
        query_hat, query_inverse = row_norm(projected[:, 0])
        key_hat, key_inverse = row_norm(projected[:, 1])
        queries = rounded(query_hat)
        key_rows = rounded(key_hat)
        values = rounded(projected[:, 2])
        same_image = (image_ids[:, None] == image_ids[None, :])[None]
        scores = jnp.einsum('qhe,khe->hqk', queries, key_rows) * score_scale
        raised = jnp.where(same_image, jnp.exp(scores), 0.0)
        weights = raised / lax.optimization_barrier(jnp.sum(raised, axis=-1, keepdims=True))
        weights_low = rounded(weights)
        attended = lax.optimization_barrier(jnp.einsum('hqk,khe->qhe', weights_low, values).astype(jnp.bfloat16).reshape(SEQ, QD))
        group_terms = jnp.einsum('rgq,gqd->grd', attended.reshape(SEQ, group_count, -1).astype(jnp.float32), w_out.reshape(group_count, -1, D).astype(jnp.float32))
        branch = lax.optimization_barrier(jnp.sum(rounded(group_terms), axis=0))
        mixed = (patch_rows.astype(jnp.float32) + branch).astype(jnp.bfloat16)
        grad_att = jnp.dot(grad_rows, w_out.T, preferred_element_type=jnp.float32)
        out_total = out_total + jnp.dot(attended.T, grad_rows, preferred_element_type=jnp.float32)
        grad_block = rounded(grad_att).reshape(SEQ, HEADS, HD)
        grad_weights = jnp.einsum('qhe,khe->hqk', grad_block, values)
        inner_sum = lax.optimization_barrier(jnp.sum(grad_weights * weights, axis=-1, keepdims=True))
        grad_scores = rounded(weights * (grad_weights - inner_sum) * score_scale)
        grad_query = jnp.einsum('hqk,khe->qhe', grad_scores, key_rows)
        grad_key = jnp.einsum('hqk,qhe->khe', grad_scores, queries)
        grad_value = jnp.einsum('hqk,qhe->khe', weights_low, grad_block)
        grad_proj = lax.optimization_barrier(jnp.stack([norm_back(grad_query, query_hat, query_inverse), norm_back(grad_key, key_hat, key_inverse), grad_value], axis=1).astype(jnp.bfloat16))
        qkv_total = qkv_total + jnp.dot(grad_proj.reshape(SEQ, 3 * QD).T, normed_low, preferred_element_type=jnp.float32).reshape(3, QD, D)
        input_terms = jnp.einsum('rcgq,cgqd->grd', grad_proj.astype(jnp.float32).reshape(SEQ, 3, group_count, -1), w_qkv.astype(jnp.float32).reshape(3, group_count, -1, D))
        input_sum = lax.optimization_barrier(jnp.sum(rounded(input_terms), axis=0))
        grad_x = (grad_rows.astype(jnp.float32) + norm_back(input_sum, normed, inverse)).astype(jnp.bfloat16)
        return ((qkv_total, out_total), (mixed, grad_x))
    zero_qkv = jnp.zeros((3, QD, D), jnp.float32)
    zero_out = jnp.zeros((QD, D), jnp.float32)
    sweep_args = (packed_rows.reshape(seq_count, SEQ, D), seg_ids.reshape(seq_count, SEQ), grad_out.reshape(seq_count, SEQ, D))
    (qkv_total, out_total), (mixed, grad_x) = lax.scan(sequence_pass, (zero_qkv, zero_out), sweep_args)
    mixed = mixed.reshape(TOKENS, D)
    grad_x = grad_x.reshape(TOKENS, D)
    local_row = jnp.arange(src_rows, dtype=jnp.int32)
    back_index = jnp.clip(starts[:, None] + local_row[None, :], 0, TOKENS - 1)
    live_rows = local_row[None, :] < lengths[:, None]
    grad_patches = jnp.where(live_rows[:, :, None], grad_x[back_index], jnp.zeros((), grad_x.dtype)).reshape(seq_count * src_rows, D)
    total_scale = 1.0 / math.sqrt(TOKENS)
    return (mixed, grad_patches, qkv_total * total_scale, out_total * total_scale)
```

```python
import math

import jax
import jax.numpy as jnp
from jax import lax
from jax.experimental import pallas as pl
from jax.experimental.pallas import tpu as pltpu
from jax.sharding import PartitionSpec as P

HD = 88
PAD = 128
SEQ = 256
SRC = 384
SPILL = 64
COLS = 352
MODEL = 1408
QW = 176
HALF = 384
NT = 4
NX = 4
NZ = 8
SHARE = 22
CORE_ROWS = 24
norm_eps = 1e-06
score_scale = HD ** (-0.5)
total_scale = 1.0 / math.sqrt(16384.0)

BF = jnp.bfloat16
F32 = jnp.float32
MESH = pl.DeviceIdType.MESH


def dot(a, b, ca=1, cb=0):
    return lax.dot_general(a, b, (((ca,), (cb,)), ((), ())), preferred_element_type=F32)


def grid2(rows, cols):
    r = lax.broadcasted_iota(jnp.int32, (rows, cols), 0)
    c = lax.broadcasted_iota(jnp.int32, (rows, cols), 1)
    return r, c


def hot(mask):
    return jnp.where(mask, 1.0, 0.0).astype(BF)


def kernel(
    cut_ref, seg_ref, patches_ref, wqkv_ref, wout_ref, gout_ref,
    mixed_ref, gpatch_ref, gqkv_ref, gwout_ref,
    go_full, x_full, n_low, n_t, go_t, w_pad, wo_pad,
    snd_next, from_prev, from_next, bsnd_next, bfrom_prev, bfrom_next, gx,
    rs_send, rs_rin, rs_fin, share, right_side, h_send, h_recv, h_keep,
    xs_send, xs_rin, xs_fin, z_send, z_recv, t_buf, f_recv,
    ssem, rsem,
):
    d = lax.axis_index("dp")
    t = lax.axis_index("tensor")
    xi = d // 16
    zi = lax.rem(d // 2, NZ)
    core = lax.rem(d, 2)
    inner = lax.rem(d, 16)
    t_right, t_left, t_far = lax.rem(t + 1, NT), lax.rem(t + 3, NT), lax.rem(t + 2, NT)
    x_right, x_left, x_far = lax.rem(xi + 1, NX), lax.rem(xi + 3, NX), lax.rem(xi + 2, NX)
    dp_next = (lax.rem(d + 1, 64), t)
    dp_prev = (lax.rem(d + 63, 64), t)
    mate = (d + 1 - 2 * core, t)
    y_right, y_left = (d, t_right), (d, t_left)
    px_right, px_left = (x_right * 16 + inner, t), (x_left * 16 + inner, t)
    z_peers = [
        (lax.rem(zi + k, NZ), (xi * 16 + lax.rem(zi + k, NZ) * 2 + core, t)) for k in range(1, NZ)
    ]

    barrier = pltpu.get_barrier_semaphore()
    greet = [dp_next, dp_prev, y_right, y_left, px_right, px_left] + [p for _, p in z_peers]
    for peer in greet:
        pl.semaphore_signal(barrier, inc=1, device_id=peer, device_id_type=MESH)

    counter = [0]
    pending = []

    def remote(src, dst, dev):
        k = counter[0]
        counter[0] += 1
        copy = pltpu.make_async_remote_copy(
            src_ref=src, dst_ref=dst, send_sem=ssem.at[k], recv_sem=rsem.at[k],
            device_id=dev, device_id_type=MESH,
        )
        copy.start()
        pending.append(copy)
        return copy

    lower = cut_ref[0, 0]
    upper = cut_ref[0, 1]
    head = jnp.maximum(lower, 0)
    tail = jnp.maximum(-upper, 0)

    r, c = grid2(SPILL, SRC)
    base = SEQ - lower + jnp.minimum(upper, 0)
    snd_next[...] = dot(hot(c == r + base), patches_ref[...]).astype(BF)

    pl.semaphore_wait(barrier, len(greet))

    to_next = remote(snd_next, from_prev, dp_next)
    to_prev = remote(patches_ref.at[pl.ds(0, SPILL)], from_next, dp_prev)

    half = SEQ // 2
    lo, hi = pl.ds(0, half), pl.ds(half, half)

    def gather_start(src, full):
        ra = remote(src.at[lo], full.at[t, lo], y_right)
        lb = remote(src.at[hi], full.at[t, hi], y_left)
        rb = remote(src.at[hi], full.at[t, hi], y_right)
        la = remote(src.at[lo], full.at[t, lo], y_left)
        return ra, lb, rb, la

    def gather_relay(full, first):
        ra, lb, rb, la = first
        ra.wait_recv()
        fa = remote(full.at[t_left, lo], full.at[t_left, lo], y_right)
        lb.wait_recv()
        fb = remote(full.at[t_right, hi], full.at[t_right, hi], y_left)
        return rb, la, fa, fb

    def gather_finish(rest):
        for copy in rest:
            copy.wait_recv()

    go_first = gather_start(gout_ref, go_full)
    go_full[t] = gout_ref[...]

    r, c = grid2(SEQ, SRC)
    mine = (c == r - lower) & (r >= head) & (r < SEQ - tail)
    own = dot(hot(mine), patches_ref[...])
    r, c = grid2(SEQ, SPILL)
    pick_prev = hot((c == r) & (r < head))
    pick_next = hot((c == r - (SEQ - tail)) & (r >= SEQ - tail))
    to_next.wait_recv()
    to_prev.wait_recv()
    own = own + dot(pick_prev, from_prev[...]) + dot(pick_next, from_next[...])
    x_full[t] = own.astype(BF)
    x_first = gather_start(x_full.at[t], x_full)
    go_rest = gather_relay(go_full, go_first)

    r, c = grid2(2 * PAD, QW)
    pad_rows = hot(((r < PAD) & (c == r) & (c < HD)) | ((r >= PAD) & (c == r - PAD + HD) & (c >= HD)))
    for u in range(NT):
        span = slice(u * COLS, (u + 1) * COLS)
        for part in range(3):
            w_pad[u, part * 256 : (part + 1) * 256, :] = dot(
                pad_rows, wqkv_ref[part, :, span]
            ).astype(BF)
        wo_pad[u] = dot(pad_rows, wout_ref[:, span]).astype(BF)

    x_rest = gather_relay(x_full, x_first)

    r, c = grid2(COLS, COLS)
    eye = hot(r == c)
    gather_finish(go_rest)
    grad_att = jnp.zeros((SEQ, 2 * PAD), F32)
    for u in range(NT):
        grad_att = grad_att + dot(go_full[u], wo_pad[u], 1, 1)
        go_t[u] = dot(eye, go_full[u], 1, 1).astype(BF)
    grad_att = grad_att.astype(BF)

    gather_finish(x_rest)
    mean = jnp.zeros((SEQ, 1), F32)
    for u in range(NT):
        mean = mean + jnp.sum(x_full[u].astype(F32), axis=-1, keepdims=True)
    mean = mean * (1.0 / MODEL)
    spread = jnp.zeros((SEQ, 1), F32)
    for u in range(NT):
        center = x_full[u].astype(F32) - mean
        spread = spread + jnp.sum(center * center, axis=-1, keepdims=True)
    rstd = lax.rsqrt(spread * (1.0 / MODEL) + norm_eps)
    proj = jnp.zeros((SEQ, 6 * PAD), F32)
    for u in range(NT):
        low = ((x_full[u].astype(F32) - mean) * rstd).astype(BF)
        n_low[u] = low
        proj = proj + dot(low, w_pad[u], 1, 1)

    live = lax.broadcasted_iota(jnp.int32, (SEQ, PAD), 1) < HD

    def head_norm(v):
        center = jnp.where(live, v - jnp.sum(v, axis=-1, keepdims=True) * (1.0 / HD), 0.0)
        var = jnp.sum(center * center, axis=-1, keepdims=True) * (1.0 / HD)
        inverse = lax.rsqrt(var + norm_eps)
        return center * inverse, inverse

    def head_back(g, normed, inverse):
        first = jnp.sum(g, axis=-1, keepdims=True) * (1.0 / HD)
        second = jnp.sum(g * normed, axis=-1, keepdims=True) * (1.0 / HD)
        return jnp.where(live, inverse * (g - first - normed * second), 0.0)

    seg_row = seg_ref[...].astype(F32)
    r, c = grid2(SEQ, SEQ)
    seg_col = jnp.sum(jnp.where(r == c, seg_row, 0.0), axis=-1, keepdims=True)
    same = seg_col == seg_row

    saved = []
    att_parts = []
    for h in range(2):
        q_hat, q_inv = head_norm(proj[:, h * PAD : (h + 1) * PAD])
        k_hat, k_inv = head_norm(proj[:, (2 + h) * PAD : (3 + h) * PAD])
        v = proj[:, (4 + h) * PAD : (5 + h) * PAD].astype(BF)
        q, k = q_hat.astype(BF), k_hat.astype(BF)
        raised = jnp.where(same, jnp.exp(dot(q, k, 1, 1) * score_scale), 0.0)
        weights = raised / jnp.sum(raised, axis=-1, keepdims=True)
        weights_low = weights.astype(BF)
        att_parts.append(dot(weights_low, v).astype(BF))
        saved.append((q_hat, q_inv, k_hat, k_inv, q, k, v, weights, weights_low))
    att = jnp.concatenate(att_parts, axis=1)

    def scatter_start(send, rin, make, far, right, left, to_right, to_left, cut_at):
        a, b = pl.ds(0, cut_at), pl.ds(cut_at, cut_at)
        send[0] = make(far).astype(BF)
        ra = remote(send.at[0, a], rin.at[0], to_right)
        lb = remote(send.at[0, b], rin.at[1], to_left)
        return ra, lb

    def scatter_plain(send, fin, make, right, left, to_right, to_left, cut_at):
        a, b = pl.ds(0, cut_at), pl.ds(cut_at, cut_at)
        send[1] = make(right).astype(BF)
        rb = remote(send.at[1, b], fin.at[0, b], to_right)
        send[2] = make(left).astype(BF)
        la = remote(send.at[2, a], fin.at[1, a], to_left)
        return rb, la

    def scatter_relay(send, rin, fin, first, plain, to_right, to_left, cut_at):
        a, b = pl.ds(0, cut_at), pl.ds(cut_at, cut_at)
        ra, lb = first
        rb, la = plain
        ra.wait_recv()
        send[1, a] = (send[1, a].astype(F32) + rin[0].astype(F32)).astype(BF)
        fa = remote(send.at[1, a], fin.at[0, a], to_right)
        lb.wait_recv()
        send[2, b] = (send[2, b].astype(F32) + rin[1].astype(F32)).astype(BF)
        fb = remote(send.at[2, b], fin.at[1, b], to_left)
        return rb, la, fa, fb

    def branch(u):
        return dot(att, wo_pad[u])

    b_send, b_rin, b_fin = rs_send.at[0], rs_rin.at[0], rs_fin.at[0]
    b_first = scatter_start(b_send, b_rin, branch, t_far, t_right, t_left, y_right, y_left, half)
    b_plain = scatter_plain(b_send, b_fin, branch, t_right, t_left, y_right, y_left, half)
    mixed_own = x_full[t].astype(F32) + branch(t)

    grads = {}
    for h in range(2):
        q_hat, q_inv, k_hat, k_inv, q, k, v, weights, weights_low = saved[h]
        ga = grad_att[:, h * PAD : (h + 1) * PAD]
        gw = dot(ga, v, 1, 1)
        inner_sum = jnp.sum(gw * weights, axis=-1, keepdims=True)
        gs = (weights * (gw - inner_sum) * score_scale).astype(BF)
        gq = dot(gs, k)
        gk = dot(gs, q, 0, 0)
        gv = dot(weights_low, ga, 0, 0)
        grads[0, h] = head_back(gq, q_hat, q_inv).astype(BF)
        grads[1, h] = head_back(gk, k_hat, k_inv).astype(BF)
        grads[2, h] = gv.astype(BF)
    gp = jnp.concatenate([grads[p, h] for p in range(3) for h in range(2)], axis=1)

    b_rest = scatter_relay(b_send, b_rin, b_fin, b_first, b_plain, y_right, y_left, half)

    r, c = grid2(4 * PAD, HALF)
    squeeze = c == -1
    for a in range(4):
        squeeze = squeeze | ((r - a * PAD == c - a * HD) & (r >= a * PAD) & (r < a * PAD + HD))
    squeeze = hot(squeeze)
    right_side[0, 0:SEQ, :] = dot(gp[:, 0 : 4 * PAD], squeeze).astype(BF)
    right_side[0, SEQ : 2 * SEQ, :] = jnp.zeros((SEQ, HALF), BF)
    right_side[1, 0:SEQ, :] = dot(gp[:, 4 * PAD : 6 * PAD], squeeze[0 : 2 * PAD]).astype(BF)
    right_side[1, SEQ : 2 * SEQ, :] = dot(att, squeeze[2 * PAD : 4 * PAD]).astype(BF)

    order = [x_far, x_right, x_left, xi]
    for u in range(NT):
        n_t[u] = dot(eye, n_low[u], 1, 1).astype(BF)

    def weight_grad(u, side):
        return dot(n_t[u], right_side[side, 0:SEQ, :]) + dot(
            go_t[u], right_side[side, SEQ : 2 * SEQ, :]
        )

    h_copies = []
    for u in order:
        h_send[u] = weight_grad(u, 1 - core).astype(BF)
        h_copies.append(remote(h_send.at[u], h_recv.at[u], mate))

    s1 = jnp.zeros((SEQ, 1), F32)
    s2 = jnp.zeros((SEQ, 1), F32)
    for u in range(NT):
        part = dot(gp, w_pad[u])
        share[u] = part
        s1 = s1 + jnp.sum(part, axis=-1, keepdims=True)
        s2 = s2 + jnp.sum(
            part * ((x_full[u].astype(F32) - mean) * rstd), axis=-1, keepdims=True
        )
    s1 = s1 * (1.0 / MODEL)
    s2 = s2 * (1.0 / MODEL)

    def back(u):
        return rstd * (share[u] - s1 - ((x_full[u].astype(F32) - mean) * rstd) * s2)

    g_send, g_rin, g_fin = rs_send.at[1], rs_rin.at[1], rs_fin.at[1]
    g_first = scatter_start(g_send, g_rin, back, t_far, t_right, t_left, y_right, y_left, half)
    g_plain = scatter_plain(g_send, g_fin, back, t_right, t_left, y_right, y_left, half)

    for u in order:
        h_keep[u] = weight_grad(u, core)

    def pair(u):
        return h_keep[u] + h_recv[u].astype(F32)

    cut_x = COLS // 2
    h_copies[0].wait_recv()
    x_fst = scatter_start(xs_send, xs_rin, pair, x_far, x_right, x_left, px_right, px_left, cut_x)
    h_copies[1].wait_recv()
    h_copies[2].wait_recv()
    x_pln = scatter_plain(xs_send, xs_fin, pair, x_right, x_left, px_right, px_left, cut_x)

    gx_own = gout_ref[...].astype(F32) + back(t)

    for copy in b_rest:
        copy.wait_recv()
    mixed_ref[...] = (mixed_own + b_fin[0].astype(F32) + b_fin[1].astype(F32)).astype(BF)

    g_rest = scatter_relay(g_send, g_rin, g_fin, g_first, g_plain, y_right, y_left, half)
    x_rst = scatter_relay(xs_send, xs_rin, xs_fin, x_fst, x_pln, px_right, px_left, cut_x)
    h_copies[3].wait_recv()

    for copy in g_rest:
        copy.wait_recv()
    gx[...] = (gx_own + g_fin[0].astype(F32) + g_fin[1].astype(F32)).astype(BF)
    r, c = grid2(SPILL, SEQ)
    bsnd_next[...] = dot(hot(c == r + SEQ - tail), gx[...]).astype(BF)
    back_next = remote(bsnd_next, bfrom_prev, dp_next)
    back_prev = remote(gx.at[pl.ds(0, SPILL)], bfrom_next, dp_prev)

    for copy in x_rst:
        copy.wait_recv()
    summed = (pair(xi) + xs_fin[0].astype(F32) + xs_fin[1].astype(F32)).astype(BF)
    block = 2 * CORE_ROWS
    for k in range(NZ):
        r, c = grid2(block, COLS)
        first = (r < SHARE) & (c == r + 2 * k * SHARE)
        second = (r >= CORE_ROWS) & (r < CORE_ROWS + SHARE)
        second = second & (c == r - CORE_ROWS + (2 * k + 1) * SHARE)
        z_send[k] = dot(hot(first | second), summed).astype(BF)
    z_copies = [remote(z_send.at[pz], z_recv.at[zi], dev) for pz, dev in z_peers]

    length = SEQ + upper - lower
    behind = jnp.maximum(-lower, 0)
    ahead = jnp.maximum(upper, 0)
    r, c = grid2(SRC, SEQ)
    mine = hot((c == r + lower) & (r >= behind) & (r < length - ahead))
    src_rows = dot(mine, gx[...])
    r, c = grid2(SRC, SPILL)
    pick_prev = hot((c == r) & (r < behind))
    pick_next = hot((c == r - (length - ahead)) & (r >= length - ahead) & (r < length))
    back_next.wait_recv()
    back_prev.wait_recv()
    src_rows = src_rows + dot(pick_prev, bfrom_prev[...]) + dot(pick_next, bfrom_next[...])
    gpatch_ref[...] = src_rows.astype(BF)

    total = z_send[zi].astype(F32)
    for copy in z_copies:
        copy.wait_recv()
    for pz, _ in z_peers:
        total = total + z_recv[pz].astype(F32)
    total = total * total_scale
    t_buf[0] = total[0:CORE_ROWS]
    t_buf[1] = total[CORE_ROWS : 2 * CORE_ROWS]
    last = remote(t_buf.at[1 - core], f_recv, mate)
    kept = t_buf[core]
    last.wait_recv()
    got = f_recv[...]
    qk = jnp.where(core == 0, kept, got)
    vo = jnp.where(core == 0, got, kept)
    fill = jnp.zeros((PAD - CORE_ROWS, HALF), F32)
    qk = jnp.transpose(jnp.concatenate([qk, fill], axis=0))
    vo = jnp.transpose(jnp.concatenate([vo, fill], axis=0))
    gqkv_ref[0] = qk[0:QW, 0:SHARE]
    gqkv_ref[1] = qk[QW : 2 * QW, 0:SHARE]
    gqkv_ref[2] = vo[0:QW, 0:SHARE]
    gwout_ref[...] = vo[QW : 2 * QW, 0:SHARE]

    for copy in pending:
        copy.wait_send()


COPIES = 48


def body(patches, seg_ids, cut, w_qkv, w_out, grad_out):
    vmem = pl.BlockSpec(memory_space=pltpu.VMEM)
    smem = pl.BlockSpec(memory_space=pltpu.SMEM)
    scratch = [
        pltpu.VMEM((NT, SEQ, COLS), BF),
        pltpu.VMEM((NT, SEQ, COLS), BF),
        pltpu.VMEM((NT, SEQ, COLS), BF),
        pltpu.VMEM((NT, COLS, SEQ), BF),
        pltpu.VMEM((NT, COLS, SEQ), BF),
        pltpu.VMEM((NT, 6 * PAD, COLS), BF),
        pltpu.VMEM((NT, 2 * PAD, COLS), BF),
        pltpu.VMEM((SPILL, COLS), BF),
        pltpu.VMEM((SPILL, COLS), BF),
        pltpu.VMEM((SPILL, COLS), BF),
        pltpu.VMEM((SPILL, COLS), BF),
        pltpu.VMEM((SPILL, COLS), BF),
        pltpu.VMEM((SPILL, COLS), BF),
        pltpu.VMEM((SEQ, COLS), BF),
        pltpu.VMEM((2, 3, SEQ, COLS), BF),
        pltpu.VMEM((2, 2, SEQ // 2, COLS), BF),
        pltpu.VMEM((2, 2, SEQ, COLS), BF),
        pltpu.VMEM((NT, SEQ, COLS), F32),
        pltpu.VMEM((2, 2 * SEQ, HALF), BF),
        pltpu.VMEM((NT, COLS, HALF), BF),
        pltpu.VMEM((NT, COLS, HALF), BF),
        pltpu.VMEM((NT, COLS, HALF), F32),
        pltpu.VMEM((3, COLS, HALF), BF),
        pltpu.VMEM((2, COLS // 2, HALF), BF),
        pltpu.VMEM((2, COLS, HALF), BF),
        pltpu.VMEM((NZ, 2 * CORE_ROWS, HALF), BF),
        pltpu.VMEM((NZ, 2 * CORE_ROWS, HALF), BF),
        pltpu.VMEM((2, CORE_ROWS, HALF), F32),
        pltpu.VMEM((CORE_ROWS, HALF), F32),
        pltpu.SemaphoreType.DMA((COPIES,)),
        pltpu.SemaphoreType.DMA((COPIES,)),
    ]
    return pl.pallas_call(
        kernel,
        out_shape=(
            jax.ShapeDtypeStruct((SEQ, COLS), BF),
            jax.ShapeDtypeStruct((SRC, COLS), BF),
            jax.ShapeDtypeStruct((3, QW, SHARE), F32),
            jax.ShapeDtypeStruct((QW, SHARE), F32),
        ),
        in_specs=[smem, vmem, vmem, vmem, vmem, vmem],
        out_specs=(vmem, vmem, vmem, vmem),
        scratch_shapes=scratch,
        compiler_params=pltpu.CompilerParams(
            collective_id=0, has_side_effects=True, vmem_limit_bytes=56 * 1024 * 1024
        ),
    )(cut, seg_ids.reshape(1, SEQ), patches, w_qkv, w_out, grad_out)


def solution(mesh):
    in_specs = (
        P("dp", "tensor"),
        P("dp"),
        P("dp", None),
        P(None, "tensor", None),
        P("tensor", None),
        P("dp", "tensor"),
    )
    out_specs = (P("dp", "tensor"), P("dp", "tensor"), P(None, "tensor", "dp"), P("tensor", "dp"))
    return jax.shard_map(body, mesh=mesh, in_specs=in_specs, out_specs=out_specs, check_vma=False)
```

```python
import math

import jax
import jax.numpy as jnp
from jax import lax
from jax.experimental import pallas as pl
from jax.experimental.pallas import tpu as pltpu
from jax.sharding import PartitionSpec as P

HD = 88
SEQ = 256
SRC = 384
SPILL = 64
COLS = 352
MODEL = 1408
QW = 176
NT = 4
NX = 4
NZ = 8
SHARE = 22
CORE_ROWS = 24
norm_eps = 1e-06
score_scale = HD ** (-0.5)
total_scale = 1.0 / math.sqrt(16384.0)

BF = jnp.bfloat16
F32 = jnp.float32
MESH = pl.DeviceIdType.MESH


def dot(a, b, ca=1, cb=0):
    return lax.dot_general(a, b, (((ca,), (cb,)), ((), ())), preferred_element_type=F32)


def grid2(rows, cols):
    r = lax.broadcasted_iota(jnp.int32, (rows, cols), 0)
    c = lax.broadcasted_iota(jnp.int32, (rows, cols), 1)
    return r, c


def hot(mask):
    return jnp.where(mask, 1.0, 0.0).astype(BF)


def kernel(
    cut_ref, seg_ref, patches_ref, wqkv_ref, wout_ref, gout_ref,
    mixed_ref, gpatch_ref, gqkv_ref, gwout_ref,
    acts, x_full, w_t, wo_t,
    snd_next, snd_prev, from_prev, from_next, bsnd_next, bsnd_prev, bfrom_prev, bfrom_next,
    rs_send, rs_rin, rs_fin, share, gp_buf, h_send, h_recv, h_keep,
    xs_send, xs_rin, xs_fin, z_send, z_recv, t_buf, f_recv,
    ssem, rsem,
):
    d = lax.axis_index("dp")
    t = lax.axis_index("tensor")
    xi = d // 16
    zi = lax.rem(d // 2, NZ)
    core = lax.rem(d, 2)
    inner = lax.rem(d, 16)
    t_right, t_left, t_far = lax.rem(t + 1, NT), lax.rem(t + 3, NT), lax.rem(t + 2, NT)
    x_right, x_left, x_far = lax.rem(xi + 1, NX), lax.rem(xi + 3, NX), lax.rem(xi + 2, NX)
    dp_next = (lax.rem(d + 1, 64), t)
    dp_prev = (lax.rem(d + 63, 64), t)
    mate = (d + 1 - 2 * core, t)
    y_right, y_left = (d, t_right), (d, t_left)
    px_right, px_left = (x_right * 16 + inner, t), (x_left * 16 + inner, t)
    z_peers = [
        (lax.rem(zi + k, NZ), (xi * 16 + lax.rem(zi + k, NZ) * 2 + core, t)) for k in range(1, NZ)
    ]
    n_low, go_full = acts.at[0], acts.at[1]

    barrier = pltpu.get_barrier_semaphore()
    greet = [dp_next, dp_prev, y_right, y_left, px_right, px_left] + [p for _, p in z_peers]
    for peer in greet:
        pl.semaphore_signal(barrier, inc=1, device_id=peer, device_id_type=MESH)

    counter = [0]
    pending = []

    def remote(src, dst, dev):
        k = counter[0]
        counter[0] += 1
        copy = pltpu.make_async_remote_copy(
            src_ref=src, dst_ref=dst, send_sem=ssem.at[k], recv_sem=rsem.at[k],
            device_id=dev, device_id_type=MESH,
        )
        copy.start()
        pending.append(copy)
        return copy

    lower = cut_ref[0, 0]
    upper = cut_ref[0, 1]
    head = jnp.maximum(lower, 0)
    tail = jnp.maximum(-upper, 0)

    r, c = grid2(SPILL, SRC)
    base = SEQ - lower + jnp.minimum(upper, 0)
    snd_next[...] = dot(hot(c == r + base), patches_ref[...], 1, 1).astype(BF)
    snd_prev[...] = dot(hot(c == r), patches_ref[...], 1, 1).astype(BF)

    pl.semaphore_wait(barrier, len(greet))

    to_next = remote(snd_next, from_prev, dp_next)
    to_prev = remote(snd_prev, from_next, dp_prev)

    half = COLS // 2
    lo, hi = pl.ds(0, half), pl.ds(half, half)

    def gather_start(src, full):
        ra = remote(src.at[lo], full.at[t, lo], y_right)
        lb = remote(src.at[hi], full.at[t, hi], y_left)
        rb = remote(src.at[hi], full.at[t, hi], y_right)
        la = remote(src.at[lo], full.at[t, lo], y_left)
        return ra, lb, rb, la

    def gather_relay(full, first):
        ra, lb, rb, la = first
        ra.wait_recv()
        fa = remote(full.at[t_left, lo], full.at[t_left, lo], y_right)
        lb.wait_recv()
        fb = remote(full.at[t_right, hi], full.at[t_right, hi], y_left)
        return rb, la, fa, fb

    def gather_finish(rest):
        for copy in rest:
            copy.wait_recv()

    go_first = gather_start(gout_ref, go_full)
    go_full[t] = gout_ref[...]

    r, c = grid2(SRC, SEQ)
    mine = (r == c - lower) & (c >= head) & (c < SEQ - tail)
    own = dot(patches_ref[...], hot(mine))
    r, c = grid2(SPILL, SEQ)
    pick_prev = hot((c == r) & (c < head))
    pick_next = hot((r == c - (SEQ - tail)) & (c >= SEQ - tail))
    to_next.wait_recv()
    to_prev.wait_recv()
    own = own + dot(from_prev[...], pick_prev, 0, 0) + dot(from_next[...], pick_next, 0, 0)
    x_full[t] = own.astype(BF)
    x_first = gather_start(x_full.at[t], x_full)
    go_rest = gather_relay(go_full, go_first)

    w_t[...] = jnp.transpose(wqkv_ref[...])
    wo_t[...] = jnp.transpose(wout_ref[...])

    x_rest = gather_relay(x_full, x_first)

    gather_finish(go_rest)
    grad_att = dot(wout_ref[...], go_full[...].reshape(MODEL, SEQ))

    gather_finish(x_rest)

    def rows_of(u):
        return x_full[u].astype(F32)

    mean = jnp.zeros((1, SEQ), F32)
    for u in range(NT):
        mean = mean + jnp.sum(rows_of(u), axis=0, keepdims=True)
    mean = mean * (1.0 / MODEL)
    spread = jnp.zeros((1, SEQ), F32)
    for u in range(NT):
        center = rows_of(u) - mean
        spread = spread + jnp.sum(center * center, axis=0, keepdims=True)
    rstd = lax.rsqrt(spread * (1.0 / MODEL) + norm_eps)
    for u in range(NT):
        n_low[u] = ((rows_of(u) - mean) * rstd).astype(BF)
    proj = dot(wqkv_ref[...], n_low[...].reshape(MODEL, SEQ))

    def head_norm(v):
        center = v - jnp.sum(v, axis=0, keepdims=True) * (1.0 / HD)
        var = jnp.sum(center * center, axis=0, keepdims=True) * (1.0 / HD)
        inverse = lax.rsqrt(var + norm_eps)
        return center * inverse, inverse

    def head_back(g, normed, inverse):
        first = jnp.sum(g, axis=0, keepdims=True) * (1.0 / HD)
        second = jnp.sum(g * normed, axis=0, keepdims=True) * (1.0 / HD)
        return inverse * (g - first - normed * second)

    seg_row = seg_ref[...].astype(F32)
    r, c = grid2(SEQ, SEQ)
    seg_col = jnp.sum(jnp.where(r == c, seg_row, 0.0), axis=-1, keepdims=True)
    same = seg_col == seg_row

    saved = []
    att_parts = []
    for h in range(2):
        q_hat, q_inv = head_norm(proj[h * HD : (h + 1) * HD])
        k_hat, k_inv = head_norm(proj[(2 + h) * HD : (3 + h) * HD])
        v = proj[(4 + h) * HD : (5 + h) * HD].astype(BF)
        q, k = q_hat.astype(BF), k_hat.astype(BF)
        raised = jnp.where(same, jnp.exp(dot(k, q, 0, 0) * score_scale), 0.0)
        weights = raised / jnp.sum(raised, axis=0, keepdims=True)
        weights_low = weights.astype(BF)
        att_parts.append(dot(v, weights_low))
        saved.append((q_hat, q_inv, k_hat, k_inv, q, k, v, weights, weights_low))
    att = jnp.concatenate(att_parts, axis=0).astype(BF)
    gp_buf[3] = att

    def scatter_start(send, rin, make, far, to_right, to_left, cut_at):
        a, b = pl.ds(0, cut_at), pl.ds(cut_at, cut_at)
        send[0] = make(far).astype(BF)
        ra = remote(send.at[0, a], rin.at[0], to_right)
        lb = remote(send.at[0, b], rin.at[1], to_left)
        return ra, lb

    def scatter_plain(send, fin, make, right, left, to_right, to_left, cut_at):
        a, b = pl.ds(0, cut_at), pl.ds(cut_at, cut_at)
        send[1] = make(right).astype(BF)
        rb = remote(send.at[1, b], fin.at[0, b], to_right)
        send[2] = make(left).astype(BF)
        la = remote(send.at[2, a], fin.at[1, a], to_left)
        return rb, la

    def scatter_relay(send, rin, fin, first, plain, to_right, to_left, cut_at):
        a, b = pl.ds(0, cut_at), pl.ds(cut_at, cut_at)
        ra, lb = first
        rb, la = plain
        ra.wait_recv()
        send[1, a] = (send[1, a].astype(F32) + rin[0].astype(F32)).astype(BF)
        fa = remote(send.at[1, a], fin.at[0, a], to_right)
        lb.wait_recv()
        send[2, b] = (send[2, b].astype(F32) + rin[1].astype(F32)).astype(BF)
        fb = remote(send.at[2, b], fin.at[1, b], to_left)
        return rb, la, fa, fb

    def branch(u):
        return dot(wo_t[pl.ds(pl.multiple_of(u * COLS, COLS), COLS), :], att)

    b_send, b_rin, b_fin = rs_send.at[0], rs_rin.at[0], rs_fin.at[0]
    b_first = scatter_start(b_send, b_rin, branch, t_far, y_right, y_left, half)
    b_plain = scatter_plain(b_send, b_fin, branch, t_right, t_left, y_right, y_left, half)
    mixed_own = x_full[t].astype(F32) + branch(t)

    grads = {}
    for h in range(2):
        q_hat, q_inv, k_hat, k_inv, q, k, v, weights, weights_low = saved[h]
        ga = grad_att[h * HD : (h + 1) * HD].astype(BF)
        gw = dot(v, ga, 0, 0)
        inner_sum = jnp.sum(gw * weights, axis=0, keepdims=True)
        gs = (weights * (gw - inner_sum) * score_scale).astype(BF)
        grads[0, h] = head_back(dot(k, gs), q_hat, q_inv)
        grads[1, h] = head_back(dot(q, gs, 1, 1), k_hat, k_inv)
        grads[2, h] = dot(ga, weights_low, 1, 1)
    for p in range(3):
        gp_buf[p] = jnp.concatenate([grads[p, 0], grads[p, 1]], axis=0).astype(BF)

    b_rest = scatter_relay(b_send, b_rin, b_fin, b_first, b_plain, y_right, y_left, half)

    order = [x_far, x_right, x_left, xi]

    def weight_grad(u, side):
        first = dot(n_low[u], gp_buf[2 * side], 1, 1)
        second = dot(acts[side, u], gp_buf[2 * side + 1], 1, 1)
        return jnp.concatenate([first, second], axis=1)

    h_copies = []
    for u in order:
        h_send[u] = weight_grad(u, 1 - core).astype(BF)
        h_copies.append(remote(h_send.at[u], h_recv.at[u], mate))

    gp = gp_buf[0:3].reshape(3 * QW, SEQ)
    s1 = jnp.zeros((1, SEQ), F32)
    s2 = jnp.zeros((1, SEQ), F32)
    for u in range(NT):
        part = dot(w_t[u * COLS : (u + 1) * COLS, :], gp)
        share[u] = part
        s1 = s1 + jnp.sum(part, axis=0, keepdims=True)
        s2 = s2 + jnp.sum(part * ((rows_of(u) - mean) * rstd), axis=0, keepdims=True)
    s1 = s1 * (1.0 / MODEL)
    s2 = s2 * (1.0 / MODEL)

    def back(u):
        return rstd * (share[u] - s1 - ((rows_of(u) - mean) * rstd) * s2)

    g_send, g_rin, g_fin = rs_send.at[1], rs_rin.at[1], rs_fin.at[1]
    g_first = scatter_start(g_send, g_rin, back, t_far, y_right, y_left, half)
    g_plain = scatter_plain(g_send, g_fin, back, t_right, t_left, y_right, y_left, half)

    for u in order:
        h_keep[u] = weight_grad(u, core)

    def pair(u):
        return h_keep[u] + h_recv[u].astype(F32)

    cut_x = COLS // 2
    h_copies[0].wait_recv()
    x_fst = scatter_start(xs_send, xs_rin, pair, x_far, px_right, px_left, cut_x)
    h_copies[1].wait_recv()
    h_copies[2].wait_recv()
    x_pln = scatter_plain(xs_send, xs_fin, pair, x_right, x_left, px_right, px_left, cut_x)

    gx_own = gout_ref[...].astype(F32) + back(t)

    for copy in b_rest:
        copy.wait_recv()
    mixed_ref[...] = (mixed_own + b_fin[0].astype(F32) + b_fin[1].astype(F32)).astype(BF)

    g_rest = scatter_relay(g_send, g_rin, g_fin, g_first, g_plain, y_right, y_left, half)
    x_rst = scatter_relay(xs_send, xs_rin, xs_fin, x_fst, x_pln, px_right, px_left, cut_x)
    h_copies[3].wait_recv()

    for copy in g_rest:
        copy.wait_recv()
    gx = (gx_own + g_fin[0].astype(F32) + g_fin[1].astype(F32)).astype(BF)
    r, c = grid2(SPILL, SEQ)
    bsnd_next[...] = dot(hot(c == r + SEQ - tail), gx, 1, 1).astype(BF)
    bsnd_prev[...] = dot(hot(c == r), gx, 1, 1).astype(BF)
    back_next = remote(bsnd_next, bfrom_prev, dp_next)
    back_prev = remote(bsnd_prev, bfrom_next, dp_prev)

    for copy in x_rst:
        copy.wait_recv()
    summed = (pair(xi) + xs_fin[0].astype(F32) + xs_fin[1].astype(F32)).astype(BF)
    block = 2 * CORE_ROWS
    for k in range(NZ):
        r, c = grid2(block, COLS)
        first = (r < SHARE) & (c == r + 2 * k * SHARE)
        second = (r >= CORE_ROWS) & (r < CORE_ROWS + SHARE)
        second = second & (c == r - CORE_ROWS + (2 * k + 1) * SHARE)
        z_send[k] = dot(hot(first | second), summed).astype(BF)
    z_copies = [remote(z_send.at[pz], z_recv.at[zi], dev) for pz, dev in z_peers]

    length = SEQ + upper - lower
    behind = jnp.maximum(-lower, 0)
    ahead = jnp.maximum(upper, 0)
    r, c = grid2(SEQ, SRC)
    mine = hot((r == c + lower) & (c >= behind) & (c < length - ahead))
    src_rows = dot(gx, mine)
    r, c = grid2(SPILL, SRC)
    pick_prev = hot((c == r) & (c < behind))
    pick_next = hot((r == c - (length - ahead)) & (c >= length - ahead) & (c < length))
    back_next.wait_recv()
    back_prev.wait_recv()
    src_rows = (
        src_rows + dot(bfrom_prev[...], pick_prev, 0, 0) + dot(bfrom_next[...], pick_next, 0, 0)
    )
    gpatch_ref[...] = src_rows.astype(BF)

    total = z_send[zi].astype(F32)
    for copy in z_copies:
        copy.wait_recv()
    for pz, _ in z_peers:
        total = total + z_recv[pz].astype(F32)
    total = total * total_scale
    t_buf[0] = total[0:CORE_ROWS]
    t_buf[1] = total[CORE_ROWS : 2 * CORE_ROWS]
    last = remote(t_buf.at[1 - core], f_recv, mate)
    kept = t_buf[core]
    last.wait_recv()
    got = f_recv[...]
    qk = jnp.where(core == 0, kept, got)
    vo = jnp.where(core == 0, got, kept)
    gqkv_ref[0] = qk[0:SHARE, 0:QW]
    gqkv_ref[1] = qk[0:SHARE, QW : 2 * QW]
    gqkv_ref[2] = vo[0:SHARE, 0:QW]
    gwout_ref[...] = vo[0:SHARE, QW : 2 * QW]

    for copy in pending:
        copy.wait_send()


COPIES = 48


def body(patches, seg_ids, cut, w_qkv, w_out, grad_out):
    vmem = pl.BlockSpec(memory_space=pltpu.VMEM)
    smem = pl.BlockSpec(memory_space=pltpu.SMEM)
    halo = pltpu.VMEM((SPILL, COLS), BF)
    scratch = [
        pltpu.VMEM((2, NT, COLS, SEQ), BF),
        pltpu.VMEM((NT, COLS, SEQ), BF),
        pltpu.VMEM((MODEL, 3 * QW), BF),
        pltpu.VMEM((MODEL, QW), BF),
        halo, halo, halo, halo, halo, halo, halo, halo,
        pltpu.VMEM((2, 3, COLS, SEQ), BF),
        pltpu.VMEM((2, 2, COLS // 2, SEQ), BF),
        pltpu.VMEM((2, 2, COLS, SEQ), BF),
        pltpu.VMEM((NT, COLS, SEQ), F32),
        pltpu.VMEM((4, QW, SEQ), BF),
        pltpu.VMEM((NT, COLS, COLS), BF),
        pltpu.VMEM((NT, COLS, COLS), BF),
        pltpu.VMEM((NT, COLS, COLS), F32),
        pltpu.VMEM((3, COLS, COLS), BF),
        pltpu.VMEM((2, COLS // 2, COLS), BF),
        pltpu.VMEM((2, COLS, COLS), BF),
        pltpu.VMEM((NZ, 2 * CORE_ROWS, COLS), BF),
        pltpu.VMEM((NZ, 2 * CORE_ROWS, COLS), BF),
        pltpu.VMEM((2, CORE_ROWS, COLS), F32),
        pltpu.VMEM((CORE_ROWS, COLS), F32),
        pltpu.SemaphoreType.DMA((COPIES,)),
        pltpu.SemaphoreType.DMA((COPIES,)),
    ]
    mixed, grad_patches, qkv_grad, out_grad = pl.pallas_call(
        kernel,
        out_shape=(
            jax.ShapeDtypeStruct((COLS, SEQ), BF),
            jax.ShapeDtypeStruct((COLS, SRC), BF),
            jax.ShapeDtypeStruct((3, SHARE, QW), F32),
            jax.ShapeDtypeStruct((SHARE, QW), F32),
        ),
        in_specs=[smem, vmem, vmem, vmem, vmem, vmem],
        out_specs=(vmem, vmem, vmem, vmem),
        scratch_shapes=scratch,
        compiler_params=pltpu.CompilerParams(
            collective_id=0, has_side_effects=True, vmem_limit_bytes=56 * 1024 * 1024
        ),
    )(cut, seg_ids.reshape(1, SEQ), patches.T, w_qkv.reshape(3 * QW, MODEL), w_out, grad_out.T)
    return mixed.T, grad_patches.T, jnp.swapaxes(qkv_grad, 1, 2), out_grad.T


def solution(mesh):
    in_specs = (
        P("dp", "tensor"),
        P("dp"),
        P("dp", None),
        P(None, "tensor", None),
        P("tensor", None),
        P("dp", "tensor"),
    )
    out_specs = (P("dp", "tensor"), P("dp", "tensor"), P(None, "tensor", "dp"), P("tensor", "dp"))
    return jax.shard_map(body, mesh=mesh, in_specs=in_specs, out_specs=out_specs, check_vma=False)
```

```python
import math

import jax
import jax.numpy as jnp
from jax import lax
from jax.experimental import pallas as pl
from jax.experimental.pallas import tpu as pltpu
from jax.sharding import PartitionSpec as P

HD = 88
SEQ = 256
SRC = 384
SPILL = 64
COLS = 352
MODEL = 1408
QW = 176
NT = 4
NX = 4
NZ = 8
SHARE = 22
CORE_ROWS = 24
KEPT = NZ * CORE_ROWS
norm_eps = 1e-06
score_scale = HD ** (-0.5)
total_scale = 1.0 / math.sqrt(16384.0)

BF = jnp.bfloat16
F32 = jnp.float32
MESH = pl.DeviceIdType.MESH


def dot(a, b, ca=1, cb=0):
    return lax.dot_general(a, b, (((ca,), (cb,)), ((), ())), preferred_element_type=F32)


def grid2(rows, cols):
    r = lax.broadcasted_iota(jnp.int32, (rows, cols), 0)
    c = lax.broadcasted_iota(jnp.int32, (rows, cols), 1)
    return r, c


def hot(mask):
    return jnp.where(mask, 1.0, 0.0).astype(BF)


def kernel(
    cut_ref, seg_ref, patches_ref, wqkv_ref, wout_ref, gout_ref,
    mixed_ref, gpatch_ref, gqkv_ref, gwout_ref,
    acts, x_full, w_t, wo_t,
    snd_next, snd_prev, from_prev, from_next, bsnd_next, bsnd_prev, bfrom_prev, bfrom_next,
    rs_send, rs_rin, rs_fin, share, gp_buf, gp_mate, own_sel, out_sel, mate_sel,
    xs_send, xs_rin, xs_fin, z_send, z_recv,
    ssem, rsem,
):
    d = lax.axis_index("dp")
    t = lax.axis_index("tensor")
    xi = d // 16
    zi = lax.rem(d // 2, NZ)
    core = lax.rem(d, 2)
    inner = lax.rem(d, 16)
    t_right, t_left, t_far = lax.rem(t + 1, NT), lax.rem(t + 3, NT), lax.rem(t + 2, NT)
    x_right, x_left, x_far = lax.rem(xi + 1, NX), lax.rem(xi + 3, NX), lax.rem(xi + 2, NX)
    dp_next = (lax.rem(d + 1, 64), t)
    dp_prev = (lax.rem(d + 63, 64), t)
    mate = (d + 1 - 2 * core, t)
    y_right, y_left = (d, t_right), (d, t_left)
    px_right, px_left = (x_right * 16 + inner, t), (x_left * 16 + inner, t)
    z_peers = [
        (lax.rem(zi + k, NZ), (xi * 16 + lax.rem(zi + k, NZ) * 2 + core, t)) for k in range(1, NZ)
    ]
    n_low, go_full = acts.at[0], acts.at[1]

    barrier = pltpu.get_barrier_semaphore()
    greet = [dp_next, dp_prev, y_right, y_left, px_right, px_left] + [p for _, p in z_peers]
    for peer in greet:
        pl.semaphore_signal(barrier, inc=1, device_id=peer, device_id_type=MESH)

    counter = [0]
    pending = []

    def remote(src, dst, dev):
        k = counter[0]
        counter[0] += 1
        copy = pltpu.make_async_remote_copy(
            src_ref=src, dst_ref=dst, send_sem=ssem.at[k], recv_sem=rsem.at[k],
            device_id=dev, device_id_type=MESH,
        )
        copy.start()
        pending.append(copy)
        return copy

    lower = cut_ref[0, 0]
    upper = cut_ref[0, 1]
    head = jnp.maximum(lower, 0)
    tail = jnp.maximum(-upper, 0)

    r, c = grid2(SPILL, SRC)
    base = SEQ - lower + jnp.minimum(upper, 0)
    snd_next[...] = dot(hot(c == r + base), patches_ref[...], 1, 1).astype(BF)
    snd_prev[...] = dot(hot(c == r), patches_ref[...], 1, 1).astype(BF)

    pl.semaphore_wait(barrier, len(greet))

    to_next = remote(snd_next, from_prev, dp_next)
    to_prev = remote(snd_prev, from_next, dp_prev)

    half = COLS // 2
    lo, hi = pl.ds(0, half), pl.ds(half, half)

    def gather_start(src, full):
        ra = remote(src.at[lo], full.at[t, lo], y_right)
        lb = remote(src.at[hi], full.at[t, hi], y_left)
        rb = remote(src.at[hi], full.at[t, hi], y_right)
        la = remote(src.at[lo], full.at[t, lo], y_left)
        return ra, lb, rb, la

    def gather_relay(full, first):
        ra, lb, rb, la = first
        ra.wait_recv()
        fa = remote(full.at[t_left, lo], full.at[t_left, lo], y_right)
        lb.wait_recv()
        fb = remote(full.at[t_right, hi], full.at[t_right, hi], y_left)
        return rb, la, fa, fb

    def gather_finish(rest):
        for copy in rest:
            copy.wait_recv()

    go_first = gather_start(gout_ref, go_full)
    go_full[t] = gout_ref[...]

    r, c = grid2(SRC, SEQ)
    mine = (r == c - lower) & (c >= head) & (c < SEQ - tail)
    own = dot(patches_ref[...], hot(mine))
    r, c = grid2(SPILL, SEQ)
    pick_prev = hot((c == r) & (c < head))
    pick_next = hot((r == c - (SEQ - tail)) & (c >= SEQ - tail))
    to_next.wait_recv()
    to_prev.wait_recv()
    own = own + dot(from_prev[...], pick_prev, 0, 0) + dot(from_next[...], pick_next, 0, 0)
    x_full[t] = own.astype(BF)
    x_first = gather_start(x_full.at[t], x_full)

    w_t[...] = jnp.transpose(wqkv_ref[...])
    wo_t[...] = jnp.transpose(wout_ref[...])

    r, c = grid2(KEPT, COLS)

    def chosen(parity):
        mask = c < 0
        for k in range(NZ):
            at = r - k * CORE_ROWS
            mask = mask | ((at >= 0) & (at < SHARE) & (c == at + (2 * k + parity) * SHARE))
        return hot(mask)

    sel_own, sel_mate = chosen(core), chosen(1 - core)

    x_rest = gather_relay(x_full, x_first)
    go_rest = gather_relay(go_full, go_first)
    gather_finish(x_rest)

    def rows_of(u):
        return x_full[u].astype(F32)

    mean = jnp.zeros((1, SEQ), F32)
    for u in range(NT):
        mean = mean + jnp.sum(rows_of(u), axis=0, keepdims=True)
    mean = mean * (1.0 / MODEL)
    spread = jnp.zeros((1, SEQ), F32)
    for u in range(NT):
        center = rows_of(u) - mean
        spread = spread + jnp.sum(center * center, axis=0, keepdims=True)
    rstd = lax.rsqrt(spread * (1.0 / MODEL) + norm_eps)
    for u in range(NT):
        n_low[u] = ((rows_of(u) - mean) * rstd).astype(BF)
    proj = dot(wqkv_ref[...], n_low[...].reshape(MODEL, SEQ))

    def pick(kind):
        for u in range(NT):
            out_sel[kind, u] = dot(sel_mate, acts[kind, u]).astype(BF)
        copy = remote(out_sel.at[kind], mate_sel.at[kind], mate)
        for u in range(NT):
            own_sel[kind, u] = dot(sel_own, acts[kind, u]).astype(BF)
        return copy

    n_copy = pick(0)

    def head_norm(v):
        center = v - jnp.sum(v, axis=0, keepdims=True) * (1.0 / HD)
        var = jnp.sum(center * center, axis=0, keepdims=True) * (1.0 / HD)
        inverse = lax.rsqrt(var + norm_eps)
        return center * inverse, inverse

    def head_back(g, normed, inverse):
        first = jnp.sum(g, axis=0, keepdims=True) * (1.0 / HD)
        second = jnp.sum(g * normed, axis=0, keepdims=True) * (1.0 / HD)
        return inverse * (g - first - normed * second)

    seg_row = seg_ref[...].astype(F32)
    r, c = grid2(SEQ, SEQ)
    seg_col = jnp.sum(jnp.where(r == c, seg_row, 0.0), axis=-1, keepdims=True)
    same = seg_col == seg_row

    saved = []
    att_parts = []
    for h in range(2):
        q_hat, q_inv = head_norm(proj[h * HD : (h + 1) * HD])
        k_hat, k_inv = head_norm(proj[(2 + h) * HD : (3 + h) * HD])
        v = proj[(4 + h) * HD : (5 + h) * HD].astype(BF)
        q, k = q_hat.astype(BF), k_hat.astype(BF)
        raised = jnp.where(same, jnp.exp(dot(k, q, 0, 0) * score_scale), 0.0)
        weights = raised / jnp.sum(raised, axis=0, keepdims=True)
        weights_low = weights.astype(BF)
        att_parts.append(dot(v, weights_low))
        saved.append((q_hat, q_inv, k_hat, k_inv, q, k, v, weights, weights_low))
    att = jnp.concatenate(att_parts, axis=0).astype(BF)
    gp_buf[3] = att
    att_copy = remote(gp_buf.at[3], gp_mate.at[3], mate)

    def scatter_far(send, rin, make, far, to_right, to_left, cut_at):
        a, b = pl.ds(0, cut_at), pl.ds(cut_at, cut_at)
        send[0] = make(far).astype(BF)
        ra = remote(send.at[0, a], rin.at[0], to_right)
        lb = remote(send.at[0, b], rin.at[1], to_left)
        return ra, lb

    def scatter_plain(send, fin, make, right, left, to_right, to_left, cut_at):
        a, b = pl.ds(0, cut_at), pl.ds(cut_at, cut_at)
        send[1] = make(right).astype(BF)
        rb = remote(send.at[1, b], fin.at[0, b], to_right)
        send[2] = make(left).astype(BF)
        la = remote(send.at[2, a], fin.at[1, a], to_left)
        return rb, la

    def scatter_relay(send, rin, fin, first, plain, to_right, to_left, cut_at):
        a, b = pl.ds(0, cut_at), pl.ds(cut_at, cut_at)
        ra, lb = first
        rb, la = plain
        ra.wait_recv()
        send[1, a] = (send[1, a].astype(F32) + rin[0].astype(F32)).astype(BF)
        fa = remote(send.at[1, a], fin.at[0, a], to_right)
        lb.wait_recv()
        send[2, b] = (send[2, b].astype(F32) + rin[1].astype(F32)).astype(BF)
        fb = remote(send.at[2, b], fin.at[1, b], to_left)
        return rb, la, fa, fb

    def branch(u):
        return dot(wo_t[pl.ds(pl.multiple_of(u * COLS, COLS), COLS), :], att)

    b_send, b_rin, b_fin = rs_send.at[0], rs_rin.at[0], rs_fin.at[0]
    b_far = scatter_far(b_send, b_rin, branch, t_far, y_right, y_left, half)

    gather_finish(go_rest)
    grad_att = dot(wout_ref[...], go_full[...].reshape(MODEL, SEQ))
    gas = [grad_att[h * HD : (h + 1) * HD].astype(BF) for h in range(2)]
    gvs = [dot(gas[h], saved[h][8], 1, 1) for h in range(2)]
    gp_buf[2] = jnp.concatenate(gvs, axis=0).astype(BF)
    v_copy = remote(gp_buf.at[2], gp_mate.at[2], mate)
    go_copy = pick(1)

    gqs, gks = [], []
    for h in range(2):
        q_hat, q_inv, k_hat, k_inv, q, k, v, weights, weights_low = saved[h]
        gw = dot(v, gas[h], 0, 0)
        inner_sum = jnp.sum(gw * weights, axis=0, keepdims=True)
        gs = (weights * (gw - inner_sum) * score_scale).astype(BF)
        gqs.append(head_back(dot(k, gs), q_hat, q_inv))
        gks.append(head_back(dot(q, gs, 1, 1), k_hat, k_inv))
    gp_buf[0] = jnp.concatenate(gqs, axis=0).astype(BF)
    gp_buf[1] = jnp.concatenate(gks, axis=0).astype(BF)
    qk_copy = remote(gp_buf.at[pl.ds(0, 2)], gp_mate.at[pl.ds(0, 2)], mate)

    def grad_vo(u):
        first = dot(own_sel[0, u], gp_buf[2], 1, 1) + dot(mate_sel[0, u], gp_mate[2], 1, 1)
        second = dot(own_sel[1, u], gp_buf[3], 1, 1) + dot(mate_sel[1, u], gp_mate[3], 1, 1)
        return jnp.concatenate([first, second], axis=1)

    def grad_qk(u):
        ours = gp_buf[0:2].reshape(2 * QW, SEQ)
        theirs = gp_mate[0:2].reshape(2 * QW, SEQ)
        return dot(own_sel[0, u], ours, 1, 1) + dot(mate_sel[0, u], theirs, 1, 1)

    cut_x = KEPT // 2
    n_copy.wait_recv()
    att_copy.wait_recv()
    v_copy.wait_recv()
    go_copy.wait_recv()
    v_send, v_rin, v_fin = xs_send.at[0], xs_rin.at[0], xs_fin.at[0]
    q_send, q_rin, q_fin = xs_send.at[1], xs_rin.at[1], xs_fin.at[1]
    v_far = scatter_far(v_send, v_rin, grad_vo, x_far, px_right, px_left, cut_x)
    v_plain = scatter_plain(
        v_send, v_fin, grad_vo, x_right, x_left, px_right, px_left, cut_x
    )

    gp = gp_buf[0:3].reshape(3 * QW, SEQ)
    s1 = jnp.zeros((1, SEQ), F32)
    s2 = jnp.zeros((1, SEQ), F32)
    for u in range(NT):
        part = dot(w_t[u * COLS : (u + 1) * COLS, :], gp)
        share[u] = part
        s1 = s1 + jnp.sum(part, axis=0, keepdims=True)
        s2 = s2 + jnp.sum(part * ((rows_of(u) - mean) * rstd), axis=0, keepdims=True)
    s1 = s1 * (1.0 / MODEL)
    s2 = s2 * (1.0 / MODEL)

    def back(u):
        return rstd * (share[u] - s1 - ((rows_of(u) - mean) * rstd) * s2)

    g_send, g_rin, g_fin = rs_send.at[1], rs_rin.at[1], rs_fin.at[1]
    g_far = scatter_far(g_send, g_rin, back, t_far, y_right, y_left, half)
    g_plain = scatter_plain(g_send, g_fin, back, t_right, t_left, y_right, y_left, half)

    qk_copy.wait_recv()
    q_far = scatter_far(q_send, q_rin, grad_qk, x_far, px_right, px_left, cut_x)
    q_plain = scatter_plain(
        q_send, q_fin, grad_qk, x_right, x_left, px_right, px_left, cut_x
    )
    v_rest = scatter_relay(v_send, v_rin, v_fin, v_far, v_plain, px_right, px_left, cut_x)
    g_rest = scatter_relay(g_send, g_rin, g_fin, g_far, g_plain, y_right, y_left, half)
    q_rest = scatter_relay(q_send, q_rin, q_fin, q_far, q_plain, px_right, px_left, cut_x)
    b_plain = scatter_plain(b_send, b_fin, branch, t_right, t_left, y_right, y_left, half)
    b_rest = scatter_relay(b_send, b_rin, b_fin, b_far, b_plain, y_right, y_left, half)

    mixed_own = x_full[t].astype(F32) + branch(t)
    gx_own = gout_ref[...].astype(F32) + back(t)
    v_own = grad_vo(xi)
    q_own = grad_qk(xi)

    for copy in g_rest:
        copy.wait_recv()
    gx = (gx_own + g_fin[0].astype(F32) + g_fin[1].astype(F32)).astype(BF)
    r, c = grid2(SPILL, SEQ)
    bsnd_next[...] = dot(hot(c == r + SEQ - tail), gx, 1, 1).astype(BF)
    bsnd_prev[...] = dot(hot(c == r), gx, 1, 1).astype(BF)
    back_next = remote(bsnd_next, bfrom_prev, dp_next)
    back_prev = remote(bsnd_prev, bfrom_next, dp_prev)

    for copy in v_rest:
        copy.wait_recv()
    v_sum = v_own + v_fin[0].astype(F32) + v_fin[1].astype(F32)
    for copy in q_rest:
        copy.wait_recv()
    q_sum = q_own + q_fin[0].astype(F32) + q_fin[1].astype(F32)
    for k in range(NZ):
        at = slice(k * CORE_ROWS, (k + 1) * CORE_ROWS)
        z_send[k] = jnp.concatenate([q_sum[at], v_sum[at]], axis=0).astype(BF)
    z_copies = [remote(z_send.at[pz], z_recv.at[zi], dev) for pz, dev in z_peers]

    length = SEQ + upper - lower
    behind = jnp.maximum(-lower, 0)
    ahead = jnp.maximum(upper, 0)
    r, c = grid2(SEQ, SRC)
    mine = hot((r == c + lower) & (c >= behind) & (c < length - ahead))
    src_rows = dot(gx, mine)
    r, c = grid2(SPILL, SRC)
    pick_prev = hot((c == r) & (c < behind))
    pick_next = hot((r == c - (length - ahead)) & (c >= length - ahead) & (c < length))
    back_next.wait_recv()
    back_prev.wait_recv()
    src_rows = (
        src_rows + dot(bfrom_prev[...], pick_prev, 0, 0) + dot(bfrom_next[...], pick_next, 0, 0)
    )
    gpatch_ref[...] = src_rows.astype(BF)

    for copy in b_rest:
        copy.wait_recv()
    mixed_ref[...] = (mixed_own + b_fin[0].astype(F32) + b_fin[1].astype(F32)).astype(BF)

    total = z_send[zi].astype(F32)
    for copy in z_copies:
        copy.wait_recv()
    for pz, _ in z_peers:
        total = total + z_recv[pz].astype(F32)
    total = total * total_scale
    gqkv_ref[0] = total[0:SHARE, 0:QW]
    gqkv_ref[1] = total[0:SHARE, QW : 2 * QW]
    gqkv_ref[2] = total[CORE_ROWS : CORE_ROWS + SHARE, 0:QW]
    gwout_ref[...] = total[CORE_ROWS : CORE_ROWS + SHARE, QW : 2 * QW]

    for copy in pending:
        copy.wait_send()


def hand_out(a, b, c, e, a_out, b_out, c_out, e_out, sems):
    pairs = [(a, a_out), (b, b_out), (c, c_out), (e, e_out)]
    copies = [
        pltpu.make_async_copy(src, dst, sems.at[k]) for k, (src, dst) in enumerate(pairs)
    ]
    for copy in copies:
        copy.start()
    for copy in copies:
        copy.wait()


COPIES = 56


def body(patches, seg_ids, cut, w_qkv, w_out, grad_out):
    vmem = pl.BlockSpec(memory_space=pltpu.VMEM)
    smem = pl.BlockSpec(memory_space=pltpu.SMEM)
    anym = pl.BlockSpec(memory_space=pl.ANY)
    halo = pltpu.VMEM((SPILL, COLS), BF)
    scratch = [
        pltpu.VMEM((2, NT, COLS, SEQ), BF),
        pltpu.VMEM((NT, COLS, SEQ), BF),
        pltpu.VMEM((MODEL, 3 * QW), BF),
        pltpu.VMEM((MODEL, QW), BF),
        halo, halo, halo, halo, halo, halo, halo, halo,
        pltpu.VMEM((2, 3, COLS, SEQ), BF),
        pltpu.VMEM((2, 2, COLS // 2, SEQ), BF),
        pltpu.VMEM((2, 2, COLS, SEQ), BF),
        pltpu.VMEM((NT, COLS, SEQ), F32),
        pltpu.VMEM((4, QW, SEQ), BF),
        pltpu.VMEM((4, QW, SEQ), BF),
        pltpu.VMEM((2, NX, KEPT, SEQ), BF),
        pltpu.VMEM((2, NX, KEPT, SEQ), BF),
        pltpu.VMEM((2, NX, KEPT, SEQ), BF),
        pltpu.VMEM((2, 3, KEPT, COLS), BF),
        pltpu.VMEM((2, 2, KEPT // 2, COLS), BF),
        pltpu.VMEM((2, 2, KEPT, COLS), BF),
        pltpu.VMEM((NZ, 2 * CORE_ROWS, COLS), BF),
        pltpu.VMEM((NZ, 2 * CORE_ROWS, COLS), BF),
        pltpu.SemaphoreType.DMA((COPIES,)),
        pltpu.SemaphoreType.DMA((COPIES,)),
    ]
    out_shape = (
        jax.ShapeDtypeStruct((COLS, SEQ), BF),
        jax.ShapeDtypeStruct((COLS, SRC), BF),
        jax.ShapeDtypeStruct((3, SHARE, QW), F32),
        jax.ShapeDtypeStruct((SHARE, QW), F32),
    )
    results = pl.pallas_call(
        kernel,
        out_shape=out_shape,
        in_specs=[smem, vmem, vmem, vmem, vmem, vmem],
        out_specs=(vmem, vmem, vmem, vmem),
        scratch_shapes=scratch,
        compiler_params=pltpu.CompilerParams(
            collective_id=0, has_side_effects=True, vmem_limit_bytes=56 * 1024 * 1024
        ),
    )(cut, seg_ids.reshape(1, SEQ), patches.T, w_qkv.reshape(3 * QW, MODEL), w_out, grad_out.T)
    mixed, grad_patches, qkv_grad, out_grad = pl.pallas_call(
        hand_out,
        out_shape=out_shape,
        in_specs=[anym, anym, anym, anym],
        out_specs=(anym, anym, anym, anym),
        scratch_shapes=[pltpu.SemaphoreType.DMA((4,))],
    )(*results)
    return mixed.T, grad_patches.T, jnp.swapaxes(qkv_grad, 1, 2), out_grad.T


def solution(mesh):
    in_specs = (
        P("dp", "tensor"),
        P("dp"),
        P("dp", None),
        P(None, "tensor", None),
        P("tensor", None),
        P("dp", "tensor"),
    )
    out_specs = (P("dp", "tensor"), P("dp", "tensor"), P(None, "tensor", "dp"), P("tensor", "dp"))
    return jax.shard_map(body, mesh=mesh, in_specs=in_specs, out_specs=out_specs, check_vma=False)
```

```python
import math

import jax
import jax.numpy as jnp
from jax import lax
from jax.experimental import pallas as pl
from jax.experimental.pallas import tpu as pltpu
from jax.sharding import PartitionSpec as P

HD = 88
SEQ = 256
SRC = 384
SPILL = 64
COLS = 352
MODEL = 1408
QW = 176
NT = 4
NX = 4
NZ = 8
SHARE = 22
CORE_ROWS = 24
KEPT = NZ * CORE_ROWS
norm_eps = 1e-06
score_scale = HD ** (-0.5)
total_scale = 1.0 / math.sqrt(16384.0)

BF = jnp.bfloat16
F32 = jnp.float32
MESH = pl.DeviceIdType.MESH


def dot(a, b, ca=1, cb=0):
    return lax.dot_general(a, b, (((ca,), (cb,)), ((), ())), preferred_element_type=F32)


def grid2(rows, cols):
    r = lax.broadcasted_iota(jnp.int32, (rows, cols), 0)
    c = lax.broadcasted_iota(jnp.int32, (rows, cols), 1)
    return r, c


def hot(mask):
    return jnp.where(mask, 1.0, 0.0).astype(BF)


def kernel(
    cut_ref, seg_ref, patches_ref, wqkv_ref, wout_ref, gout_ref,
    mixed_ref, gpatch_ref, gqkv_ref, gwout_ref,
    acts, x_full, w_t, wo_t,
    snd_next, snd_prev, from_prev, from_next, bsnd_next, bsnd_prev, bfrom_prev, bfrom_next,
    rs_send, rs_rin, rs_fin, share, gp_buf, gp_mate, own_sel, out_sel, mate_sel,
    xs_send, xs_rin, xs_fin, z_send, z_recv,
    ssem, rsem,
):
    d = lax.axis_index("dp")
    t = lax.axis_index("tensor")
    xi = d // 16
    zi = lax.rem(d // 2, NZ)
    core = lax.rem(d, 2)
    inner = lax.rem(d, 16)
    t_right, t_left, t_far = lax.rem(t + 1, NT), lax.rem(t + 3, NT), lax.rem(t + 2, NT)
    x_right, x_left, x_far = lax.rem(xi + 1, NX), lax.rem(xi + 3, NX), lax.rem(xi + 2, NX)
    dp_next = (lax.rem(d + 1, 64), t)
    dp_prev = (lax.rem(d + 63, 64), t)
    mate = (d + 1 - 2 * core, t)
    y_right, y_left = (d, t_right), (d, t_left)
    px_right, px_left = (x_right * 16 + inner, t), (x_left * 16 + inner, t)
    z_peers = [
        (lax.rem(zi + k, NZ), (xi * 16 + lax.rem(zi + k, NZ) * 2 + core, t)) for k in range(1, NZ)
    ]
    n_low, go_full = acts.at[0], acts.at[1]

    barrier = pltpu.get_barrier_semaphore()
    greet = [dp_next, dp_prev, y_right, y_left, px_right, px_left] + [p for _, p in z_peers]
    for peer in greet:
        pl.semaphore_signal(barrier, inc=1, device_id=peer, device_id_type=MESH)

    counter = [0]
    pending = []

    def remote(src, dst, dev):
        k = counter[0]
        counter[0] += 1
        copy = pltpu.make_async_remote_copy(
            src_ref=src, dst_ref=dst, send_sem=ssem.at[k], recv_sem=rsem.at[k],
            device_id=dev, device_id_type=MESH,
        )
        copy.start()
        pending.append(copy)
        return copy

    lower = cut_ref[0, 0]
    upper = cut_ref[0, 1]
    head = jnp.maximum(lower, 0)
    tail = jnp.maximum(-upper, 0)

    r, c = grid2(SPILL, SRC)
    base = SEQ - lower + jnp.minimum(upper, 0)
    snd_next[...] = dot(hot(c == r + base), patches_ref[...], 1, 1).astype(BF)
    snd_prev[...] = dot(hot(c == r), patches_ref[...], 1, 1).astype(BF)

    pl.semaphore_wait(barrier, len(greet))

    to_next = remote(snd_next, from_prev, dp_next)
    to_prev = remote(snd_prev, from_next, dp_prev)

    half = COLS // 2
    lo, hi = pl.ds(0, half), pl.ds(half, half)

    def gather_start(src, full):
        ra = remote(src.at[lo], full.at[t, lo], y_right)
        lb = remote(src.at[hi], full.at[t, hi], y_left)
        rb = remote(src.at[hi], full.at[t, hi], y_right)
        la = remote(src.at[lo], full.at[t, lo], y_left)
        return ra, lb, rb, la

    def gather_relay(full, first):
        ra, lb, rb, la = first
        ra.wait_recv()
        fa = remote(full.at[t_left, lo], full.at[t_left, lo], y_right)
        lb.wait_recv()
        fb = remote(full.at[t_right, hi], full.at[t_right, hi], y_left)
        return rb, la, fa, fb

    def gather_finish(rest):
        for copy in rest:
            copy.wait_recv()

    go_first = gather_start(gout_ref, go_full)
    go_full[t] = gout_ref[...]

    r, c = grid2(SRC, SEQ)
    mine = (r == c - lower) & (c >= head) & (c < SEQ - tail)
    own = dot(patches_ref[...], hot(mine))
    r, c = grid2(SPILL, SEQ)
    pick_prev = hot((c == r) & (c < head))
    pick_next = hot((r == c - (SEQ - tail)) & (c >= SEQ - tail))
    to_next.wait_recv()
    to_prev.wait_recv()
    own = own + dot(from_prev[...], pick_prev, 0, 0) + dot(from_next[...], pick_next, 0, 0)
    x_full[t] = own.astype(BF)
    x_first = gather_start(x_full.at[t], x_full)

    w_t[...] = jnp.transpose(wqkv_ref[...])
    wo_t[...] = jnp.transpose(wout_ref[...])

    r, c = grid2(KEPT, COLS)

    def chosen(parity):
        mask = c < 0
        for k in range(NZ):
            at = r - k * CORE_ROWS
            mask = mask | ((at >= 0) & (at < SHARE) & (c == at + (2 * k + parity) * SHARE))
        return hot(mask)

    sel_own, sel_mate = chosen(core), chosen(1 - core)

    x_rest = gather_relay(x_full, x_first)
    go_rest = gather_relay(go_full, go_first)
    gather_finish(x_rest)

    def rows_of(u):
        return x_full[u].astype(F32)

    mean = jnp.zeros((1, SEQ), F32)
    for u in range(NT):
        mean = mean + jnp.sum(rows_of(u), axis=0, keepdims=True)
    mean = mean * (1.0 / MODEL)
    spread = jnp.zeros((1, SEQ), F32)
    for u in range(NT):
        center = rows_of(u) - mean
        spread = spread + jnp.sum(center * center, axis=0, keepdims=True)
    rstd = lax.rsqrt(spread * (1.0 / MODEL) + norm_eps)
    for u in range(NT):
        n_low[u] = ((rows_of(u) - mean) * rstd).astype(BF)
    proj = dot(wqkv_ref[...], n_low[...].reshape(MODEL, SEQ))

    def pick(kind):
        for u in range(NT):
            out_sel[kind, u] = dot(sel_mate, acts[kind, u]).astype(BF)
        copy = remote(out_sel.at[kind], mate_sel.at[kind], mate)
        for u in range(NT):
            own_sel[kind, u] = dot(sel_own, acts[kind, u]).astype(BF)
        return copy

    n_copy = pick(0)

    def head_norm(v):
        center = v - jnp.sum(v, axis=0, keepdims=True) * (1.0 / HD)
        var = jnp.sum(center * center, axis=0, keepdims=True) * (1.0 / HD)
        inverse = lax.rsqrt(var + norm_eps)
        return center * inverse, inverse

    def head_back(g, normed, inverse):
        first = jnp.sum(g, axis=0, keepdims=True) * (1.0 / HD)
        second = jnp.sum(g * normed, axis=0, keepdims=True) * (1.0 / HD)
        return inverse * (g - first - normed * second)

    seg_row = seg_ref[...].astype(F32)
    r, c = grid2(SEQ, SEQ)
    seg_col = jnp.sum(jnp.where(r == c, seg_row, 0.0), axis=-1, keepdims=True)
    same = seg_col == seg_row

    saved = []
    att_parts = []
    for h in range(2):
        q_hat, q_inv = head_norm(proj[h * HD : (h + 1) * HD])
        k_hat, k_inv = head_norm(proj[(2 + h) * HD : (3 + h) * HD])
        v = proj[(4 + h) * HD : (5 + h) * HD].astype(BF)
        q, k = q_hat.astype(BF), k_hat.astype(BF)
        raised = jnp.where(same, jnp.exp(dot(k, q, 0, 0) * score_scale), 0.0)
        weights = raised / jnp.sum(raised, axis=0, keepdims=True)
        weights_low = weights.astype(BF)
        att_parts.append(dot(v, weights_low))
        saved.append((q_hat, q_inv, k_hat, k_inv, q, k, v, weights, weights_low))
    att = jnp.concatenate(att_parts, axis=0).astype(BF)
    gp_buf[3] = att
    att_copy = remote(gp_buf.at[3], gp_mate.at[3], mate)

    def scatter_far(send, rin, make, far, to_right, to_left, cut_at):
        a, b = pl.ds(0, cut_at), pl.ds(cut_at, cut_at)
        send[0] = make(far).astype(BF)
        ra = remote(send.at[0, a], rin.at[0], to_right)
        lb = remote(send.at[0, b], rin.at[1], to_left)
        return ra, lb

    def scatter_plain(send, fin, make, right, left, to_right, to_left, cut_at):
        a, b = pl.ds(0, cut_at), pl.ds(cut_at, cut_at)
        send[1] = make(right).astype(BF)
        rb = remote(send.at[1, b], fin.at[0, b], to_right)
        send[2] = make(left).astype(BF)
        la = remote(send.at[2, a], fin.at[1, a], to_left)
        return rb, la

    def scatter_relay(send, rin, fin, first, plain, to_right, to_left, cut_at):
        a, b = pl.ds(0, cut_at), pl.ds(cut_at, cut_at)
        ra, lb = first
        rb, la = plain
        ra.wait_recv()
        send[1, a] = (send[1, a].astype(F32) + rin[0].astype(F32)).astype(BF)
        fa = remote(send.at[1, a], fin.at[0, a], to_right)
        lb.wait_recv()
        send[2, b] = (send[2, b].astype(F32) + rin[1].astype(F32)).astype(BF)
        fb = remote(send.at[2, b], fin.at[1, b], to_left)
        return rb, la, fa, fb

    def branch(u):
        return dot(wo_t[pl.ds(pl.multiple_of(u * COLS, COLS), COLS), :], att)

    b_send, b_rin, b_fin = rs_send.at[0], rs_rin.at[0], rs_fin.at[0]
    b_far = scatter_far(b_send, b_rin, branch, t_far, y_right, y_left, half)

    gather_finish(go_rest)
    grad_att = dot(wout_ref[...], go_full[...].reshape(MODEL, SEQ))
    gas = [grad_att[h * HD : (h + 1) * HD].astype(BF) for h in range(2)]
    gvs = [dot(gas[h], saved[h][8], 1, 1) for h in range(2)]
    gp_buf[2] = jnp.concatenate(gvs, axis=0).astype(BF)
    v_copy = remote(gp_buf.at[2], gp_mate.at[2], mate)
    go_copy = pick(1)

    gqs, gks = [], []
    for h in range(2):
        q_hat, q_inv, k_hat, k_inv, q, k, v, weights, weights_low = saved[h]
        gw = dot(v, gas[h], 0, 0)
        inner_sum = jnp.sum(gw * weights, axis=0, keepdims=True)
        gs = (weights * (gw - inner_sum) * score_scale).astype(BF)
        gqs.append(head_back(dot(k, gs), q_hat, q_inv))
        gks.append(head_back(dot(q, gs, 1, 1), k_hat, k_inv))
    gp_buf[0] = jnp.concatenate(gqs, axis=0).astype(BF)
    gp_buf[1] = jnp.concatenate(gks, axis=0).astype(BF)
    qk_copy = remote(gp_buf.at[pl.ds(0, 2)], gp_mate.at[pl.ds(0, 2)], mate)

    def grad_vo(u):
        first = dot(own_sel[0, u], gp_buf[2], 1, 1) + dot(mate_sel[0, u], gp_mate[2], 1, 1)
        second = dot(own_sel[1, u], gp_buf[3], 1, 1) + dot(mate_sel[1, u], gp_mate[3], 1, 1)
        return jnp.concatenate([first, second], axis=1)

    def grad_qk(u):
        ours = gp_buf[0:2].reshape(2 * QW, SEQ)
        theirs = gp_mate[0:2].reshape(2 * QW, SEQ)
        return dot(own_sel[0, u], ours, 1, 1) + dot(mate_sel[0, u], theirs, 1, 1)

    cut_x = KEPT // 2
    n_copy.wait_recv()
    att_copy.wait_recv()
    v_copy.wait_recv()
    go_copy.wait_recv()
    v_send, v_rin, v_fin = xs_send.at[0], xs_rin.at[0], xs_fin.at[0]
    q_send, q_rin, q_fin = xs_send.at[1], xs_rin.at[1], xs_fin.at[1]
    v_far = scatter_far(v_send, v_rin, grad_vo, x_far, px_right, px_left, cut_x)
    v_plain = scatter_plain(
        v_send, v_fin, grad_vo, x_right, x_left, px_right, px_left, cut_x
    )

    gp = gp_buf[0:3].reshape(3 * QW, SEQ)
    s1 = jnp.zeros((1, SEQ), F32)
    s2 = jnp.zeros((1, SEQ), F32)
    for u in range(NT):
        part = dot(w_t[u * COLS : (u + 1) * COLS, :], gp)
        share[u] = part
        s1 = s1 + jnp.sum(part, axis=0, keepdims=True)
        s2 = s2 + jnp.sum(part * ((rows_of(u) - mean) * rstd), axis=0, keepdims=True)
    s1 = s1 * (1.0 / MODEL)
    s2 = s2 * (1.0 / MODEL)

    def back(u):
        return rstd * (share[u] - s1 - ((rows_of(u) - mean) * rstd) * s2)

    g_send, g_rin, g_fin = rs_send.at[1], rs_rin.at[1], rs_fin.at[1]
    g_far = scatter_far(g_send, g_rin, back, t_far, y_right, y_left, half)
    g_plain = scatter_plain(g_send, g_fin, back, t_right, t_left, y_right, y_left, half)

    qk_copy.wait_recv()
    q_far = scatter_far(q_send, q_rin, grad_qk, x_far, px_right, px_left, cut_x)
    q_plain = scatter_plain(
        q_send, q_fin, grad_qk, x_right, x_left, px_right, px_left, cut_x
    )
    v_rest = scatter_relay(v_send, v_rin, v_fin, v_far, v_plain, px_right, px_left, cut_x)
    g_rest = scatter_relay(g_send, g_rin, g_fin, g_far, g_plain, y_right, y_left, half)
    q_rest = scatter_relay(q_send, q_rin, q_fin, q_far, q_plain, px_right, px_left, cut_x)
    b_plain = scatter_plain(b_send, b_fin, branch, t_right, t_left, y_right, y_left, half)
    b_rest = scatter_relay(b_send, b_rin, b_fin, b_far, b_plain, y_right, y_left, half)

    mixed_own = x_full[t].astype(F32) + branch(t)
    gx_own = gout_ref[...].astype(F32) + back(t)
    v_own = grad_vo(xi)
    q_own = grad_qk(xi)

    for copy in g_rest:
        copy.wait_recv()
    gx = (gx_own + g_fin[0].astype(F32) + g_fin[1].astype(F32)).astype(BF)
    r, c = grid2(SPILL, SEQ)
    bsnd_next[...] = dot(hot(c == r + SEQ - tail), gx, 1, 1).astype(BF)
    bsnd_prev[...] = dot(hot(c == r), gx, 1, 1).astype(BF)
    back_next = remote(bsnd_next, bfrom_prev, dp_next)
    back_prev = remote(bsnd_prev, bfrom_next, dp_prev)

    for copy in v_rest:
        copy.wait_recv()
    v_sum = v_own + v_fin[0].astype(F32) + v_fin[1].astype(F32)
    for copy in q_rest:
        copy.wait_recv()
    q_sum = q_own + q_fin[0].astype(F32) + q_fin[1].astype(F32)
    for k in range(NZ):
        at = slice(k * CORE_ROWS, (k + 1) * CORE_ROWS)
        z_send[k] = jnp.concatenate([q_sum[at], v_sum[at]], axis=0).astype(BF)
    z_copies = [remote(z_send.at[pz], z_recv.at[zi], dev) for pz, dev in z_peers]

    length = SEQ + upper - lower
    behind = jnp.maximum(-lower, 0)
    ahead = jnp.maximum(upper, 0)
    r, c = grid2(SEQ, SRC)
    mine = hot((r == c + lower) & (c >= behind) & (c < length - ahead))
    src_rows = dot(gx, mine)
    r, c = grid2(SPILL, SRC)
    pick_prev = hot((c == r) & (c < behind))
    pick_next = hot((r == c - (length - ahead)) & (c >= length - ahead) & (c < length))
    back_next.wait_recv()
    back_prev.wait_recv()
    src_rows = (
        src_rows + dot(bfrom_prev[...], pick_prev, 0, 0) + dot(bfrom_next[...], pick_next, 0, 0)
    )
    gpatch_ref[...] = src_rows.astype(BF)

    for copy in b_rest:
        copy.wait_recv()
    mixed_ref[...] = (mixed_own + b_fin[0].astype(F32) + b_fin[1].astype(F32)).astype(BF)

    total = z_send[zi].astype(F32)
    for copy in z_copies:
        copy.wait_recv()
    for pz, _ in z_peers:
        total = total + z_recv[pz].astype(F32)
    total = total * total_scale
    gqkv_ref[0] = total[0:SHARE, 0:QW]
    gqkv_ref[1] = total[0:SHARE, QW : 2 * QW]
    gqkv_ref[2] = total[CORE_ROWS : CORE_ROWS + SHARE, 0:QW]
    gwout_ref[...] = total[CORE_ROWS : CORE_ROWS + SHARE, QW : 2 * QW]

    for copy in pending:
        copy.wait_send()


def hand_out(a, b, c, e, a_out, b_out, c_out, e_out):
    a_out[...] = a[...]
    b_out[...] = b[...]
    c_out[...] = c[...]
    e_out[...] = e[...]


COPIES = 56


def body(patches, seg_ids, cut, w_qkv, w_out, grad_out):
    vmem = pl.BlockSpec(memory_space=pltpu.VMEM)
    smem = pl.BlockSpec(memory_space=pltpu.SMEM)
    halo = pltpu.VMEM((SPILL, COLS), BF)
    scratch = [
        pltpu.VMEM((2, NT, COLS, SEQ), BF),
        pltpu.VMEM((NT, COLS, SEQ), BF),
        pltpu.VMEM((MODEL, 3 * QW), BF),
        pltpu.VMEM((MODEL, QW), BF),
        halo, halo, halo, halo, halo, halo, halo, halo,
        pltpu.VMEM((2, 3, COLS, SEQ), BF),
        pltpu.VMEM((2, 2, COLS // 2, SEQ), BF),
        pltpu.VMEM((2, 2, COLS, SEQ), BF),
        pltpu.VMEM((NT, COLS, SEQ), F32),
        pltpu.VMEM((4, QW, SEQ), BF),
        pltpu.VMEM((4, QW, SEQ), BF),
        pltpu.VMEM((2, NX, KEPT, SEQ), BF),
        pltpu.VMEM((2, NX, KEPT, SEQ), BF),
        pltpu.VMEM((2, NX, KEPT, SEQ), BF),
        pltpu.VMEM((2, 3, KEPT, COLS), BF),
        pltpu.VMEM((2, 2, KEPT // 2, COLS), BF),
        pltpu.VMEM((2, 2, KEPT, COLS), BF),
        pltpu.VMEM((NZ, 2 * CORE_ROWS, COLS), BF),
        pltpu.VMEM((NZ, 2 * CORE_ROWS, COLS), BF),
        pltpu.SemaphoreType.DMA((COPIES,)),
        pltpu.SemaphoreType.DMA((COPIES,)),
    ]
    out_shape = (
        jax.ShapeDtypeStruct((COLS, SEQ), BF),
        jax.ShapeDtypeStruct((COLS, SRC), BF),
        jax.ShapeDtypeStruct((3, SHARE, QW), F32),
        jax.ShapeDtypeStruct((SHARE, QW), F32),
    )
    results = pl.pallas_call(
        kernel,
        out_shape=out_shape,
        in_specs=[smem, vmem, vmem, vmem, vmem, vmem],
        out_specs=(vmem, vmem, vmem, vmem),
        scratch_shapes=scratch,
        compiler_params=pltpu.CompilerParams(
            collective_id=0, has_side_effects=True, vmem_limit_bytes=56 * 1024 * 1024
        ),
    )(cut, seg_ids.reshape(1, SEQ), patches.T, w_qkv.reshape(3 * QW, MODEL), w_out, grad_out.T)
    mixed, grad_patches, qkv_grad, out_grad = pl.pallas_call(
        hand_out,
        out_shape=out_shape,
        in_specs=[vmem, vmem, vmem, vmem],
        out_specs=(vmem, vmem, vmem, vmem),
    )(*results)
    return mixed.T, grad_patches.T, jnp.swapaxes(qkv_grad, 1, 2), out_grad.T


def solution(mesh):
    in_specs = (
        P("dp", "tensor"),
        P("dp"),
        P("dp", None),
        P(None, "tensor", None),
        P("tensor", None),
        P("dp", "tensor"),
    )
    out_specs = (P("dp", "tensor"), P("dp", "tensor"), P(None, "tensor", "dp"), P("tensor", "dp"))
    return jax.shard_map(body, mesh=mesh, in_specs=in_specs, out_specs=out_specs, check_vma=False)
```

```python
import math

import jax
import jax.numpy as jnp
from jax import lax
from jax.experimental import pallas as pl
from jax.experimental.pallas import tpu as pltpu
from jax.sharding import PartitionSpec as P

HD = 88
SEQ = 256
SRC = 384
SPILL = 64
COLS = 352
MODEL = 1408
QW = 176
NT = 4
NX = 4
NZ = 8
SHARE = 22
XROWS = 16
ZROWS = SHARE - XROWS
KEPT = NZ * XROWS
REST = NX * ZROWS
norm_eps = 1e-06
score_scale = HD ** (-0.5)
total_scale = 1.0 / math.sqrt(16384.0)

BF = jnp.bfloat16
F32 = jnp.float32
MESH = pl.DeviceIdType.MESH


def dot(a, b, ca=1, cb=0):
    return lax.dot_general(a, b, (((ca,), (cb,)), ((), ())), preferred_element_type=F32)


def grid2(rows, cols):
    r = lax.broadcasted_iota(jnp.int32, (rows, cols), 0)
    c = lax.broadcasted_iota(jnp.int32, (rows, cols), 1)
    return r, c


def hot(mask):
    return jnp.where(mask, 1.0, 0.0).astype(BF)


def kernel(
    cut_ref, seg_ref, patches_in, wqkv_in, wout_in, gout_in,
    mixed_ref, gpatch_ref, gqkv_ref, gwout_ref,
    patches_ref, wqkv_ref, wout_ref, acts, x_full, w_t, wo_t,
    snd_next, snd_prev, from_prev, from_next, bsnd_next, bsnd_prev, bfrom_prev, bfrom_next,
    rs_send, rs_rin, rs_fin, share, gp_buf, gp_mate, own_sel, out_sel, mate_sel,
    z_pick, own_rest, out_rest, mate_rest,
    xs_send, xs_rin, xs_fin, z_send, z_recv, rz_send, rz_recv, rx_send, rx_recv,
    ssem, rsem, lsem,
):
    d = lax.axis_index("dp")
    t = lax.axis_index("tensor")
    xi = d // 16
    zi = lax.rem(d // 2, NZ)
    core = lax.rem(d, 2)
    inner = lax.rem(d, 16)
    t_right, t_left, t_far = lax.rem(t + 1, NT), lax.rem(t + 3, NT), lax.rem(t + 2, NT)
    x_right, x_left, x_far = lax.rem(xi + 1, NX), lax.rem(xi + 3, NX), lax.rem(xi + 2, NX)
    dp_next = (lax.rem(d + 1, 64), t)
    dp_prev = (lax.rem(d + 63, 64), t)
    mate = (d + 1 - 2 * core, t)
    y_right, y_left = (d, t_right), (d, t_left)
    px_right, px_left = (x_right * 16 + inner, t), (x_left * 16 + inner, t)
    z_peers = [
        (lax.rem(zi + k, NZ), (xi * 16 + lax.rem(zi + k, NZ) * 2 + core, t)) for k in (4, 3, 5, 2, 6, 1, 7)
    ]
    n_low, go_full = acts.at[0], acts.at[1]

    loads = [
        pltpu.make_async_copy(src, dst, lsem.at[k])
        for k, (src, dst) in enumerate(
            [
                (patches_in, patches_ref),
                (gout_in, go_full.at[t]),
                (wqkv_in, wqkv_ref),
                (wout_in, wout_ref),
            ]
        )
    ]
    for load in loads:
        load.start()

    barrier = pltpu.get_barrier_semaphore()
    px_far = (x_far * 16 + inner, t)
    greet = [dp_next, dp_prev, y_right, y_left, px_right, px_left, px_far]
    greet = greet + [p for _, p in z_peers]
    for peer in greet:
        pl.semaphore_signal(barrier, inc=1, device_id=peer, device_id_type=MESH)

    counter = [0]
    pending = []

    def remote(src, dst, dev):
        k = counter[0]
        counter[0] += 1
        copy = pltpu.make_async_remote_copy(
            src_ref=src, dst_ref=dst, send_sem=ssem.at[k], recv_sem=rsem.at[k],
            device_id=dev, device_id_type=MESH,
        )
        copy.start()
        pending.append(copy)
        return copy

    lower = cut_ref[0, 0]
    upper = cut_ref[0, 1]
    head = jnp.maximum(lower, 0)
    tail = jnp.maximum(-upper, 0)

    loads[0].wait()
    r, c = grid2(SPILL, SRC)
    base = SEQ - lower + jnp.minimum(upper, 0)
    snd_next[...] = dot(hot(c == r + base), patches_ref[...], 1, 1).astype(BF)
    snd_prev[...] = dot(hot(c == r), patches_ref[...], 1, 1).astype(BF)

    pl.semaphore_wait(barrier, len(greet))

    to_next = remote(snd_next, from_prev, dp_next)
    to_prev = remote(snd_prev, from_next, dp_prev)

    half = COLS // 2
    lo, hi = pl.ds(0, half), pl.ds(half, half)

    lo_pieces = pl.ds(0, 96), pl.ds(96, 80)
    hi_pieces = pl.ds(half, 96), pl.ds(half + 96, 80)

    def gather_handed(full):
        handed = []
        for low, high in zip(lo_pieces, hi_pieces):
            handed.append(remote(full.at[t, low], full.at[t, low], y_right))
            handed.append(remote(full.at[t, high], full.at[t, high], y_left))
        return handed

    def gather_other(full):
        rb = remote(full.at[t, hi], full.at[t, hi], y_right)
        la = remote(full.at[t, lo], full.at[t, lo], y_left)
        return [rb, la]

    def gather_relay(full, handed):
        rest = []
        for k, (low, high) in enumerate(zip(lo_pieces, hi_pieces)):
            handed[2 * k].wait_recv()
            rest.append(remote(full.at[t_left, low], full.at[t_left, low], y_right))
            handed[2 * k + 1].wait_recv()
            rest.append(remote(full.at[t_right, high], full.at[t_right, high], y_left))
        return rest

    def gather_finish(rest):
        for copy in rest:
            copy.wait_recv()

    loads[1].wait()
    go_handed = gather_handed(go_full)
    go_other = gather_other(go_full)

    r, c = grid2(SRC, SEQ)
    mine = (r == c - lower) & (c >= head) & (c < SEQ - tail)
    own = dot(patches_ref[...], hot(mine))
    r, c = grid2(SPILL, SEQ)
    pick_prev = hot((c == r) & (c < head))
    pick_next = hot((r == c - (SEQ - tail)) & (c >= SEQ - tail))
    loads[2].wait()
    loads[3].wait()
    w_t[...] = jnp.transpose(wqkv_ref[...])
    wo_t[...] = jnp.transpose(wout_ref[...])

    to_next.wait_recv()
    to_prev.wait_recv()
    own = own + dot(from_prev[...], pick_prev, 0, 0) + dot(from_next[...], pick_next, 0, 0)
    x_full[t] = own.astype(BF)
    x_handed = gather_handed(x_full)
    x_other = gather_other(x_full)
    go_rest = gather_relay(go_full, go_handed)

    r = lax.broadcasted_iota(jnp.int32, (KEPT, 1), 0)
    zk = sum((r >= k * XROWS).astype(jnp.int32) for k in range(1, NZ))
    at_x = r - zk * XROWS + 2 * SHARE * zk
    _, c = grid2(KEPT, COLS)
    x_own, x_mate = (hot(c == at_x + SHARE * side) for side in (core, 1 - core))
    r = lax.broadcasted_iota(jnp.int32, (NZ * REST, 1), 0)
    zk = sum((r >= k * REST).astype(jnp.int32) for k in range(1, NZ))
    r = r - zk * REST
    xk = sum((r >= k * ZROWS).astype(jnp.int32) for k in range(1, NX))
    at_z = r - xk * ZROWS + COLS * xk + 2 * SHARE * zk + XROWS
    _, c = grid2(NZ * REST, MODEL)
    z_pick[0] = hot(c == at_z + SHARE * core)
    z_pick[1] = hot(c == at_z + SHARE * (1 - core))

    def pick_rest(kind):
        everything = acts[kind].reshape(MODEL, SEQ)
        out_rest[kind] = dot(z_pick[1], everything).astype(BF)
        copy = remote(out_rest.at[kind], mate_rest.at[kind], mate)
        own_rest[kind] = dot(z_pick[0], everything).astype(BF)
        return copy

    def pick(kind, u):
        out_sel[kind, u] = dot(x_mate, acts[kind, u]).astype(BF)
        return remote(out_sel.at[kind, u], mate_sel.at[kind, u], mate)

    def pick_own(kind, u):
        own_sel[kind, u] = dot(x_own, acts[kind, u]).astype(BF)

    def rows_of(u):
        return x_full[u].astype(F32)

    def chunk_stats(u):
        rows = rows_of(u)
        centre = jnp.sum(rows, axis=0, keepdims=True) * (1.0 / COLS)
        rows = rows - centre
        return centre, jnp.sum(rows * rows, axis=0, keepdims=True)

    x_rest = gather_relay(x_full, x_handed)
    gather_finish(go_other)
    go_copies = [pick(1, u) for u in (t, t_left, t_right)]
    gather_finish(x_other)
    stats = [chunk_stats(u) for u in (t, t_left, t_right)]
    gather_finish(go_rest)
    go_copies.append(pick(1, t_far))
    go_copies.append(pick_rest(1))
    grad_att = dot(wout_ref[...], go_full[...].reshape(MODEL, SEQ))
    gas = [grad_att[h * HD : (h + 1) * HD].astype(BF) for h in range(2)]
    gather_finish(x_rest)
    stats.append(chunk_stats(t_far))

    mean = (stats[0][0] + stats[1][0] + stats[2][0] + stats[3][0]) * (1.0 / NT)
    spread = jnp.zeros((1, SEQ), F32)
    for centre, squares in stats:
        spread = spread + squares + COLS * (centre - mean) * (centre - mean)
    rstd = lax.rsqrt(spread * (1.0 / MODEL) + norm_eps)
    for u in range(NT):
        n_low[u] = ((rows_of(u) - mean) * rstd).astype(BF)
    proj = dot(wqkv_ref[...], n_low[...].reshape(MODEL, SEQ))
    n_copies = [pick(0, u) for u in range(NT)] + [pick_rest(0)]

    def head_norm(v):
        center = v - jnp.sum(v, axis=0, keepdims=True) * (1.0 / HD)
        var = jnp.sum(center * center, axis=0, keepdims=True) * (1.0 / HD)
        inverse = lax.rsqrt(var + norm_eps)
        return center * inverse, inverse

    def head_back(g, normed, inverse):
        first = jnp.sum(g, axis=0, keepdims=True) * (1.0 / HD)
        second = jnp.sum(g * normed, axis=0, keepdims=True) * (1.0 / HD)
        return inverse * (g - first - normed * second)

    seg_row = seg_ref[...].astype(F32)
    r, c = grid2(SEQ, SEQ)
    seg_col = jnp.sum(jnp.where(r == c, seg_row, 0.0), axis=-1, keepdims=True)
    same = seg_col == seg_row

    saved = []
    att_parts = []
    for h in range(2):
        q_hat, q_inv = head_norm(proj[h * HD : (h + 1) * HD])
        k_hat, k_inv = head_norm(proj[(2 + h) * HD : (3 + h) * HD])
        v = proj[(4 + h) * HD : (5 + h) * HD].astype(BF)
        q, k = q_hat.astype(BF), k_hat.astype(BF)
        raised = jnp.where(same, jnp.exp(dot(k, q, 0, 0) * score_scale), 0.0)
        weights = raised / jnp.sum(raised, axis=0, keepdims=True)
        weights_low = weights.astype(BF)
        att_parts.append(dot(v, weights_low))
        saved.append((q_hat, q_inv, k_hat, k_inv, q, k, v, weights, weights_low))
    att = jnp.concatenate(att_parts, axis=0).astype(BF)
    gp_buf[3] = att
    att_copy = remote(gp_buf.at[3], gp_mate.at[3], mate)

    def scatter_far(send, rin, make, far, to_right, to_left, cut_at):
        a, b = cut_at
        send[0] = make(far).astype(BF)
        ra = remote(send.at[0, a], rin.at[a], to_right)
        lb = remote(send.at[0, b], rin.at[b], to_left)
        return ra, lb

    def scatter_plain(send, fin, make, right, left, to_right, to_left, cut_at):
        a, b = cut_at
        send[1] = make(right).astype(BF)
        rb = remote(send.at[1, b], fin.at[0, b], to_right)
        send[2] = make(left).astype(BF)
        la = remote(send.at[2, a], fin.at[1, a], to_left)
        return rb, la

    def scatter_relay(send, rin, fin, first, plain, to_right, to_left, cut_at):
        a, b = cut_at
        ra, lb = first
        rb, la = plain
        ra.wait_recv()
        send[1, a] = (send[1, a].astype(F32) + rin[a].astype(F32)).astype(BF)
        fa = remote(send.at[1, a], fin.at[0, a], to_right)
        lb.wait_recv()
        send[2, b] = (send[2, b].astype(F32) + rin[b].astype(F32)).astype(BF)
        fb = remote(send.at[2, b], fin.at[1, b], to_left)
        return rb, la, fa, fb

    cut_y = lo, hi

    def branch(u):
        return dot(wo_t[pl.ds(pl.multiple_of(u * COLS, COLS), COLS), :], att)

    b_send, b_rin, b_fin = rs_send.at[0], rs_rin.at[0], rs_fin.at[0]

    b_far = scatter_far(b_send, b_rin, branch, t_far, y_right, y_left, cut_y)
    gvs = [dot(gas[h], saved[h][8], 1, 1) for h in range(2)]
    gp_buf[2] = jnp.concatenate(gvs, axis=0).astype(BF)
    v_copy = remote(gp_buf.at[2], gp_mate.at[2], mate)
    gqs, gks = [], []
    for h in range(2):
        q_hat, q_inv, k_hat, k_inv, q, k, v, weights, weights_low = saved[h]
        gw = dot(v, gas[h], 0, 0)
        inner_sum = jnp.sum(gw * weights, axis=0, keepdims=True)
        gs = (weights * (gw - inner_sum) * score_scale).astype(BF)
        gqs.append(head_back(dot(k, gs), q_hat, q_inv))
        gks.append(head_back(dot(q, gs, 1, 1), k_hat, k_inv))
    gp_buf[0] = jnp.concatenate(gqs, axis=0).astype(BF)
    gp_buf[1] = jnp.concatenate(gks, axis=0).astype(BF)
    qk_copy = remote(gp_buf.at[pl.ds(0, 2)], gp_mate.at[pl.ds(0, 2)], mate)

    def vo_of(n_own, n_mate, go_own, go_mate):
        first = dot(n_own, gp_buf[2], 1, 1) + dot(n_mate, gp_mate[2], 1, 1)
        second = dot(go_own, gp_buf[3], 1, 1) + dot(go_mate, gp_mate[3], 1, 1)
        return jnp.concatenate([first, second], axis=1)

    def qk_of(n_own, n_mate):
        ours = gp_buf[0:2].reshape(2 * QW, SEQ)
        theirs = gp_mate[0:2].reshape(2 * QW, SEQ)
        return dot(n_own, ours, 1, 1) + dot(n_mate, theirs, 1, 1)

    def grad_vo(u):
        return vo_of(own_sel[0, u], mate_sel[0, u], own_sel[1, u], mate_sel[1, u])

    def grad_qk(u):
        return qk_of(own_sel[0, u], mate_sel[0, u])

    cut_x = pl.ds(0, KEPT // 2), pl.ds(KEPT // 2, KEPT // 2)
    order = [x_far, x_right, x_left, xi]
    for u in order:
        pick_own(1, u)
        pick_own(0, u)
    for copy in n_copies + go_copies + [att_copy, v_copy]:
        copy.wait_recv()
    v_send, v_rin, v_fin = xs_send.at[0], xs_rin.at[0], xs_fin.at[0]
    q_send, q_rin, q_fin = xs_send.at[1], xs_rin.at[1], xs_fin.at[1]
    v_far = scatter_far(v_send, v_rin, grad_vo, x_far, px_right, px_left, cut_x)
    v_plain = scatter_plain(
        v_send, v_fin, grad_vo, x_right, x_left, px_right, px_left, cut_x
    )

    gp = gp_buf[0:3].reshape(3 * QW, SEQ)
    s1 = jnp.zeros((1, SEQ), F32)
    s2 = jnp.zeros((1, SEQ), F32)
    for u in range(NT):
        part = dot(w_t[u * COLS : (u + 1) * COLS, :], gp)
        share[u] = part
        s1 = s1 + jnp.sum(part, axis=0, keepdims=True)
        s2 = s2 + jnp.sum(part * ((rows_of(u) - mean) * rstd), axis=0, keepdims=True)
    s1 = s1 * (1.0 / MODEL)
    s2 = s2 * (1.0 / MODEL)

    def back(u):
        return rstd * (share[u] - s1 - ((rows_of(u) - mean) * rstd) * s2)

    g_send, g_rin, g_fin = rs_send.at[1], rs_rin.at[1], rs_fin.at[1]
    g_far = scatter_far(g_send, g_rin, back, t_far, y_right, y_left, cut_y)
    g_plain = scatter_plain(g_send, g_fin, back, t_right, t_left, y_right, y_left, cut_y)

    qk_copy.wait_recv()
    q_far = scatter_far(q_send, q_rin, grad_qk, x_far, px_right, px_left, cut_x)
    rest_q = qk_of(own_rest[0], mate_rest[0])
    rest_v = vo_of(own_rest[0], mate_rest[0], own_rest[1], mate_rest[1])
    for k in range(NZ):
        at = slice(k * REST, (k + 1) * REST)
        rz_send[k] = jnp.concatenate([rest_q[at], rest_v[at]], axis=0).astype(BF)
    rz_copies = [remote(rz_send.at[pz], rz_recv.at[zi], dev) for pz, dev in z_peers]
    q_plain = scatter_plain(
        q_send, q_fin, grad_qk, x_right, x_left, px_right, px_left, cut_x
    )
    v_rest = scatter_relay(v_send, v_rin, v_fin, v_far, v_plain, px_right, px_left, cut_x)
    g_rest = scatter_relay(g_send, g_rin, g_fin, g_far, g_plain, y_right, y_left, cut_y)
    q_rest = scatter_relay(q_send, q_rin, q_fin, q_far, q_plain, px_right, px_left, cut_x)
    b_plain = scatter_plain(b_send, b_fin, branch, t_right, t_left, y_right, y_left, cut_y)
    b_rest = scatter_relay(b_send, b_rin, b_fin, b_far, b_plain, y_right, y_left, cut_y)

    mixed_own = x_full[t].astype(F32) + branch(t)
    gx_own = go_full[t].astype(F32) + back(t)
    v_own = grad_vo(xi)
    q_own = grad_qk(xi)

    for copy in g_rest:
        copy.wait_recv()
    gx = (gx_own + g_fin[0].astype(F32) + g_fin[1].astype(F32)).astype(BF)
    r, c = grid2(SPILL, SEQ)
    bsnd_next[...] = dot(hot(c == r + SEQ - tail), gx, 1, 1).astype(BF)
    bsnd_prev[...] = dot(hot(c == r), gx, 1, 1).astype(BF)
    back_next = remote(bsnd_next, bfrom_prev, dp_next)
    back_prev = remote(bsnd_prev, bfrom_next, dp_prev)

    def along_z(rest, mine, fin, slot):
        for copy in rest:
            copy.wait_recv()
        summed = mine + fin[0].astype(F32) + fin[1].astype(F32)
        z_send[slot] = summed.astype(BF).reshape(NZ, XROWS, COLS)
        return [remote(z_send.at[slot, pz], z_recv.at[slot, zi], dev) for pz, dev in z_peers]

    vz_copies = along_z(v_rest, v_own, v_fin, 1)
    qz_copies = along_z(q_rest, q_own, q_fin, 0)

    rest = rz_send[zi].astype(F32)
    for copy in rz_copies:
        copy.wait_recv()
    for pz, _ in z_peers:
        rest = rest + rz_recv[pz].astype(F32)
    r, c = grid2(NX * XROWS, 2 * REST)
    mask = c < 0
    for k in range(NX):
        at = r - k * XROWS
        mask = mask | ((at >= 0) & (at < ZROWS) & (c == at + k * ZROWS))
        at = at - 8
        mask = mask | ((at >= 0) & (at < ZROWS) & (c == at + k * ZROWS + REST))
    rest = dot(hot(mask), rest.astype(BF)).astype(BF)
    rx_send[...] = rest.reshape(NX, XROWS, COLS)
    rx_copies = [
        remote(rx_send.at[px], rx_recv.at[xi], (px * 16 + inner, t))
        for px in (x_far, x_right, x_left)
    ]

    length = SEQ + upper - lower
    behind = jnp.maximum(-lower, 0)
    ahead = jnp.maximum(upper, 0)
    r, c = grid2(SEQ, SRC)
    mine = hot((r == c + lower) & (c >= behind) & (c < length - ahead))
    src_rows = dot(gx, mine)
    r, c = grid2(SPILL, SRC)
    pick_prev = hot((c == r) & (c < behind))
    pick_next = hot((r == c - (length - ahead)) & (c >= length - ahead) & (c < length))
    back_next.wait_recv()
    back_prev.wait_recv()
    src_rows = (
        src_rows + dot(bfrom_prev[...], pick_prev, 0, 0) + dot(bfrom_next[...], pick_next, 0, 0)
    )
    gpatch_ref[...] = src_rows.astype(BF)

    for copy in b_rest:
        copy.wait_recv()
    mixed_ref[...] = (mixed_own + b_fin[0].astype(F32) + b_fin[1].astype(F32)).astype(BF)

    last = rx_send[xi].astype(F32)
    for copy in rx_copies:
        copy.wait_recv()
    for px in (x_far, x_right, x_left):
        last = last + rx_recv[px].astype(F32)
    last = last * total_scale

    def finish(copies, slot):
        total = z_send[slot, zi].astype(F32)
        for copy in copies:
            copy.wait_recv()
        for pz, _ in z_peers:
            total = total + z_recv[slot, pz].astype(F32)
        return total * total_scale

    vo = finish(vz_copies, 1)
    qk = finish(qz_copies, 0)
    gqkv_ref[0, 0:XROWS] = qk[:, 0:QW]
    gqkv_ref[0, XROWS:SHARE] = last[0:ZROWS, 0:QW]
    gqkv_ref[1, 0:XROWS] = qk[:, QW : 2 * QW]
    gqkv_ref[1, XROWS:SHARE] = last[0:ZROWS, QW : 2 * QW]
    gqkv_ref[2, 0:XROWS] = vo[:, 0:QW]
    gqkv_ref[2, XROWS:SHARE] = last[8 : 8 + ZROWS, 0:QW]
    gwout_ref[0:XROWS] = vo[:, QW : 2 * QW]
    gwout_ref[XROWS:SHARE] = last[8 : 8 + ZROWS, QW : 2 * QW]

    for copy in pending:
        copy.wait_send()


def hand_out(a, b, c, e, a_out, b_out, c_out, e_out):
    a_out[...] = a[...]
    b_out[...] = b[...]
    c_out[...] = c[...]
    e_out[...] = e[...]


COPIES = 88


def body(patches, seg_ids, cut, w_qkv, w_out, grad_out):
    vmem = pl.BlockSpec(memory_space=pltpu.VMEM)
    anym = pl.BlockSpec(memory_space=pl.ANY)
    smem = pl.BlockSpec(memory_space=pltpu.SMEM)
    halo = pltpu.VMEM((SPILL, COLS), BF)
    scratch = [
        pltpu.VMEM((COLS, SRC), BF),
        pltpu.VMEM((3 * QW, MODEL), BF),
        pltpu.VMEM((QW, MODEL), BF),
        pltpu.VMEM((2, NT, COLS, SEQ), BF),
        pltpu.VMEM((NT, COLS, SEQ), BF),
        pltpu.VMEM((MODEL, 3 * QW), BF),
        pltpu.VMEM((MODEL, QW), BF),
        halo, halo, halo, halo, halo, halo, halo, halo,
        pltpu.VMEM((2, 3, COLS, SEQ), BF),
        pltpu.VMEM((2, COLS, SEQ), BF),
        pltpu.VMEM((2, 2, COLS, SEQ), BF),
        pltpu.VMEM((NT, COLS, SEQ), F32),
        pltpu.VMEM((4, QW, SEQ), BF),
        pltpu.VMEM((4, QW, SEQ), BF),
        pltpu.VMEM((2, NX, KEPT, SEQ), BF),
        pltpu.VMEM((2, NX, KEPT, SEQ), BF),
        pltpu.VMEM((2, NX, KEPT, SEQ), BF),
        pltpu.VMEM((2, NZ * REST, MODEL), BF),
        pltpu.VMEM((2, NZ * REST, SEQ), BF),
        pltpu.VMEM((2, NZ * REST, SEQ), BF),
        pltpu.VMEM((2, NZ * REST, SEQ), BF),
        pltpu.VMEM((2, 3, KEPT, COLS), BF),
        pltpu.VMEM((2, KEPT, COLS), BF),
        pltpu.VMEM((2, 2, KEPT, COLS), BF),
        pltpu.VMEM((2, NZ, XROWS, COLS), BF),
        pltpu.VMEM((2, NZ, XROWS, COLS), BF),
        pltpu.VMEM((NZ, 2 * REST, COLS), BF),
        pltpu.VMEM((NZ, 2 * REST, COLS), BF),
        pltpu.VMEM((NX, XROWS, COLS), BF),
        pltpu.VMEM((NX, XROWS, COLS), BF),
        pltpu.SemaphoreType.DMA((COPIES,)),
        pltpu.SemaphoreType.DMA((COPIES,)),
        pltpu.SemaphoreType.DMA((4,)),
    ]
    out_shape = (
        jax.ShapeDtypeStruct((COLS, SEQ), BF),
        jax.ShapeDtypeStruct((COLS, SRC), BF),
        jax.ShapeDtypeStruct((3, SHARE, QW), F32),
        jax.ShapeDtypeStruct((SHARE, QW), F32),
    )
    results = pl.pallas_call(
        kernel,
        out_shape=out_shape,
        in_specs=[smem, vmem, anym, anym, anym, anym],
        out_specs=(vmem, vmem, vmem, vmem),
        scratch_shapes=scratch,
        compiler_params=pltpu.CompilerParams(
            collective_id=0, has_side_effects=True, vmem_limit_bytes=56 * 1024 * 1024
        ),
    )(cut, seg_ids.reshape(1, SEQ), patches.T, w_qkv.reshape(3 * QW, MODEL), w_out, grad_out.T)
    mixed, grad_patches, qkv_grad, out_grad = pl.pallas_call(
        hand_out,
        out_shape=out_shape,
        in_specs=[vmem, vmem, vmem, vmem],
        out_specs=(vmem, vmem, vmem, vmem),
    )(*results)
    return mixed.T, grad_patches.T, jnp.swapaxes(qkv_grad, 1, 2), out_grad.T


def solution(mesh):
    in_specs = (
        P("dp", "tensor"),
        P("dp"),
        P("dp", None),
        P(None, "tensor", None),
        P("tensor", None),
        P("dp", "tensor"),
    )
    out_specs = (P("dp", "tensor"), P("dp", "tensor"), P(None, "tensor", "dp"), P("tensor", "dp"))
    return jax.shard_map(body, mesh=mesh, in_specs=in_specs, out_specs=out_specs, check_vma=False)
```

```python
import math

import jax
import jax.numpy as jnp
from jax import lax
from jax.experimental import pallas as pl
from jax.experimental.pallas import tpu as pltpu
from jax.sharding import PartitionSpec as P

HD = 88
SEQ = 256
SRC = 384
SPILL = 64
COLS = 352
MODEL = 1408
QW = 176
NT = 4
NX = 4
NZ = 8
SHARE = 22
XROWS = 16
ZROWS = SHARE - XROWS
KEPT = NZ * XROWS
REST = NX * ZROWS
norm_eps = 1e-06
score_scale = HD ** (-0.5)
total_scale = 1.0 / math.sqrt(16384.0)

BF = jnp.bfloat16
F32 = jnp.float32
MESH = pl.DeviceIdType.MESH


def dot(a, b, ca=1, cb=0):
    return lax.dot_general(a, b, (((ca,), (cb,)), ((), ())), preferred_element_type=F32)


def grid2(rows, cols):
    r = lax.broadcasted_iota(jnp.int32, (rows, cols), 0)
    c = lax.broadcasted_iota(jnp.int32, (rows, cols), 1)
    return r, c


def hot(mask):
    return jnp.where(mask, 1.0, 0.0).astype(BF)


def kernel(
    cut_in, seg_in, patches_in, wqkv_in, wout_in, gout_in,
    mixed_out, gpatch_out, gqkv_ref, gwout_ref,
    cut_ref, seg_ref, mixed_ref, gpatch_ref, patches_ref, wqkv_ref, wout_ref, acts, x_full, w_t, wo_t,
    snd_next, snd_prev, from_prev, from_next, bsnd_next, bsnd_prev, bfrom_prev, bfrom_next,
    rs_send, rs_rin, rs_fin, gp_buf, gp_mate, own_sel, out_sel, mate_sel,
    z_pick, own_rest, out_rest, mate_rest,
    xs_send, xs_rin, xs_fin, z_send, z_recv, rz_send, rz_recv, rx_send, rx_recv,
    ssem, rsem, lsem,
):
    d = lax.axis_index("dp")
    t = lax.axis_index("tensor")
    xi = d // 16
    zi = lax.rem(d // 2, NZ)
    core = lax.rem(d, 2)
    inner = lax.rem(d, 16)
    t_right, t_left, t_far = lax.rem(t + 1, NT), lax.rem(t + 3, NT), lax.rem(t + 2, NT)
    x_right, x_left, x_far = lax.rem(xi + 1, NX), lax.rem(xi + 3, NX), lax.rem(xi + 2, NX)
    dp_next = (lax.rem(d + 1, 64), t)
    dp_prev = (lax.rem(d + 63, 64), t)
    mate = (d + 1 - 2 * core, t)
    y_right, y_left = (d, t_right), (d, t_left)
    px_right, px_left = (x_right * 16 + inner, t), (x_left * 16 + inner, t)
    z_peers = [
        (lax.rem(zi + k, NZ), (xi * 16 + lax.rem(zi + k, NZ) * 2 + core, t)) for k in (4, 3, 5, 2, 6, 1, 7)
    ]
    n_low, go_full = acts.at[0], acts.at[1]

    barrier = pltpu.get_barrier_semaphore()
    px_far = (x_far * 16 + inner, t)
    greet = [dp_next, dp_prev, y_right, y_left, px_right, px_left, px_far]
    greet = greet + [p for _, p in z_peers]
    for peer in greet:
        pl.semaphore_signal(barrier, inc=1, device_id=peer, device_id_type=MESH)

    loads = [
        pltpu.make_async_copy(src, dst, lsem.at[k])
        for k, (src, dst) in enumerate(
            [
                (patches_in, patches_ref),
                (gout_in, go_full.at[t]),
                (wqkv_in, wqkv_ref),
                (wout_in, wout_ref),
                (cut_in, cut_ref),
                (seg_in, seg_ref),
            ]
        )
    ]
    for load in loads:
        load.start()

    counter = [0]
    pending = []

    def remote(src, dst, dev):
        k = counter[0]
        counter[0] += 1
        copy = pltpu.make_async_remote_copy(
            src_ref=src, dst_ref=dst, send_sem=ssem.at[k], recv_sem=rsem.at[k],
            device_id=dev, device_id_type=MESH,
        )
        copy.start()
        pending.append(copy)
        return copy

    loads[4].wait()
    lower = cut_ref[0, 0]
    upper = cut_ref[0, 1]
    head = jnp.maximum(lower, 0)
    tail = jnp.maximum(-upper, 0)

    loads[0].wait()
    r, c = grid2(SPILL, SRC)
    base = SEQ - lower + jnp.minimum(upper, 0)
    snd_next[...] = dot(hot(c == r + base), patches_ref[...], 1, 1).astype(BF)
    snd_prev[...] = dot(hot(c == r), patches_ref[...], 1, 1).astype(BF)

    pl.semaphore_wait(barrier, len(greet))

    to_next = remote(snd_next, from_prev, dp_next)
    to_prev = remote(snd_prev, from_next, dp_prev)

    half = COLS // 2
    lo, hi = pl.ds(0, half), pl.ds(half, half)

    lo_pieces, hi_pieces = (lo,), (hi,)

    def gather_handed(full):
        handed = []
        for low, high in zip(lo_pieces, hi_pieces):
            handed.append(remote(full.at[t, low], full.at[t, low], y_right))
            handed.append(remote(full.at[t, high], full.at[t, high], y_left))
        return handed

    def gather_other(full):
        rb = remote(full.at[t, hi], full.at[t, hi], y_right)
        la = remote(full.at[t, lo], full.at[t, lo], y_left)
        return [rb, la]

    def gather_relay(full, handed):
        rest = []
        for k, (low, high) in enumerate(zip(lo_pieces, hi_pieces)):
            handed[2 * k].wait_recv()
            rest.append(remote(full.at[t_left, low], full.at[t_left, low], y_right))
            handed[2 * k + 1].wait_recv()
            rest.append(remote(full.at[t_right, high], full.at[t_right, high], y_left))
        return rest

    def gather_finish(rest):
        for copy in rest:
            copy.wait_recv()

    loads[1].wait()
    go_handed = gather_handed(go_full)
    go_other = gather_other(go_full)

    r, c = grid2(SRC, SEQ)
    mine = (r == c - lower) & (c >= head) & (c < SEQ - tail)
    own = dot(patches_ref[...], hot(mine))
    r, c = grid2(SPILL, SEQ)
    pick_prev = hot((c == r) & (c < head))
    pick_next = hot((r == c - (SEQ - tail)) & (c >= SEQ - tail))
    loads[2].wait()
    loads[3].wait()
    w_t[...] = jnp.transpose(wqkv_ref[...])
    w_sums = jnp.sum(wqkv_ref[...].astype(F32), axis=-1, keepdims=True)
    wo_t[...] = jnp.transpose(wout_ref[...])

    to_next.wait_recv()
    to_prev.wait_recv()
    own = own + dot(from_prev[...], pick_prev, 0, 0) + dot(from_next[...], pick_next, 0, 0)
    x_full[t] = own.astype(BF)
    x_handed = gather_handed(x_full)
    x_other = gather_other(x_full)
    go_rest = gather_relay(go_full, go_handed)

    r = lax.broadcasted_iota(jnp.int32, (KEPT, 1), 0)
    zk = sum((r >= k * XROWS).astype(jnp.int32) for k in range(1, NZ))
    at_x = r - zk * XROWS + 2 * SHARE * zk
    _, c = grid2(KEPT, COLS)
    x_pick = jnp.concatenate([hot(c == at_x + SHARE * side) for side in (core, 1 - core)], axis=0)
    r = lax.broadcasted_iota(jnp.int32, (NZ * REST, 1), 0)
    zk = sum((r >= k * REST).astype(jnp.int32) for k in range(1, NZ))
    r = r - zk * REST
    xk = sum((r >= k * ZROWS).astype(jnp.int32) for k in range(1, NX))
    at_z = r - xk * ZROWS + COLS * xk + 2 * SHARE * zk + XROWS
    _, c = grid2(NZ * REST, MODEL)
    z_pick[0 : NZ * REST] = hot(c == at_z + SHARE * core)
    z_pick[NZ * REST :] = hot(c == at_z + SHARE * (1 - core))

    def pick_rest(kind):
        everything = acts[kind].reshape(MODEL, SEQ)
        both = dot(z_pick[...], everything).astype(BF)
        out_rest[kind] = both[NZ * REST :]
        own_rest[kind] = both[0 : NZ * REST]
        return remote(out_rest.at[kind], mate_rest.at[kind], mate)

    def pick(kind, u, send=True):
        both = dot(x_pick, acts[kind, u]).astype(BF)
        out_sel[kind, u] = both[KEPT:]
        own_sel[kind, u] = both[0:KEPT]
        return remote(out_sel.at[kind, u], mate_sel.at[kind, u], mate) if send else None

    def rows_of(u):
        return x_full[u].astype(F32)

    def chunk_stats(u):
        rows = rows_of(u)
        centre = jnp.sum(rows, axis=0, keepdims=True) * (1.0 / COLS)
        rows = rows - centre
        return centre, jnp.sum(rows * rows, axis=0, keepdims=True)

    x_rest = gather_relay(x_full, x_handed)
    gather_finish(go_other)
    for u in (t, t_left, t_right):
        pick(1, u, False)
    gather_finish(x_other)
    stats = [chunk_stats(u) for u in (t, t_left, t_right)]
    gather_finish(go_rest)
    pick(1, t_far, False)
    go_copies = [remote(out_sel.at[1], mate_sel.at[1], mate), pick_rest(1)]
    grad_att = dot(wout_ref[...], go_full[...].reshape(MODEL, SEQ))
    gas = [grad_att[h * HD : (h + 1) * HD].astype(BF) for h in range(2)]
    gather_finish(x_rest)
    stats.append(chunk_stats(t_far))

    mean = (stats[0][0] + stats[1][0] + stats[2][0] + stats[3][0]) * (1.0 / NT)
    spread = jnp.zeros((1, SEQ), F32)
    for centre, squares in stats:
        spread = spread + squares + COLS * (centre - mean) * (centre - mean)
    rstd = lax.rsqrt(spread * (1.0 / MODEL) + norm_eps)
    for u in range(NT):
        n_low[u] = ((rows_of(u) - mean) * rstd).astype(BF)
    proj = dot(wqkv_ref[...], n_low[...].reshape(MODEL, SEQ))
    for u in range(NT):
        pick(0, u, False)
    n_copies = [remote(out_sel.at[0], mate_sel.at[0], mate)]

    def head_norm(v):
        center = v - jnp.sum(v, axis=0, keepdims=True) * (1.0 / HD)
        var = jnp.sum(center * center, axis=0, keepdims=True) * (1.0 / HD)
        inverse = lax.rsqrt(var + norm_eps)
        return center * inverse, inverse

    def head_back(g, normed, inverse):
        first = jnp.sum(g, axis=0, keepdims=True) * (1.0 / HD)
        second = jnp.sum(g * normed, axis=0, keepdims=True) * (1.0 / HD)
        return inverse * (g - first - normed * second)

    loads[5].wait()
    seg_row = seg_ref[...].astype(F32)
    r, c = grid2(SEQ, SEQ)
    seg_col = jnp.sum(jnp.where(r == c, seg_row, 0.0), axis=-1, keepdims=True)
    same = seg_col == seg_row

    saved = []
    att_parts = []
    for h in range(2):
        q_hat, q_inv = head_norm(proj[h * HD : (h + 1) * HD])
        k_hat, k_inv = head_norm(proj[(2 + h) * HD : (3 + h) * HD])
        v = proj[(4 + h) * HD : (5 + h) * HD].astype(BF)
        q, k = q_hat.astype(BF), k_hat.astype(BF)
        raised = jnp.where(same, jnp.exp(dot(k, q, 0, 0) * score_scale), 0.0)
        weights = raised / jnp.sum(raised, axis=0, keepdims=True)
        weights_low = weights.astype(BF)
        att_parts.append(dot(v, weights_low))
        saved.append((q_hat, q_inv, k_hat, k_inv, q, k, v, weights, weights_low))
    att = jnp.concatenate(att_parts, axis=0).astype(BF)
    gp_buf[3] = att
    att_copy = remote(gp_buf.at[3], gp_mate.at[3], mate)

    def scatter_far(send, rin, make, far, to_right, to_left, cut_at):
        a, b = cut_at
        send[0] = make(far).astype(BF)
        ra = remote(send.at[0, a], rin.at[a], to_right)
        lb = remote(send.at[0, b], rin.at[b], to_left)
        return ra, lb

    def scatter_plain(send, fin, make, right, left, to_right, to_left, cut_at):
        a, b = cut_at
        send[1] = make(right).astype(BF)
        rb = remote(send.at[1, b], fin.at[0, b], to_right)
        send[2] = make(left).astype(BF)
        la = remote(send.at[2, a], fin.at[1, a], to_left)
        return rb, la

    def scatter_relay(send, rin, fin, first, plain, to_right, to_left, cut_at):
        a, b = cut_at
        ra, lb = first
        rb, la = plain
        ra.wait_recv()
        send[1, a] = (send[1, a].astype(F32) + rin[a].astype(F32)).astype(BF)
        fa = remote(send.at[1, a], fin.at[0, a], to_right)
        lb.wait_recv()
        send[2, b] = (send[2, b].astype(F32) + rin[b].astype(F32)).astype(BF)
        fb = remote(send.at[2, b], fin.at[1, b], to_left)
        return rb, la, fa, fb

    cut_y = lo, hi

    def branch(u):
        return dot(wo_t[pl.ds(pl.multiple_of(u * COLS, COLS), COLS), :], att)

    b_send, b_rin, b_fin = rs_send.at[0], rs_rin.at[0], rs_fin.at[0]

    b_far = scatter_far(b_send, b_rin, branch, t_far, y_right, y_left, cut_y)
    gvs = [dot(gas[h], saved[h][8], 1, 1) for h in range(2)]
    gp_buf[2] = jnp.concatenate(gvs, axis=0).astype(BF)
    v_copy = remote(gp_buf.at[2], gp_mate.at[2], mate)
    gqs, gks = [], []
    for h in range(2):
        q_hat, q_inv, k_hat, k_inv, q, k, v, weights, weights_low = saved[h]
        gw = dot(v, gas[h], 0, 0)
        inner_sum = jnp.sum(gw * weights, axis=0, keepdims=True)
        gs = (weights * (gw - inner_sum) * score_scale).astype(BF)
        gqs.append(head_back(dot(k, gs), q_hat, q_inv))
        gks.append(head_back(dot(q, gs, 1, 1), k_hat, k_inv))
    gp_buf[0] = jnp.concatenate(gqs, axis=0).astype(BF)
    gp_buf[1] = jnp.concatenate(gks, axis=0).astype(BF)
    qk_copy = remote(gp_buf.at[pl.ds(0, 2)], gp_mate.at[pl.ds(0, 2)], mate)

    def vo_of(n_own, n_mate, go_own, go_mate):
        first = dot(n_own, gp_buf[2], 1, 1) + dot(n_mate, gp_mate[2], 1, 1)
        second = dot(go_own, gp_buf[3], 1, 1) + dot(go_mate, gp_mate[3], 1, 1)
        return jnp.concatenate([first, second], axis=1)

    def qk_of(n_own, n_mate):
        ours = gp_buf[0:2].reshape(2 * QW, SEQ)
        theirs = gp_mate[0:2].reshape(2 * QW, SEQ)
        return dot(n_own, ours, 1, 1) + dot(n_mate, theirs, 1, 1)

    def grad_vo(u):
        return vo_of(own_sel[0, u], mate_sel[0, u], own_sel[1, u], mate_sel[1, u])

    def grad_qk(u):
        return qk_of(own_sel[0, u], mate_sel[0, u])

    cut_x = pl.ds(0, KEPT // 2), pl.ds(KEPT // 2, KEPT // 2)
    order = [x_far, x_right, x_left, xi]
    rest_copy = pick_rest(0)
    for copy in n_copies + go_copies + [att_copy, v_copy]:
        copy.wait_recv()
    v_send, v_rin, v_fin = xs_send.at[0], xs_rin.at[0], xs_fin.at[0]
    q_send, q_rin, q_fin = xs_send.at[1], xs_rin.at[1], xs_fin.at[1]
    v_far = scatter_far(v_send, v_rin, grad_vo, x_far, px_right, px_left, cut_x)
    v_plain = scatter_plain(
        v_send, v_fin, grad_vo, x_right, x_left, px_right, px_left, cut_x
    )

    gp = gp_buf[0:3].reshape(3 * QW, SEQ)
    gp_wide = gp.astype(F32)
    s1 = jnp.sum(gp_wide * w_sums, axis=0, keepdims=True) * (1.0 / MODEL)
    s2 = jnp.sum(gp_wide * proj, axis=0, keepdims=True) * (1.0 / MODEL)

    def back(u):
        part = dot(w_t[pl.ds(pl.multiple_of(u * COLS, COLS), COLS), :], gp)
        return rstd * (part - s1 - ((rows_of(u) - mean) * rstd) * s2)

    g_send, g_rin, g_fin = rs_send.at[1], rs_rin.at[1], rs_fin.at[1]
    g_far = scatter_far(g_send, g_rin, back, t_far, y_right, y_left, cut_y)
    g_plain = scatter_plain(g_send, g_fin, back, t_right, t_left, y_right, y_left, cut_y)

    qk_copy.wait_recv()
    q_far = scatter_far(q_send, q_rin, grad_qk, x_far, px_right, px_left, cut_x)
    rest_copy.wait_recv()
    rest_q = qk_of(own_rest[0], mate_rest[0])
    rest_v = vo_of(own_rest[0], mate_rest[0], own_rest[1], mate_rest[1])
    for k in range(NZ):
        at = slice(k * REST, (k + 1) * REST)
        rz_send[k] = jnp.concatenate([rest_q[at], rest_v[at]], axis=0).astype(BF)
    rz_copies = [remote(rz_send.at[pz], rz_recv.at[zi], dev) for pz, dev in z_peers]
    q_plain = scatter_plain(
        q_send, q_fin, grad_qk, x_right, x_left, px_right, px_left, cut_x
    )
    v_rest = scatter_relay(v_send, v_rin, v_fin, v_far, v_plain, px_right, px_left, cut_x)
    g_rest = scatter_relay(g_send, g_rin, g_fin, g_far, g_plain, y_right, y_left, cut_y)
    q_rest = scatter_relay(q_send, q_rin, q_fin, q_far, q_plain, px_right, px_left, cut_x)
    b_plain = scatter_plain(b_send, b_fin, branch, t_right, t_left, y_right, y_left, cut_y)
    b_rest = scatter_relay(b_send, b_rin, b_fin, b_far, b_plain, y_right, y_left, cut_y)

    mixed_own = x_full[t].astype(F32) + branch(t)
    gx_own = go_full[t].astype(F32) + back(t)
    v_own = grad_vo(xi)
    q_own = grad_qk(xi)

    for copy in g_rest:
        copy.wait_recv()
    gx = (gx_own + g_fin[0].astype(F32) + g_fin[1].astype(F32)).astype(BF)
    r, c = grid2(SPILL, SEQ)
    bsnd_next[...] = dot(hot(c == r + SEQ - tail), gx, 1, 1).astype(BF)
    bsnd_prev[...] = dot(hot(c == r), gx, 1, 1).astype(BF)
    back_next = remote(bsnd_next, bfrom_prev, dp_next)
    back_prev = remote(bsnd_prev, bfrom_next, dp_prev)

    def along_z(rest, mine, fin, slot):
        for copy in rest:
            copy.wait_recv()
        summed = mine + fin[0].astype(F32) + fin[1].astype(F32)
        z_send[slot] = summed.astype(BF).reshape(NZ, XROWS, COLS)
        return [remote(z_send.at[slot, pz], z_recv.at[slot, zi], dev) for pz, dev in z_peers]

    earlier = list(pending)
    pending.clear()
    vz_copies = along_z(v_rest, v_own, v_fin, 1)
    qz_copies = along_z(q_rest, q_own, q_fin, 0)

    rest = rz_send[zi].astype(F32)
    for copy in rz_copies:
        copy.wait_recv()
    for pz, _ in z_peers:
        rest = rest + rz_recv[pz].astype(F32)
    r, c = grid2(NX * XROWS, 2 * REST)
    mask = c < 0
    for k in range(NX):
        at = r - k * XROWS
        mask = mask | ((at >= 0) & (at < ZROWS) & (c == at + k * ZROWS))
        at = at - 8
        mask = mask | ((at >= 0) & (at < ZROWS) & (c == at + k * ZROWS + REST))
    rest = dot(hot(mask), rest.astype(BF)).astype(BF)
    rx_send[...] = rest.reshape(NX, XROWS, COLS)
    rx_copies = [
        remote(rx_send.at[px], rx_recv.at[xi], (px * 16 + inner, t))
        for px in (x_far, x_right, x_left)
    ]

    length = SEQ + upper - lower
    behind = jnp.maximum(-lower, 0)
    ahead = jnp.maximum(upper, 0)
    r, c = grid2(SEQ, SRC)
    mine = hot((r == c + lower) & (c >= behind) & (c < length - ahead))
    src_rows = dot(gx, mine)
    r, c = grid2(SPILL, SRC)
    pick_prev = hot((c == r) & (c < behind))
    pick_next = hot((r == c - (length - ahead)) & (c >= length - ahead) & (c < length))
    back_next.wait_recv()
    back_prev.wait_recv()
    src_rows = (
        src_rows + dot(bfrom_prev[...], pick_prev, 0, 0) + dot(bfrom_next[...], pick_next, 0, 0)
    )
    gpatch_ref[...] = src_rows.astype(BF)
    gpatch_copy = pltpu.make_async_copy(gpatch_ref, gpatch_out, lsem.at[6])
    gpatch_copy.start()

    for copy in earlier:
        copy.wait_send()
    for copy in b_rest:
        copy.wait_recv()
    mixed_ref[...] = (mixed_own + b_fin[0].astype(F32) + b_fin[1].astype(F32)).astype(BF)
    mixed_copy = pltpu.make_async_copy(mixed_ref, mixed_out, lsem.at[7])
    mixed_copy.start()

    last = rx_send[xi].astype(F32)
    for copy in rx_copies:
        copy.wait_recv()
    for px in (x_far, x_right, x_left):
        last = last + rx_recv[px].astype(F32)
    last = last * total_scale

    def finish(copies, slot):
        total = z_send[slot, zi].astype(F32)
        for copy in copies:
            copy.wait_recv()
        for pz, _ in z_peers:
            total = total + z_recv[slot, pz].astype(F32)
        return total * total_scale

    vo = finish(vz_copies, 1)
    qk = finish(qz_copies, 0)
    gqkv_ref[0, 0:XROWS] = qk[:, 0:QW]
    gqkv_ref[0, XROWS:SHARE] = last[0:ZROWS, 0:QW]
    gqkv_ref[1, 0:XROWS] = qk[:, QW : 2 * QW]
    gqkv_ref[1, XROWS:SHARE] = last[0:ZROWS, QW : 2 * QW]
    gqkv_ref[2, 0:XROWS] = vo[:, 0:QW]
    gqkv_ref[2, XROWS:SHARE] = last[8 : 8 + ZROWS, 0:QW]
    gwout_ref[0:XROWS] = vo[:, QW : 2 * QW]
    gwout_ref[XROWS:SHARE] = last[8 : 8 + ZROWS, QW : 2 * QW]

    for copy in pending:
        copy.wait_send()
    gpatch_copy.wait()
    mixed_copy.wait()


def hand_out(a, b, c, e, a_out, b_out, c_out, e_out):
    a_out[...] = a[...]
    b_out[...] = b[...]
    c_out[...] = c[...]
    e_out[...] = e[...]


COPIES = 88


def body(patches, seg_ids, cut, w_qkv, w_out, grad_out):
    vmem = pl.BlockSpec(memory_space=pltpu.VMEM)
    anym = pl.BlockSpec(memory_space=pl.ANY)
    halo = pltpu.VMEM((SPILL, COLS), BF)
    scratch = [
        pltpu.SMEM((1, 2), jnp.int32),
        pltpu.VMEM((1, SEQ), jnp.int32),
        pltpu.VMEM((COLS, SEQ), BF),
        pltpu.VMEM((COLS, SRC), BF),
        pltpu.VMEM((COLS, SRC), BF),
        pltpu.VMEM((3 * QW, MODEL), BF),
        pltpu.VMEM((QW, MODEL), BF),
        pltpu.VMEM((2, NT, COLS, SEQ), BF),
        pltpu.VMEM((NT, COLS, SEQ), BF),
        pltpu.VMEM((MODEL, 3 * QW), BF),
        pltpu.VMEM((MODEL, QW), BF),
        halo, halo, halo, halo, halo, halo, halo, halo,
        pltpu.VMEM((2, 3, COLS, SEQ), BF),
        pltpu.VMEM((2, COLS, SEQ), BF),
        pltpu.VMEM((2, 2, COLS, SEQ), BF),
        pltpu.VMEM((4, QW, SEQ), BF),
        pltpu.VMEM((4, QW, SEQ), BF),
        pltpu.VMEM((2, NX, KEPT, SEQ), BF),
        pltpu.VMEM((2, NX, KEPT, SEQ), BF),
        pltpu.VMEM((2, NX, KEPT, SEQ), BF),
        pltpu.VMEM((2 * NZ * REST, MODEL), BF),
        pltpu.VMEM((2, NZ * REST, SEQ), BF),
        pltpu.VMEM((2, NZ * REST, SEQ), BF),
        pltpu.VMEM((2, NZ * REST, SEQ), BF),
        pltpu.VMEM((2, 3, KEPT, COLS), BF),
        pltpu.VMEM((2, KEPT, COLS), BF),
        pltpu.VMEM((2, 2, KEPT, COLS), BF),
        pltpu.VMEM((2, NZ, XROWS, COLS), BF),
        pltpu.VMEM((2, NZ, XROWS, COLS), BF),
        pltpu.VMEM((NZ, 2 * REST, COLS), BF),
        pltpu.VMEM((NZ, 2 * REST, COLS), BF),
        pltpu.VMEM((NX, XROWS, COLS), BF),
        pltpu.VMEM((NX, XROWS, COLS), BF),
        pltpu.SemaphoreType.DMA((COPIES,)),
        pltpu.SemaphoreType.DMA((COPIES,)),
        pltpu.SemaphoreType.DMA((8,)),
    ]
    out_shape = (
        jax.ShapeDtypeStruct((COLS, SEQ), BF),
        jax.ShapeDtypeStruct((COLS, SRC), BF),
        jax.ShapeDtypeStruct((3, SHARE, QW), F32),
        jax.ShapeDtypeStruct((SHARE, QW), F32),
    )
    results = pl.pallas_call(
        kernel,
        out_shape=out_shape,
        in_specs=[anym, anym, anym, anym, anym, anym],
        out_specs=(anym, anym, vmem, vmem),
        scratch_shapes=scratch,
        compiler_params=pltpu.CompilerParams(
            collective_id=0, has_side_effects=True, vmem_limit_bytes=56 * 1024 * 1024
        ),
    )(cut, seg_ids.reshape(1, SEQ), patches.T, w_qkv.reshape(3 * QW, MODEL), w_out, grad_out.T)
    mixed, grad_patches, qkv_grad, out_grad = pl.pallas_call(
        hand_out,
        out_shape=out_shape,
        in_specs=[vmem, vmem, vmem, vmem],
        out_specs=(vmem, vmem, vmem, vmem),
    )(*results)
    return mixed.T, grad_patches.T, jnp.swapaxes(qkv_grad, 1, 2), out_grad.T


def solution(mesh):
    in_specs = (
        P("dp", "tensor"),
        P("dp"),
        P("dp", None),
        P(None, "tensor", None),
        P("tensor", None),
        P("dp", "tensor"),
    )
    out_specs = (P("dp", "tensor"), P("dp", "tensor"), P(None, "tensor", "dp"), P("tensor", "dp"))
    return jax.shard_map(body, mesh=mesh, in_specs=in_specs, out_specs=out_specs, check_vma=False)
```

```python
import math

import jax
import jax.numpy as jnp
from jax import lax
from jax.experimental import pallas as pl
from jax.experimental.pallas import tpu as pltpu
from jax.sharding import PartitionSpec as P

HD = 88
SEQ = 256
SRC = 384
SPILL = 64
COLS = 352
MODEL = 1408
QW = 176
NT = 4
NX = 4
NZ = 8
SHARE = 22
XROWS = 16
ZROWS = SHARE - XROWS
KEPT = NZ * XROWS
REST = NX * ZROWS
norm_eps = 1e-06
score_scale = HD ** (-0.5)
total_scale = 1.0 / math.sqrt(16384.0)

BF = jnp.bfloat16
F32 = jnp.float32
MESH = pl.DeviceIdType.MESH


def dot(a, b, ca=1, cb=0):
    return lax.dot_general(a, b, (((ca,), (cb,)), ((), ())), preferred_element_type=F32)


def grid2(rows, cols):
    r = lax.broadcasted_iota(jnp.int32, (rows, cols), 0)
    c = lax.broadcasted_iota(jnp.int32, (rows, cols), 1)
    return r, c


def hot(mask):
    return jnp.where(mask, 1.0, 0.0).astype(BF)


def kernel(
    cut_in, seg_in, patches_in, wqkv_in, wout_in, gout_in,
    mixed_out, gpatch_out, gqkv_ref, gwout_ref,
    cut_ref, seg_ref, mixed_ref, gpatch_ref, patches_ref, wqkv_ref, wout_ref, acts, x_full, w_t, wo_t,
    snd_next, snd_prev, from_prev, from_next, bsnd_next, bsnd_prev, bfrom_prev, bfrom_next,
    rs_send, rs_rin, rs_fin, gp_buf, gp_mate, own_sel, out_sel, mate_sel,
    z_pick, own_rest, out_rest, mate_rest,
    xs_send, xs_rin, xs_fin, z_send, z_recv, rz_send, rz_recv, rx_send, rx_recv,
    ssem, rsem, lsem,
):
    d = lax.axis_index("dp")
    t = lax.axis_index("tensor")
    xi = d // 16
    zi = lax.rem(d // 2, NZ)
    core = lax.rem(d, 2)
    inner = lax.rem(d, 16)
    t_right, t_left, t_far = lax.rem(t + 1, NT), lax.rem(t + 3, NT), lax.rem(t + 2, NT)
    x_right, x_left, x_far = lax.rem(xi + 1, NX), lax.rem(xi + 3, NX), lax.rem(xi + 2, NX)
    dp_next = (lax.rem(d + 1, 64), t)
    dp_prev = (lax.rem(d + 63, 64), t)
    mate = (d + 1 - 2 * core, t)
    y_right, y_left = (d, t_right), (d, t_left)
    px_right, px_left = (x_right * 16 + inner, t), (x_left * 16 + inner, t)
    z_peers = [
        (lax.rem(zi + k, NZ), (xi * 16 + lax.rem(zi + k, NZ) * 2 + core, t)) for k in (4, 1, 3, 7, 5, 2, 6)
    ]
    n_low, go_full = acts.at[0], acts.at[1]

    barrier = pltpu.get_barrier_semaphore()
    px_far = (x_far * 16 + inner, t)
    greet = [dp_next, dp_prev, y_right, y_left, px_right, px_left, px_far]
    greet = greet + [p for _, p in z_peers]
    for peer in greet:
        pl.semaphore_signal(barrier, inc=1, device_id=peer, device_id_type=MESH)

    loads = [
        pltpu.make_async_copy(src, dst, lsem.at[k])
        for k, (src, dst) in enumerate(
            [
                (patches_in, patches_ref),
                (gout_in, go_full.at[t]),
                (wqkv_in, wqkv_ref),
                (wout_in, wout_ref),
                (cut_in, cut_ref),
                (seg_in, seg_ref),
            ]
        )
    ]
    for load in loads:
        load.start()

    counter = [0]
    pending = []

    def remote(src, dst, dev):
        k = counter[0]
        counter[0] += 1
        copy = pltpu.make_async_remote_copy(
            src_ref=src, dst_ref=dst, send_sem=ssem.at[k], recv_sem=rsem.at[k],
            device_id=dev, device_id_type=MESH,
        )
        copy.start()
        pending.append(copy)
        return copy

    loads[4].wait()
    lower = cut_ref[0, 0]
    upper = cut_ref[0, 1]
    head = jnp.maximum(lower, 0)
    tail = jnp.maximum(-upper, 0)

    loads[0].wait()
    r, c = grid2(SPILL, SRC)
    base = SEQ - lower + jnp.minimum(upper, 0)
    snd_next[...] = dot(hot(c == r + base), patches_ref[...], 1, 1).astype(BF)
    snd_prev[...] = dot(hot(c == r), patches_ref[...], 1, 1).astype(BF)

    pl.semaphore_wait(barrier, len(greet))

    to_next = remote(snd_next, from_prev, dp_next)
    to_prev = remote(snd_prev, from_next, dp_prev)

    half = COLS // 2
    lo, hi = pl.ds(0, half), pl.ds(half, half)

    lo_pieces, hi_pieces = (lo,), (hi,)

    def gather_handed(full):
        handed = []
        for low, high in zip(lo_pieces, hi_pieces):
            handed.append(remote(full.at[t, low], full.at[t, low], y_right))
            handed.append(remote(full.at[t, high], full.at[t, high], y_left))
        return handed

    def gather_other(full):
        rb = remote(full.at[t, hi], full.at[t, hi], y_right)
        la = remote(full.at[t, lo], full.at[t, lo], y_left)
        return [rb, la]

    def gather_relay(full, handed):
        rest = []
        for k, (low, high) in enumerate(zip(lo_pieces, hi_pieces)):
            handed[2 * k].wait_recv()
            rest.append(remote(full.at[t_left, low], full.at[t_left, low], y_right))
            handed[2 * k + 1].wait_recv()
            rest.append(remote(full.at[t_right, high], full.at[t_right, high], y_left))
        return rest

    def gather_finish(rest):
        for copy in rest:
            copy.wait_recv()

    loads[1].wait()
    go_handed = gather_handed(go_full)
    go_other = gather_other(go_full)

    r, c = grid2(SRC, SEQ)
    mine = (r == c - lower) & (c >= head) & (c < SEQ - tail)
    own = dot(patches_ref[...], hot(mine))
    r, c = grid2(SPILL, SEQ)
    pick_prev = hot((c == r) & (c < head))
    pick_next = hot((r == c - (SEQ - tail)) & (c >= SEQ - tail))
    loads[2].wait()
    loads[3].wait()
    w_t[...] = jnp.transpose(wqkv_ref[...])
    w_sums = jnp.sum(wqkv_ref[...].astype(F32), axis=-1, keepdims=True)
    wo_t[...] = jnp.transpose(wout_ref[...])

    to_next.wait_recv()
    to_prev.wait_recv()
    own = own + dot(from_prev[...], pick_prev, 0, 0) + dot(from_next[...], pick_next, 0, 0)
    x_full[t] = own.astype(BF)
    x_handed = gather_handed(x_full)
    x_other = gather_other(x_full)
    go_rest = gather_relay(go_full, go_handed)

    r = lax.broadcasted_iota(jnp.int32, (KEPT, 1), 0)
    zk = sum((r >= k * XROWS).astype(jnp.int32) for k in range(1, NZ))
    at_x = r - zk * XROWS + 2 * SHARE * zk
    _, c = grid2(KEPT, COLS)
    x_pick = jnp.concatenate([hot(c == at_x + SHARE * side) for side in (core, 1 - core)], axis=0)
    r = lax.broadcasted_iota(jnp.int32, (NZ * REST, 1), 0)
    zk = sum((r >= k * REST).astype(jnp.int32) for k in range(1, NZ))
    r = r - zk * REST
    xk = sum((r >= k * ZROWS).astype(jnp.int32) for k in range(1, NX))
    at_z = r - xk * ZROWS + COLS * xk + 2 * SHARE * zk + XROWS
    _, c = grid2(NZ * REST, MODEL)
    z_pick[0 : NZ * REST] = hot(c == at_z + SHARE * core)
    z_pick[NZ * REST :] = hot(c == at_z + SHARE * (1 - core))

    def pick_rest(kind):
        everything = acts[kind].reshape(MODEL, SEQ)
        both = dot(z_pick[...], everything).astype(BF)
        out_rest[kind] = both[NZ * REST :]
        own_rest[kind] = both[0 : NZ * REST]
        return remote(out_rest.at[kind], mate_rest.at[kind], mate)

    def pick(kind, u, send=True):
        both = dot(x_pick, acts[kind, u]).astype(BF)
        out_sel[kind, u] = both[KEPT:]
        own_sel[kind, u] = both[0:KEPT]
        return remote(out_sel.at[kind, u], mate_sel.at[kind, u], mate) if send else None

    def rows_of(u):
        return x_full[u].astype(F32)

    def chunk_stats(u):
        rows = rows_of(u)
        centre = jnp.sum(rows, axis=0, keepdims=True) * (1.0 / COLS)
        rows = rows - centre
        return centre, jnp.sum(rows * rows, axis=0, keepdims=True)

    x_rest = gather_relay(x_full, x_handed)
    gather_finish(go_other)
    for u in (t, t_left, t_right):
        pick(1, u, False)
    gather_finish(x_other)
    stats = [chunk_stats(u) for u in (t, t_left, t_right)]
    gather_finish(go_rest)
    pick(1, t_far, False)
    go_copies = [remote(out_sel.at[1], mate_sel.at[1], mate), pick_rest(1)]
    grad_att = dot(wout_ref[...], go_full[...].reshape(MODEL, SEQ))
    gas = [grad_att[h * HD : (h + 1) * HD].astype(BF) for h in range(2)]
    gather_finish(x_rest)
    stats.append(chunk_stats(t_far))

    mean = (stats[0][0] + stats[1][0] + stats[2][0] + stats[3][0]) * (1.0 / NT)
    spread = jnp.zeros((1, SEQ), F32)
    for centre, squares in stats:
        spread = spread + squares + COLS * (centre - mean) * (centre - mean)
    rstd = lax.rsqrt(spread * (1.0 / MODEL) + norm_eps)
    for u in range(NT):
        n_low[u] = ((rows_of(u) - mean) * rstd).astype(BF)
    proj = dot(wqkv_ref[...], n_low[...].reshape(MODEL, SEQ))
    for u in range(NT):
        pick(0, u, False)
    n_copies = [remote(out_sel.at[0], mate_sel.at[0], mate)]

    def head_norm(v):
        center = v - jnp.sum(v, axis=0, keepdims=True) * (1.0 / HD)
        var = jnp.sum(center * center, axis=0, keepdims=True) * (1.0 / HD)
        inverse = lax.rsqrt(var + norm_eps)
        return center * inverse, inverse

    def head_back(g, normed, inverse):
        first = jnp.sum(g, axis=0, keepdims=True) * (1.0 / HD)
        second = jnp.sum(g * normed, axis=0, keepdims=True) * (1.0 / HD)
        return inverse * (g - first - normed * second)

    loads[5].wait()
    seg_row = seg_ref[...].astype(F32)
    r, c = grid2(SEQ, SEQ)
    seg_col = jnp.sum(jnp.where(r == c, seg_row, 0.0), axis=-1, keepdims=True)
    same = seg_col == seg_row

    saved = []
    att_parts = []
    for h in range(2):
        q_hat, q_inv = head_norm(proj[h * HD : (h + 1) * HD])
        k_hat, k_inv = head_norm(proj[(2 + h) * HD : (3 + h) * HD])
        v = proj[(4 + h) * HD : (5 + h) * HD].astype(BF)
        q, k = q_hat.astype(BF), k_hat.astype(BF)
        raised = jnp.where(same, jnp.exp(dot(k, q, 0, 0) * score_scale), 0.0)
        weights = raised / jnp.sum(raised, axis=0, keepdims=True)
        weights_low = weights.astype(BF)
        att_parts.append(dot(v, weights_low))
        saved.append((q_hat, q_inv, k_hat, k_inv, q, k, v, weights, weights_low))
    att = jnp.concatenate(att_parts, axis=0).astype(BF)
    gp_buf[3] = att

    def scatter_far(send, rin, make, far, to_right, to_left, cut_at):
        a, b = cut_at
        send[0] = make(far).astype(BF)
        ra = remote(send.at[0, a], rin.at[a], to_right)
        lb = remote(send.at[0, b], rin.at[b], to_left)
        return ra, lb

    def scatter_plain(send, fin, make, right, left, to_right, to_left, cut_at):
        a, b = cut_at
        send[1] = make(right).astype(BF)
        rb = remote(send.at[1, b], fin.at[0, b], to_right)
        send[2] = make(left).astype(BF)
        la = remote(send.at[2, a], fin.at[1, a], to_left)
        return rb, la

    def scatter_relay(send, rin, fin, first, plain, to_right, to_left, cut_at):
        a, b = cut_at
        ra, lb = first
        rb, la = plain
        ra.wait_recv()
        send[1, a] = (send[1, a].astype(F32) + rin[a].astype(F32)).astype(BF)
        fa = remote(send.at[1, a], fin.at[0, a], to_right)
        lb.wait_recv()
        send[2, b] = (send[2, b].astype(F32) + rin[b].astype(F32)).astype(BF)
        fb = remote(send.at[2, b], fin.at[1, b], to_left)
        return rb, la, fa, fb

    cut_y = lo, hi

    def branch(u):
        return dot(wo_t[pl.ds(pl.multiple_of(u * COLS, COLS), COLS), :], att)

    b_send, b_rin, b_fin = rs_send.at[0], rs_rin.at[0], rs_fin.at[0]

    b_far = scatter_far(b_send, b_rin, branch, t_far, y_right, y_left, cut_y)
    gvs = [dot(gas[h], saved[h][8], 1, 1) for h in range(2)]
    gp_buf[2] = jnp.concatenate(gvs, axis=0).astype(BF)
    v_copy = remote(gp_buf.at[pl.ds(2, 2)], gp_mate.at[pl.ds(2, 2)], mate)
    gqs, gks = [], []
    for h in range(2):
        q_hat, q_inv, k_hat, k_inv, q, k, v, weights, weights_low = saved[h]
        gw = dot(v, gas[h], 0, 0)
        inner_sum = jnp.sum(gw * weights, axis=0, keepdims=True)
        gs = (weights * (gw - inner_sum) * score_scale).astype(BF)
        gqs.append(head_back(dot(k, gs), q_hat, q_inv))
        gks.append(head_back(dot(q, gs, 1, 1), k_hat, k_inv))
    gp_buf[0] = jnp.concatenate(gqs, axis=0).astype(BF)
    gp_buf[1] = jnp.concatenate(gks, axis=0).astype(BF)
    qk_copy = remote(gp_buf.at[pl.ds(0, 2)], gp_mate.at[pl.ds(0, 2)], mate)

    def vo_of(n_own, n_mate, go_own, go_mate):
        first = dot(n_own, gp_buf[2], 1, 1) + dot(n_mate, gp_mate[2], 1, 1)
        second = dot(go_own, gp_buf[3], 1, 1) + dot(go_mate, gp_mate[3], 1, 1)
        return jnp.concatenate([first, second], axis=1)

    def qk_of(n_own, n_mate):
        ours = gp_buf[0:2].reshape(2 * QW, SEQ)
        theirs = gp_mate[0:2].reshape(2 * QW, SEQ)
        return dot(n_own, ours, 1, 1) + dot(n_mate, theirs, 1, 1)

    def grad_vo(u):
        return vo_of(own_sel[0, u], mate_sel[0, u], own_sel[1, u], mate_sel[1, u])

    def grad_qk(u):
        return qk_of(own_sel[0, u], mate_sel[0, u])

    cut_x = pl.ds(0, KEPT // 2), pl.ds(KEPT // 2, KEPT // 2)
    order = [x_far, x_right, x_left, xi]
    rest_copy = pick_rest(0)
    for copy in n_copies + go_copies + [v_copy]:
        copy.wait_recv()
    v_send, v_rin, v_fin = xs_send.at[0], xs_rin.at[0], xs_fin.at[0]
    q_send, q_rin, q_fin = xs_send.at[1], xs_rin.at[1], xs_fin.at[1]
    v_far = scatter_far(v_send, v_rin, grad_vo, x_far, px_right, px_left, cut_x)
    v_plain = scatter_plain(
        v_send, v_fin, grad_vo, x_right, x_left, px_right, px_left, cut_x
    )

    gp = gp_buf[0:3].reshape(3 * QW, SEQ)
    gp_wide = gp.astype(F32)
    s1 = jnp.sum(gp_wide * w_sums, axis=0, keepdims=True) * (1.0 / MODEL)
    s2 = jnp.sum(gp_wide * proj, axis=0, keepdims=True) * (1.0 / MODEL)

    def back(u):
        part = dot(w_t[pl.ds(pl.multiple_of(u * COLS, COLS), COLS), :], gp)
        return rstd * (part - s1 - ((rows_of(u) - mean) * rstd) * s2)

    g_send, g_rin, g_fin = rs_send.at[1], rs_rin.at[1], rs_fin.at[1]
    g_far = scatter_far(g_send, g_rin, back, t_far, y_right, y_left, cut_y)
    qk_copy.wait_recv()
    rest_copy.wait_recv()
    rest_q = qk_of(own_rest[0], mate_rest[0])
    rest_v = vo_of(own_rest[0], mate_rest[0], own_rest[1], mate_rest[1])
    for k in range(NZ):
        at = slice(k * REST, (k + 1) * REST)
        rz_send[k] = jnp.concatenate([rest_q[at], rest_v[at]], axis=0).astype(BF)
    rz_copies = [remote(rz_send.at[pz], rz_recv.at[zi], dev) for pz, dev in z_peers]
    g_plain = scatter_plain(g_send, g_fin, back, t_right, t_left, y_right, y_left, cut_y)

    q_far = scatter_far(q_send, q_rin, grad_qk, x_far, px_right, px_left, cut_x)
    q_plain = scatter_plain(
        q_send, q_fin, grad_qk, x_right, x_left, px_right, px_left, cut_x
    )
    g_rest = scatter_relay(g_send, g_rin, g_fin, g_far, g_plain, y_right, y_left, cut_y)
    v_rest = scatter_relay(v_send, v_rin, v_fin, v_far, v_plain, px_right, px_left, cut_x)
    q_rest = scatter_relay(q_send, q_rin, q_fin, q_far, q_plain, px_right, px_left, cut_x)
    b_plain = scatter_plain(b_send, b_fin, branch, t_right, t_left, y_right, y_left, cut_y)
    b_rest = scatter_relay(b_send, b_rin, b_fin, b_far, b_plain, y_right, y_left, cut_y)

    mixed_own = x_full[t].astype(F32) + branch(t)
    gx_own = go_full[t].astype(F32) + back(t)
    v_own = grad_vo(xi)
    q_own = grad_qk(xi)

    for copy in g_rest:
        copy.wait_recv()
    gx = (gx_own + g_fin[0].astype(F32) + g_fin[1].astype(F32)).astype(BF)
    r, c = grid2(SPILL, SEQ)
    bsnd_next[...] = dot(hot(c == r + SEQ - tail), gx, 1, 1).astype(BF)
    bsnd_prev[...] = dot(hot(c == r), gx, 1, 1).astype(BF)
    back_next = remote(bsnd_next, bfrom_prev, dp_next)
    back_prev = remote(bsnd_prev, bfrom_next, dp_prev)

    def along_z(rest, mine, fin, slot):
        for copy in rest:
            copy.wait_recv()
        summed = mine + fin[0].astype(F32) + fin[1].astype(F32)
        z_send[slot] = summed.astype(BF).reshape(NZ, XROWS, COLS)
        return [remote(z_send.at[slot, pz], z_recv.at[slot, zi], dev) for pz, dev in z_peers]

    earlier = list(pending)
    pending.clear()
    vz_copies = along_z(v_rest, v_own, v_fin, 1)
    qz_copies = along_z(q_rest, q_own, q_fin, 0)

    rest = rz_send[zi].astype(F32)
    for copy in rz_copies:
        copy.wait_recv()
    for pz, _ in z_peers:
        rest = rest + rz_recv[pz].astype(F32)
    r, c = grid2(NX * XROWS, 2 * REST)
    mask = c < 0
    for k in range(NX):
        at = r - k * XROWS
        mask = mask | ((at >= 0) & (at < ZROWS) & (c == at + k * ZROWS))
        at = at - 8
        mask = mask | ((at >= 0) & (at < ZROWS) & (c == at + k * ZROWS + REST))
    rest = dot(hot(mask), rest.astype(BF)).astype(BF)
    rx_send[...] = rest.reshape(NX, XROWS, COLS)
    rx_copies = [
        remote(rx_send.at[px], rx_recv.at[xi], (px * 16 + inner, t))
        for px in (x_far, x_right, x_left)
    ]

    length = SEQ + upper - lower
    behind = jnp.maximum(-lower, 0)
    ahead = jnp.maximum(upper, 0)
    r, c = grid2(SEQ, SRC)
    mine = hot((r == c + lower) & (c >= behind) & (c < length - ahead))
    src_rows = dot(gx, mine)
    r, c = grid2(SPILL, SRC)
    pick_prev = hot((c == r) & (c < behind))
    pick_next = hot((r == c - (length - ahead)) & (c >= length - ahead) & (c < length))
    back_next.wait_recv()
    back_prev.wait_recv()
    src_rows = (
        src_rows + dot(bfrom_prev[...], pick_prev, 0, 0) + dot(bfrom_next[...], pick_next, 0, 0)
    )
    gpatch_ref[...] = src_rows.astype(BF)
    gpatch_copy = pltpu.make_async_copy(gpatch_ref, gpatch_out, lsem.at[6])
    gpatch_copy.start()

    for copy in earlier:
        copy.wait_send()
    for copy in b_rest:
        copy.wait_recv()
    mixed_ref[...] = (mixed_own + b_fin[0].astype(F32) + b_fin[1].astype(F32)).astype(BF)
    mixed_copy = pltpu.make_async_copy(mixed_ref, mixed_out, lsem.at[7])
    mixed_copy.start()

    last = rx_send[xi].astype(F32)
    for copy in rx_copies:
        copy.wait_recv()
    for px in (x_far, x_right, x_left):
        last = last + rx_recv[px].astype(F32)
    last = last * total_scale

    def finish(copies, slot):
        total = z_send[slot, zi].astype(F32)
        for copy in copies:
            copy.wait_recv()
        for pz, _ in z_peers:
            total = total + z_recv[slot, pz].astype(F32)
        return total * total_scale

    vo = finish(vz_copies, 1)
    qk = finish(qz_copies, 0)
    gqkv_ref[0, 0:XROWS] = qk[:, 0:QW]
    gqkv_ref[0, XROWS:SHARE] = last[0:ZROWS, 0:QW]
    gqkv_ref[1, 0:XROWS] = qk[:, QW : 2 * QW]
    gqkv_ref[1, XROWS:SHARE] = last[0:ZROWS, QW : 2 * QW]
    gqkv_ref[2, 0:XROWS] = vo[:, 0:QW]
    gqkv_ref[2, XROWS:SHARE] = last[8 : 8 + ZROWS, 0:QW]
    gwout_ref[0:XROWS] = vo[:, QW : 2 * QW]
    gwout_ref[XROWS:SHARE] = last[8 : 8 + ZROWS, QW : 2 * QW]

    for copy in pending:
        copy.wait_send()
    gpatch_copy.wait()
    mixed_copy.wait()


def hand_out(a, b, c, e, a_out, b_out, c_out, e_out):
    a_out[...] = a[...]
    b_out[...] = b[...]
    c_out[...] = c[...]
    e_out[...] = e[...]


COPIES = 88


def body(patches, seg_ids, cut, w_qkv, w_out, grad_out):
    vmem = pl.BlockSpec(memory_space=pltpu.VMEM)
    anym = pl.BlockSpec(memory_space=pl.ANY)
    halo = pltpu.VMEM((SPILL, COLS), BF)
    scratch = [
        pltpu.SMEM((1, 2), jnp.int32),
        pltpu.VMEM((1, SEQ), jnp.int32),
        pltpu.VMEM((COLS, SEQ), BF),
        pltpu.VMEM((COLS, SRC), BF),
        pltpu.VMEM((COLS, SRC), BF),
        pltpu.VMEM((3 * QW, MODEL), BF),
        pltpu.VMEM((QW, MODEL), BF),
        pltpu.VMEM((2, NT, COLS, SEQ), BF),
        pltpu.VMEM((NT, COLS, SEQ), BF),
        pltpu.VMEM((MODEL, 3 * QW), BF),
        pltpu.VMEM((MODEL, QW), BF),
        halo, halo, halo, halo, halo, halo, halo, halo,
        pltpu.VMEM((2, 3, COLS, SEQ), BF),
        pltpu.VMEM((2, COLS, SEQ), BF),
        pltpu.VMEM((2, 2, COLS, SEQ), BF),
        pltpu.VMEM((4, QW, SEQ), BF),
        pltpu.VMEM((4, QW, SEQ), BF),
        pltpu.VMEM((2, NX, KEPT, SEQ), BF),
        pltpu.VMEM((2, NX, KEPT, SEQ), BF),
        pltpu.VMEM((2, NX, KEPT, SEQ), BF),
        pltpu.VMEM((2 * NZ * REST, MODEL), BF),
        pltpu.VMEM((2, NZ * REST, SEQ), BF),
        pltpu.VMEM((2, NZ * REST, SEQ), BF),
        pltpu.VMEM((2, NZ * REST, SEQ), BF),
        pltpu.VMEM((2, 3, KEPT, COLS), BF),
        pltpu.VMEM((2, KEPT, COLS), BF),
        pltpu.VMEM((2, 2, KEPT, COLS), BF),
        pltpu.VMEM((2, NZ, XROWS, COLS), BF),
        pltpu.VMEM((2, NZ, XROWS, COLS), BF),
        pltpu.VMEM((NZ, 2 * REST, COLS), BF),
        pltpu.VMEM((NZ, 2 * REST, COLS), BF),
        pltpu.VMEM((NX, XROWS, COLS), BF),
        pltpu.VMEM((NX, XROWS, COLS), BF),
        pltpu.SemaphoreType.DMA((COPIES,)),
        pltpu.SemaphoreType.DMA((COPIES,)),
        pltpu.SemaphoreType.DMA((8,)),
    ]
    out_shape = (
        jax.ShapeDtypeStruct((COLS, SEQ), BF),
        jax.ShapeDtypeStruct((COLS, SRC), BF),
        jax.ShapeDtypeStruct((3, SHARE, QW), F32),
        jax.ShapeDtypeStruct((SHARE, QW), F32),
    )
    results = pl.pallas_call(
        kernel,
        out_shape=out_shape,
        in_specs=[anym, anym, anym, anym, anym, anym],
        out_specs=(anym, anym, vmem, vmem),
        scratch_shapes=scratch,
        compiler_params=pltpu.CompilerParams(
            collective_id=0, has_side_effects=True, vmem_limit_bytes=56 * 1024 * 1024
        ),
    )(cut, seg_ids.reshape(1, SEQ), patches.T, w_qkv.reshape(3 * QW, MODEL), w_out, grad_out.T)
    mixed, grad_patches, qkv_grad, out_grad = pl.pallas_call(
        hand_out,
        out_shape=out_shape,
        in_specs=[vmem, vmem, vmem, vmem],
        out_specs=(vmem, vmem, vmem, vmem),
    )(*results)
    return mixed.T, grad_patches.T, jnp.swapaxes(qkv_grad, 1, 2), out_grad.T


def solution(mesh):
    in_specs = (
        P("dp", "tensor"),
        P("dp"),
        P("dp", None),
        P(None, "tensor", None),
        P("tensor", None),
        P("dp", "tensor"),
    )
    out_specs = (P("dp", "tensor"), P("dp", "tensor"), P(None, "tensor", "dp"), P("tensor", "dp"))
    return jax.shard_map(body, mesh=mesh, in_specs=in_specs, out_specs=out_specs, check_vma=False)
```

```python
import math

import jax
import jax.numpy as jnp
from jax import lax
from jax.experimental import pallas as pl
from jax.experimental.pallas import tpu as pltpu
from jax.sharding import PartitionSpec as P

HD = 88
SEQ = 256
SRC = 384
SPILL = 64
COLS = 352
MODEL = 1408
QW = 176
NT = 4
NX = 4
NZ = 8
SHARE = 22
XROWS = 16
ZROWS = SHARE - XROWS
KEPT = NZ * XROWS
REST = NX * ZROWS
norm_eps = 1e-06
score_scale = HD ** (-0.5)
total_scale = 1.0 / math.sqrt(16384.0)

BF = jnp.bfloat16
F32 = jnp.float32
MESH = pl.DeviceIdType.MESH


def dot(a, b, ca=1, cb=0):
    return lax.dot_general(a, b, (((ca,), (cb,)), ((), ())), preferred_element_type=F32)


def grid2(rows, cols):
    r = lax.broadcasted_iota(jnp.int32, (rows, cols), 0)
    c = lax.broadcasted_iota(jnp.int32, (rows, cols), 1)
    return r, c


def hot(mask):
    return jnp.where(mask, 1.0, 0.0).astype(BF)


def kernel(
    cut_in, seg_in, patches_in, wqkv_in, wout_in, gout_in,
    mixed_out, gpatch_out, gqkv_ref, gwout_ref,
    cut_ref, seg_ref, mixed_ref, gpatch_ref, patches_ref, wqkv_ref, wout_ref, acts, x_full, w_t, wo_t,
    snd_next, snd_prev, from_prev, from_next, bsnd_next, bsnd_prev, bfrom_prev, bfrom_next,
    rs_send, rs_rin, rs_fin, gp_buf, gp_mate, own_sel, out_sel, mate_sel,
    z_pick, own_rest, out_rest, mate_rest,
    xs_send, xs_rin, xs_fin, z_send, z_recv, rz_send, rz_recv, rx_send, rx_recv,
    ssem, rsem, lsem,
):
    d = lax.axis_index("dp")
    t = lax.axis_index("tensor")
    xi = d // 16
    zi = lax.rem(d // 2, NZ)
    core = lax.rem(d, 2)
    inner = lax.rem(d, 16)
    t_right, t_left, t_far = lax.rem(t + 1, NT), lax.rem(t + 3, NT), lax.rem(t + 2, NT)
    x_right, x_left, x_far = lax.rem(xi + 1, NX), lax.rem(xi + 3, NX), lax.rem(xi + 2, NX)
    dp_next = (lax.rem(d + 1, 64), t)
    dp_prev = (lax.rem(d + 63, 64), t)
    mate = (d + 1 - 2 * core, t)
    y_right, y_left = (d, t_right), (d, t_left)
    px_right, px_left = (x_right * 16 + inner, t), (x_left * 16 + inner, t)
    z_peers = [
        (lax.rem(zi + k, NZ), (xi * 16 + lax.rem(zi + k, NZ) * 2 + core, t)) for k in (4, 1, 3, 7, 5, 2, 6)
    ]
    n_low, go_full = acts.at[0], acts.at[1]

    barrier = pltpu.get_barrier_semaphore()
    px_far = (x_far * 16 + inner, t)
    greet = [dp_next, dp_prev, y_right, y_left, px_right, px_left, px_far]
    greet = greet + [p for _, p in z_peers]
    for peer in greet:
        pl.semaphore_signal(barrier, inc=1, device_id=peer, device_id_type=MESH)

    loads = [
        pltpu.make_async_copy(src, dst, lsem.at[k])
        for k, (src, dst) in enumerate(
            [
                (patches_in, patches_ref),
                (gout_in, go_full.at[t]),
                (wqkv_in, wqkv_ref),
                (wout_in, wout_ref),
                (cut_in, cut_ref),
                (seg_in, seg_ref),
            ]
        )
    ]
    for load in loads:
        load.start()

    counter = [0]
    pending = []

    def remote(src, dst, dev):
        k = counter[0]
        counter[0] += 1
        copy = pltpu.make_async_remote_copy(
            src_ref=src, dst_ref=dst, send_sem=ssem.at[k], recv_sem=rsem.at[k],
            device_id=dev, device_id_type=MESH,
        )
        copy.start()
        pending.append(copy)
        return copy

    loads[4].wait()
    lower = cut_ref[0, 0]
    upper = cut_ref[0, 1]
    head = jnp.maximum(lower, 0)
    tail = jnp.maximum(-upper, 0)

    loads[0].wait()
    r, c = grid2(SPILL, SRC)
    base = SEQ - lower + jnp.minimum(upper, 0)
    snd_next[...] = dot(hot(c == r + base), patches_ref[...], 1, 1).astype(BF)
    snd_prev[...] = dot(hot(c == r), patches_ref[...], 1, 1).astype(BF)

    pl.semaphore_wait(barrier, len(greet))

    to_next = remote(snd_next, from_prev, dp_next)
    to_prev = remote(snd_prev, from_next, dp_prev)

    half = COLS // 2
    lo, hi = pl.ds(0, half), pl.ds(half, half)

    halves = [(lo, hi)]
    pieces = [
        (pl.ds(0, 96), pl.ds(half, 96)),
        (pl.ds(96, 80), pl.ds(half + 96, 80)),
    ]

    def gather_handed(full, cuts):
        handed = []
        for low, high in cuts:
            handed.append(remote(full.at[t, low], full.at[t, low], y_right))
            handed.append(remote(full.at[t, high], full.at[t, high], y_left))
        return handed

    def gather_other(full):
        rb = remote(full.at[t, hi], full.at[t, hi], y_right)
        la = remote(full.at[t, lo], full.at[t, lo], y_left)
        return [rb, la]

    def gather_relay(full, handed, cuts):
        rest = []
        for k, (low, high) in enumerate(cuts):
            handed[2 * k].wait_recv()
            rest.append(remote(full.at[t_left, low], full.at[t_left, low], y_right))
            handed[2 * k + 1].wait_recv()
            rest.append(remote(full.at[t_right, high], full.at[t_right, high], y_left))
        return rest

    def gather_finish(rest):
        for copy in rest:
            copy.wait_recv()

    loads[1].wait()
    go_handed = gather_handed(go_full, halves)
    go_other = gather_other(go_full)

    r, c = grid2(SRC, SEQ)
    mine = (r == c - lower) & (c >= head) & (c < SEQ - tail)
    own = dot(patches_ref[...], hot(mine))
    r, c = grid2(SPILL, SEQ)
    pick_prev = hot((c == r) & (c < head))
    pick_next = hot((r == c - (SEQ - tail)) & (c >= SEQ - tail))
    loads[2].wait()
    loads[3].wait()
    w_t[...] = jnp.transpose(wqkv_ref[...])
    w_sums = jnp.sum(wqkv_ref[...].astype(F32), axis=-1, keepdims=True)
    wo_t[...] = jnp.transpose(wout_ref[...])

    to_next.wait_recv()
    to_prev.wait_recv()
    own = own + dot(from_prev[...], pick_prev, 0, 0) + dot(from_next[...], pick_next, 0, 0)
    x_full[t] = own.astype(BF)
    x_handed = gather_handed(x_full, pieces)
    x_other = gather_other(x_full)
    go_rest = gather_relay(go_full, go_handed, halves)

    r = lax.broadcasted_iota(jnp.int32, (KEPT, 1), 0)
    zk = sum((r >= k * XROWS).astype(jnp.int32) for k in range(1, NZ))
    at_x = r - zk * XROWS + 2 * SHARE * zk
    _, c = grid2(KEPT, COLS)
    x_pick = jnp.concatenate([hot(c == at_x + SHARE * side) for side in (core, 1 - core)], axis=0)
    r = lax.broadcasted_iota(jnp.int32, (NZ * REST, 1), 0)
    zk = sum((r >= k * REST).astype(jnp.int32) for k in range(1, NZ))
    r = r - zk * REST
    xk = sum((r >= k * ZROWS).astype(jnp.int32) for k in range(1, NX))
    at_z = r - xk * ZROWS + COLS * xk + 2 * SHARE * zk + XROWS
    _, c = grid2(NZ * REST, MODEL)
    z_pick[0 : NZ * REST] = hot(c == at_z + SHARE * core)
    z_pick[NZ * REST :] = hot(c == at_z + SHARE * (1 - core))

    def pick_rest(kind):
        everything = acts[kind].reshape(MODEL, SEQ)
        both = dot(z_pick[...], everything).astype(BF)
        out_rest[kind] = both[NZ * REST :]
        own_rest[kind] = both[0 : NZ * REST]
        return remote(out_rest.at[kind], mate_rest.at[kind], mate)

    def pick(kind, u, send=True):
        both = dot(x_pick, acts[kind, u]).astype(BF)
        out_sel[kind, u] = both[KEPT:]
        own_sel[kind, u] = both[0:KEPT]
        return remote(out_sel.at[kind, u], mate_sel.at[kind, u], mate) if send else None

    def rows_of(u):
        return x_full[u].astype(F32)

    def chunk_stats(u):
        rows = rows_of(u)
        centre = jnp.sum(rows, axis=0, keepdims=True) * (1.0 / COLS)
        rows = rows - centre
        return centre, jnp.sum(rows * rows, axis=0, keepdims=True)

    x_rest = gather_relay(x_full, x_handed, pieces)
    gather_finish(go_other)
    for u in (t, t_left, t_right):
        pick(1, u, False)
    gather_finish(x_other)
    stats = [chunk_stats(u) for u in (t, t_left, t_right)]
    gather_finish(go_rest)
    pick(1, t_far, False)
    go_copies = [remote(out_sel.at[1], mate_sel.at[1], mate), pick_rest(1)]
    grad_att = dot(wout_ref[...], go_full[...].reshape(MODEL, SEQ))
    gas = [grad_att[h * HD : (h + 1) * HD].astype(BF) for h in range(2)]
    gather_finish(x_rest)
    stats.append(chunk_stats(t_far))

    mean = (stats[0][0] + stats[1][0] + stats[2][0] + stats[3][0]) * (1.0 / NT)
    spread = jnp.zeros((1, SEQ), F32)
    for centre, squares in stats:
        spread = spread + squares + COLS * (centre - mean) * (centre - mean)
    rstd = lax.rsqrt(spread * (1.0 / MODEL) + norm_eps)
    for u in range(NT):
        n_low[u] = ((rows_of(u) - mean) * rstd).astype(BF)
    proj = dot(wqkv_ref[...], n_low[...].reshape(MODEL, SEQ))
    for u in range(NT):
        pick(0, u, False)
    n_copies = [remote(out_sel.at[0], mate_sel.at[0], mate)]

    def head_norm(v):
        center = v - jnp.sum(v, axis=0, keepdims=True) * (1.0 / HD)
        var = jnp.sum(center * center, axis=0, keepdims=True) * (1.0 / HD)
        inverse = lax.rsqrt(var + norm_eps)
        return center * inverse, inverse

    def head_back(g, normed, inverse):
        first = jnp.sum(g, axis=0, keepdims=True) * (1.0 / HD)
        second = jnp.sum(g * normed, axis=0, keepdims=True) * (1.0 / HD)
        return inverse * (g - first - normed * second)

    loads[5].wait()
    seg_row = seg_ref[...].astype(F32)
    r, c = grid2(SEQ, SEQ)
    seg_col = jnp.sum(jnp.where(r == c, seg_row, 0.0), axis=-1, keepdims=True)
    same = seg_col == seg_row

    saved = []
    att_parts = []
    for h in range(2):
        q_hat, q_inv = head_norm(proj[h * HD : (h + 1) * HD])
        k_hat, k_inv = head_norm(proj[(2 + h) * HD : (3 + h) * HD])
        v = proj[(4 + h) * HD : (5 + h) * HD].astype(BF)
        q, k = q_hat.astype(BF), k_hat.astype(BF)
        raised = jnp.where(same, jnp.exp(dot(k, q, 0, 0) * score_scale), 0.0)
        weights = raised / jnp.sum(raised, axis=0, keepdims=True)
        weights_low = weights.astype(BF)
        att_parts.append(dot(v, weights_low))
        saved.append((q_hat, q_inv, k_hat, k_inv, q, k, v, weights, weights_low))
    att = jnp.concatenate(att_parts, axis=0).astype(BF)
    gp_buf[3] = att

    def scatter_far(send, rin, make, far, to_right, to_left, cut_at):
        a, b = cut_at
        send[0] = make(far).astype(BF)
        ra = remote(send.at[0, a], rin.at[a], to_right)
        lb = remote(send.at[0, b], rin.at[b], to_left)
        return ra, lb

    def scatter_plain(send, fin, make, right, left, to_right, to_left, cut_at):
        a, b = cut_at
        send[1] = make(right).astype(BF)
        rb = remote(send.at[1, b], fin.at[0, b], to_right)
        send[2] = make(left).astype(BF)
        la = remote(send.at[2, a], fin.at[1, a], to_left)
        return rb, la

    def scatter_relay(send, rin, fin, first, plain, to_right, to_left, cut_at):
        a, b = cut_at
        ra, lb = first
        rb, la = plain
        ra.wait_recv()
        send[1, a] = (send[1, a].astype(F32) + rin[a].astype(F32)).astype(BF)
        fa = remote(send.at[1, a], fin.at[0, a], to_right)
        lb.wait_recv()
        send[2, b] = (send[2, b].astype(F32) + rin[b].astype(F32)).astype(BF)
        fb = remote(send.at[2, b], fin.at[1, b], to_left)
        return rb, la, fa, fb

    cut_y = lo, hi

    def branch(u):
        return dot(wo_t[pl.ds(pl.multiple_of(u * COLS, COLS), COLS), :], att)

    b_send, b_rin, b_fin = rs_send.at[0], rs_rin.at[0], rs_fin.at[0]

    b_far = scatter_far(b_send, b_rin, branch, t_far, y_right, y_left, cut_y)
    gvs = [dot(gas[h], saved[h][8], 1, 1) for h in range(2)]
    gp_buf[2] = jnp.concatenate(gvs, axis=0).astype(BF)
    v_copy = remote(gp_buf.at[pl.ds(2, 2)], gp_mate.at[pl.ds(2, 2)], mate)
    gqs, gks = [], []
    for h in range(2):
        q_hat, q_inv, k_hat, k_inv, q, k, v, weights, weights_low = saved[h]
        gw = dot(v, gas[h], 0, 0)
        inner_sum = jnp.sum(gw * weights, axis=0, keepdims=True)
        gs = (weights * (gw - inner_sum) * score_scale).astype(BF)
        gqs.append(head_back(dot(k, gs), q_hat, q_inv))
        gks.append(head_back(dot(q, gs, 1, 1), k_hat, k_inv))
    gp_buf[0] = jnp.concatenate(gqs, axis=0).astype(BF)
    gp_buf[1] = jnp.concatenate(gks, axis=0).astype(BF)
    qk_copy = remote(gp_buf.at[pl.ds(0, 2)], gp_mate.at[pl.ds(0, 2)], mate)

    def vo_of(n_own, n_mate, go_own, go_mate):
        first = dot(n_own, gp_buf[2], 1, 1) + dot(n_mate, gp_mate[2], 1, 1)
        second = dot(go_own, gp_buf[3], 1, 1) + dot(go_mate, gp_mate[3], 1, 1)
        return jnp.concatenate([first, second], axis=1)

    def qk_of(n_own, n_mate):
        ours = gp_buf[0:2].reshape(2 * QW, SEQ)
        theirs = gp_mate[0:2].reshape(2 * QW, SEQ)
        return dot(n_own, ours, 1, 1) + dot(n_mate, theirs, 1, 1)

    def grad_vo(u):
        return vo_of(own_sel[0, u], mate_sel[0, u], own_sel[1, u], mate_sel[1, u])

    def grad_qk(u):
        return qk_of(own_sel[0, u], mate_sel[0, u])

    cut_x = pl.ds(0, KEPT // 2), pl.ds(KEPT // 2, KEPT // 2)
    order = [x_far, x_right, x_left, xi]
    rest_copy = pick_rest(0)
    for copy in n_copies + go_copies + [v_copy]:
        copy.wait_recv()
    v_send, v_rin, v_fin = xs_send.at[0], xs_rin.at[0], xs_fin.at[0]
    q_send, q_rin, q_fin = xs_send.at[1], xs_rin.at[1], xs_fin.at[1]
    v_far = scatter_far(v_send, v_rin, grad_vo, x_far, px_right, px_left, cut_x)
    v_plain = scatter_plain(
        v_send, v_fin, grad_vo, x_right, x_left, px_right, px_left, cut_x
    )

    gp = gp_buf[0:3].reshape(3 * QW, SEQ)
    gp_wide = gp.astype(F32)
    s1 = jnp.sum(gp_wide * w_sums, axis=0, keepdims=True) * (1.0 / MODEL)
    s2 = jnp.sum(gp_wide * proj, axis=0, keepdims=True) * (1.0 / MODEL)

    def back(u):
        part = dot(w_t[pl.ds(pl.multiple_of(u * COLS, COLS), COLS), :], gp)
        return rstd * (part - s1 - ((rows_of(u) - mean) * rstd) * s2)

    g_send, g_rin, g_fin = rs_send.at[1], rs_rin.at[1], rs_fin.at[1]
    g_far = scatter_far(g_send, g_rin, back, t_far, y_right, y_left, cut_y)
    qk_copy.wait_recv()
    rest_copy.wait_recv()
    rest_q = qk_of(own_rest[0], mate_rest[0])
    rest_v = vo_of(own_rest[0], mate_rest[0], own_rest[1], mate_rest[1])
    for k in range(NZ):
        at = slice(k * REST, (k + 1) * REST)
        rz_send[k] = jnp.concatenate([rest_q[at], rest_v[at]], axis=0).astype(BF)
    rz_copies = [remote(rz_send.at[pz], rz_recv.at[zi], dev) for pz, dev in z_peers]
    g_plain = scatter_plain(g_send, g_fin, back, t_right, t_left, y_right, y_left, cut_y)

    q_far = scatter_far(q_send, q_rin, grad_qk, x_far, px_right, px_left, cut_x)
    q_plain = scatter_plain(
        q_send, q_fin, grad_qk, x_right, x_left, px_right, px_left, cut_x
    )
    g_rest = scatter_relay(g_send, g_rin, g_fin, g_far, g_plain, y_right, y_left, cut_y)
    v_rest = scatter_relay(v_send, v_rin, v_fin, v_far, v_plain, px_right, px_left, cut_x)
    q_rest = scatter_relay(q_send, q_rin, q_fin, q_far, q_plain, px_right, px_left, cut_x)
    b_plain = scatter_plain(b_send, b_fin, branch, t_right, t_left, y_right, y_left, cut_y)
    b_rest = scatter_relay(b_send, b_rin, b_fin, b_far, b_plain, y_right, y_left, cut_y)

    mixed_own = x_full[t].astype(F32) + branch(t)
    gx_own = go_full[t].astype(F32) + back(t)
    v_own = grad_vo(xi)
    q_own = grad_qk(xi)

    for copy in g_rest:
        copy.wait_recv()
    gx = (gx_own + g_fin[0].astype(F32) + g_fin[1].astype(F32)).astype(BF)
    r, c = grid2(SPILL, SEQ)
    bsnd_next[...] = dot(hot(c == r + SEQ - tail), gx, 1, 1).astype(BF)
    bsnd_prev[...] = dot(hot(c == r), gx, 1, 1).astype(BF)
    back_next = remote(bsnd_next, bfrom_prev, dp_next)
    back_prev = remote(bsnd_prev, bfrom_next, dp_prev)

    def along_z(rest, mine, fin, slot):
        for copy in rest:
            copy.wait_recv()
        summed = mine + fin[0].astype(F32) + fin[1].astype(F32)
        z_send[slot] = summed.astype(BF).reshape(NZ, XROWS, COLS)
        return [remote(z_send.at[slot, pz], z_recv.at[slot, zi], dev) for pz, dev in z_peers]

    earlier = list(pending)
    pending.clear()
    vz_copies = along_z(v_rest, v_own, v_fin, 1)
    qz_copies = along_z(q_rest, q_own, q_fin, 0)

    rest = rz_send[zi].astype(F32)
    for copy in rz_copies:
        copy.wait_recv()
    for pz, _ in z_peers:
        rest = rest + rz_recv[pz].astype(F32)
    r, c = grid2(NX * XROWS, 2 * REST)
    mask = c < 0
    for k in range(NX):
        at = r - k * XROWS
        mask = mask | ((at >= 0) & (at < ZROWS) & (c == at + k * ZROWS))
        at = at - 8
        mask = mask | ((at >= 0) & (at < ZROWS) & (c == at + k * ZROWS + REST))
    rest = dot(hot(mask), rest.astype(BF)).astype(BF)
    rx_send[...] = rest.reshape(NX, XROWS, COLS)
    rx_copies = [
        remote(rx_send.at[px], rx_recv.at[xi], (px * 16 + inner, t))
        for px in (x_far, x_right, x_left)
    ]

    length = SEQ + upper - lower
    behind = jnp.maximum(-lower, 0)
    ahead = jnp.maximum(upper, 0)
    r, c = grid2(SEQ, SRC)
    mine = hot((r == c + lower) & (c >= behind) & (c < length - ahead))
    src_rows = dot(gx, mine)
    r, c = grid2(SPILL, SRC)
    pick_prev = hot((c == r) & (c < behind))
    pick_next = hot((r == c - (length - ahead)) & (c >= length - ahead) & (c < length))
    back_next.wait_recv()
    back_prev.wait_recv()
    src_rows = (
        src_rows + dot(bfrom_prev[...], pick_prev, 0, 0) + dot(bfrom_next[...], pick_next, 0, 0)
    )
    gpatch_ref[...] = src_rows.astype(BF)
    gpatch_copy = pltpu.make_async_copy(gpatch_ref, gpatch_out, lsem.at[6])
    gpatch_copy.start()

    for copy in earlier:
        copy.wait_send()
    for copy in b_rest:
        copy.wait_recv()
    mixed_ref[...] = (mixed_own + b_fin[0].astype(F32) + b_fin[1].astype(F32)).astype(BF)
    mixed_copy = pltpu.make_async_copy(mixed_ref, mixed_out, lsem.at[7])
    mixed_copy.start()

    last = rx_send[xi].astype(F32)
    for copy in rx_copies:
        copy.wait_recv()
    for px in (x_far, x_right, x_left):
        last = last + rx_recv[px].astype(F32)
    last = last * total_scale

    def finish(copies, slot):
        total = z_send[slot, zi].astype(F32)
        for copy in copies:
            copy.wait_recv()
        for pz, _ in z_peers:
            total = total + z_recv[slot, pz].astype(F32)
        return total * total_scale

    vo = finish(vz_copies, 1)
    qk = finish(qz_copies, 0)
    gqkv_ref[0, 0:XROWS] = qk[:, 0:QW]
    gqkv_ref[0, XROWS:SHARE] = last[0:ZROWS, 0:QW]
    gqkv_ref[1, 0:XROWS] = qk[:, QW : 2 * QW]
    gqkv_ref[1, XROWS:SHARE] = last[0:ZROWS, QW : 2 * QW]
    gqkv_ref[2, 0:XROWS] = vo[:, 0:QW]
    gqkv_ref[2, XROWS:SHARE] = last[8 : 8 + ZROWS, 0:QW]
    gwout_ref[0:XROWS] = vo[:, QW : 2 * QW]
    gwout_ref[XROWS:SHARE] = last[8 : 8 + ZROWS, QW : 2 * QW]

    for copy in pending:
        copy.wait_send()
    gpatch_copy.wait()
    mixed_copy.wait()


def hand_out(a, b, c, e, a_out, b_out, c_out, e_out):
    a_out[...] = a[...]
    b_out[...] = b[...]
    c_out[...] = c[...]
    e_out[...] = e[...]


COPIES = 88


def body(patches, seg_ids, cut, w_qkv, w_out, grad_out):
    vmem = pl.BlockSpec(memory_space=pltpu.VMEM)
    anym = pl.BlockSpec(memory_space=pl.ANY)
    halo = pltpu.VMEM((SPILL, COLS), BF)
    scratch = [
        pltpu.SMEM((1, 2), jnp.int32),
        pltpu.VMEM((1, SEQ), jnp.int32),
        pltpu.VMEM((COLS, SEQ), BF),
        pltpu.VMEM((COLS, SRC), BF),
        pltpu.VMEM((COLS, SRC), BF),
        pltpu.VMEM((3 * QW, MODEL), BF),
        pltpu.VMEM((QW, MODEL), BF),
        pltpu.VMEM((2, NT, COLS, SEQ), BF),
        pltpu.VMEM((NT, COLS, SEQ), BF),
        pltpu.VMEM((MODEL, 3 * QW), BF),
        pltpu.VMEM((MODEL, QW), BF),
        halo, halo, halo, halo, halo, halo, halo, halo,
        pltpu.VMEM((2, 3, COLS, SEQ), BF),
        pltpu.VMEM((2, COLS, SEQ), BF),
        pltpu.VMEM((2, 2, COLS, SEQ), BF),
        pltpu.VMEM((4, QW, SEQ), BF),
        pltpu.VMEM((4, QW, SEQ), BF),
        pltpu.VMEM((2, NX, KEPT, SEQ), BF),
        pltpu.VMEM((2, NX, KEPT, SEQ), BF),
        pltpu.VMEM((2, NX, KEPT, SEQ), BF),
        pltpu.VMEM((2 * NZ * REST, MODEL), BF),
        pltpu.VMEM((2, NZ * REST, SEQ), BF),
        pltpu.VMEM((2, NZ * REST, SEQ), BF),
        pltpu.VMEM((2, NZ * REST, SEQ), BF),
        pltpu.VMEM((2, 3, KEPT, COLS), BF),
        pltpu.VMEM((2, KEPT, COLS), BF),
        pltpu.VMEM((2, 2, KEPT, COLS), BF),
        pltpu.VMEM((2, NZ, XROWS, COLS), BF),
        pltpu.VMEM((2, NZ, XROWS, COLS), BF),
        pltpu.VMEM((NZ, 2 * REST, COLS), BF),
        pltpu.VMEM((NZ, 2 * REST, COLS), BF),
        pltpu.VMEM((NX, XROWS, COLS), BF),
        pltpu.VMEM((NX, XROWS, COLS), BF),
        pltpu.SemaphoreType.DMA((COPIES,)),
        pltpu.SemaphoreType.DMA((COPIES,)),
        pltpu.SemaphoreType.DMA((8,)),
    ]
    out_shape = (
        jax.ShapeDtypeStruct((COLS, SEQ), BF),
        jax.ShapeDtypeStruct((COLS, SRC), BF),
        jax.ShapeDtypeStruct((3, SHARE, QW), F32),
        jax.ShapeDtypeStruct((SHARE, QW), F32),
    )
    results = pl.pallas_call(
        kernel,
        out_shape=out_shape,
        in_specs=[anym, anym, anym, anym, anym, anym],
        out_specs=(anym, anym, vmem, vmem),
        scratch_shapes=scratch,
        compiler_params=pltpu.CompilerParams(
            collective_id=0, has_side_effects=True, vmem_limit_bytes=56 * 1024 * 1024
        ),
    )(cut, seg_ids.reshape(1, SEQ), patches.T, w_qkv.reshape(3 * QW, MODEL), w_out, grad_out.T)
    mixed, grad_patches, qkv_grad, out_grad = pl.pallas_call(
        hand_out,
        out_shape=out_shape,
        in_specs=[vmem, vmem, vmem, vmem],
        out_specs=(vmem, vmem, vmem, vmem),
    )(*results)
    return mixed.T, grad_patches.T, jnp.swapaxes(qkv_grad, 1, 2), out_grad.T


def solution(mesh):
    in_specs = (
        P("dp", "tensor"),
        P("dp"),
        P("dp", None),
        P(None, "tensor", None),
        P("tensor", None),
        P("dp", "tensor"),
    )
    out_specs = (P("dp", "tensor"), P("dp", "tensor"), P(None, "tensor", "dp"), P("tensor", "dp"))
    return jax.shard_map(body, mesh=mesh, in_specs=in_specs, out_specs=out_specs, check_vma=False)
```

```python
import math

import jax
import jax.numpy as jnp
from jax import lax
from jax.experimental import pallas as pl
from jax.experimental.pallas import tpu as pltpu
from jax.sharding import PartitionSpec as P

HD = 88
SEQ = 256
SRC = 384
SPILL = 64
COLS = 352
MODEL = 1408
QW = 176
NT = 4
NX = 4
NZ = 8
SHARE = 22
XROWS = 16
ZROWS = SHARE - XROWS
KEPT = NZ * XROWS
REST = NX * ZROWS
norm_eps = 1e-06
score_scale = HD ** (-0.5)
total_scale = 1.0 / math.sqrt(16384.0)

BF = jnp.bfloat16
F32 = jnp.float32
MESH = pl.DeviceIdType.MESH


def dot(a, b, ca=1, cb=0):
    return lax.dot_general(a, b, (((ca,), (cb,)), ((), ())), preferred_element_type=F32)


def grid2(rows, cols):
    r = lax.broadcasted_iota(jnp.int32, (rows, cols), 0)
    c = lax.broadcasted_iota(jnp.int32, (rows, cols), 1)
    return r, c


def hot(mask):
    return jnp.where(mask, 1.0, 0.0).astype(BF)


def kernel(
    cut_in, seg_in, patches_in, wqkv_in, wout_in, gout_in,
    mixed_out, gpatch_out, gqkv_ref, gwout_ref,
    cut_ref, seg_ref, mixed_ref, gpatch_ref, patches_ref, wqkv_ref, wout_ref, acts, x_full, w_t, wo_t,
    snd_next, snd_prev, from_prev, from_next, bsnd_next, bsnd_prev, bfrom_prev, bfrom_next,
    rs_send, rs_rin, rs_fin, gp_buf, gp_mate, own_sel, out_sel, mate_sel,
    z_pick, own_rest, out_rest, mate_rest,
    xs_send, xs_rin, xs_fin, z_send, z_recv, rz_send, rz_recv, rx_send, rx_recv,
    ssem, rsem, lsem,
):
    d = lax.axis_index("dp")
    t = lax.axis_index("tensor")
    xi = d // 16
    zi = lax.rem(d // 2, NZ)
    core = lax.rem(d, 2)
    inner = lax.rem(d, 16)
    t_right, t_left, t_far = lax.rem(t + 1, NT), lax.rem(t + 3, NT), lax.rem(t + 2, NT)
    x_right, x_left, x_far = lax.rem(xi + 1, NX), lax.rem(xi + 3, NX), lax.rem(xi + 2, NX)
    dp_next = (lax.rem(d + 1, 64), t)
    dp_prev = (lax.rem(d + 63, 64), t)
    mate = (d + 1 - 2 * core, t)
    y_right, y_left = (d, t_right), (d, t_left)
    px_right, px_left = (x_right * 16 + inner, t), (x_left * 16 + inner, t)
    z_peers = [
        (lax.rem(zi + k, NZ), (xi * 16 + lax.rem(zi + k, NZ) * 2 + core, t)) for k in (4, 3, 5, 2, 6, 1, 7)
    ]
    n_low, go_full = acts.at[0], acts.at[1]

    barrier = pltpu.get_barrier_semaphore()
    px_far = (x_far * 16 + inner, t)
    greet = [dp_next, dp_prev, y_right, y_left, px_right, px_left, px_far]
    greet = greet + [p for _, p in z_peers]
    for peer in greet:
        pl.semaphore_signal(barrier, inc=1, device_id=peer, device_id_type=MESH)

    loads = [
        pltpu.make_async_copy(src, dst, lsem.at[k])
        for k, (src, dst) in enumerate(
            [
                (patches_in, patches_ref),
                (gout_in, go_full.at[t]),
                (wqkv_in, wqkv_ref),
                (wout_in, wout_ref),
                (cut_in, cut_ref),
                (seg_in, seg_ref),
            ]
        )
    ]
    for load in loads:
        load.start()

    counter = [0]
    pending = []

    def remote(src, dst, dev):
        k = counter[0]
        counter[0] += 1
        copy = pltpu.make_async_remote_copy(
            src_ref=src, dst_ref=dst, send_sem=ssem.at[k], recv_sem=rsem.at[k],
            device_id=dev, device_id_type=MESH,
        )
        copy.start()
        pending.append(copy)
        return copy

    loads[4].wait()
    lower = cut_ref[0, 0]
    upper = cut_ref[0, 1]
    head = jnp.maximum(lower, 0)
    tail = jnp.maximum(-upper, 0)

    loads[0].wait()
    r, c = grid2(SPILL, SRC)
    base = SEQ - lower + jnp.minimum(upper, 0)
    snd_next[...] = dot(hot(c == r + base), patches_ref[...], 1, 1).astype(BF)
    snd_prev[...] = dot(hot(c == r), patches_ref[...], 1, 1).astype(BF)

    pl.semaphore_wait(barrier, len(greet))

    to_next = remote(snd_next, from_prev, dp_next)
    to_prev = remote(snd_prev, from_next, dp_prev)

    half = COLS // 2
    lo, hi = pl.ds(0, half), pl.ds(half, half)

    lo_pieces, hi_pieces = (lo,), (hi,)

    def gather_handed(full):
        handed = []
        for low, high in zip(lo_pieces, hi_pieces):
            handed.append(remote(full.at[t, low], full.at[t, low], y_right))
            handed.append(remote(full.at[t, high], full.at[t, high], y_left))
        return handed

    def gather_other(full):
        rb = remote(full.at[t, hi], full.at[t, hi], y_right)
        la = remote(full.at[t, lo], full.at[t, lo], y_left)
        return [rb, la]

    def gather_relay(full, handed):
        rest = []
        for k, (low, high) in enumerate(zip(lo_pieces, hi_pieces)):
            handed[2 * k].wait_recv()
            rest.append(remote(full.at[t_left, low], full.at[t_left, low], y_right))
            handed[2 * k + 1].wait_recv()
            rest.append(remote(full.at[t_right, high], full.at[t_right, high], y_left))
        return rest

    def gather_finish(rest):
        for copy in rest:
            copy.wait_recv()

    loads[1].wait()
    go_handed = gather_handed(go_full)
    go_other = gather_other(go_full)

    r, c = grid2(SRC, SEQ)
    mine = (r == c - lower) & (c >= head) & (c < SEQ - tail)
    own = dot(patches_ref[...], hot(mine))
    r, c = grid2(SPILL, SEQ)
    pick_prev = hot((c == r) & (c < head))
    pick_next = hot((r == c - (SEQ - tail)) & (c >= SEQ - tail))
    loads[2].wait()
    loads[3].wait()
    w_t[...] = jnp.transpose(wqkv_ref[...])
    w_sums = jnp.sum(wqkv_ref[...].astype(F32), axis=-1, keepdims=True)
    wo_t[...] = jnp.transpose(wout_ref[...])

    to_next.wait_recv()
    to_prev.wait_recv()
    own = own + dot(from_prev[...], pick_prev, 0, 0) + dot(from_next[...], pick_next, 0, 0)
    x_full[t] = own.astype(BF)
    x_handed = gather_handed(x_full)
    x_other = gather_other(x_full)
    go_rest = gather_relay(go_full, go_handed)

    r = lax.broadcasted_iota(jnp.int32, (KEPT, 1), 0)
    zk = sum((r >= k * XROWS).astype(jnp.int32) for k in range(1, NZ))
    at_x = r - zk * XROWS + 2 * SHARE * zk
    _, c = grid2(KEPT, COLS)
    x_pick = jnp.concatenate([hot(c == at_x + SHARE * side) for side in (core, 1 - core)], axis=0)
    r = lax.broadcasted_iota(jnp.int32, (NZ * REST, 1), 0)
    zk = sum((r >= k * REST).astype(jnp.int32) for k in range(1, NZ))
    r = r - zk * REST
    xk = sum((r >= k * ZROWS).astype(jnp.int32) for k in range(1, NX))
    at_z = r - xk * ZROWS + COLS * xk + 2 * SHARE * zk + XROWS
    _, c = grid2(NZ * REST, MODEL)
    z_pick[0 : NZ * REST] = hot(c == at_z + SHARE * core)
    z_pick[NZ * REST :] = hot(c == at_z + SHARE * (1 - core))

    def pick_rest(kind):
        everything = acts[kind].reshape(MODEL, SEQ)
        both = dot(z_pick[...], everything).astype(BF)
        out_rest[kind] = both[NZ * REST :]
        own_rest[kind] = both[0 : NZ * REST]
        return remote(out_rest.at[kind], mate_rest.at[kind], mate)

    def pick(kind, u, send=True):
        both = dot(x_pick, acts[kind, u]).astype(BF)
        out_sel[kind, u] = both[KEPT:]
        own_sel[kind, u] = both[0:KEPT]
        return remote(out_sel.at[kind, u], mate_sel.at[kind, u], mate) if send else None

    def rows_of(u):
        return x_full[u].astype(F32)

    def chunk_stats(u):
        rows = rows_of(u)
        centre = jnp.sum(rows, axis=0, keepdims=True) * (1.0 / COLS)
        rows = rows - centre
        return centre, jnp.sum(rows * rows, axis=0, keepdims=True)

    x_rest = gather_relay(x_full, x_handed)
    gather_finish(go_other)
    for u in (t, t_left, t_right):
        pick(1, u, False)
    gather_finish(x_other)
    stats = [chunk_stats(u) for u in (t, t_left, t_right)]
    gather_finish(go_rest)
    pick(1, t_far, False)
    go_copies = [remote(out_sel.at[1], mate_sel.at[1], mate), pick_rest(1)]
    grad_att = dot(wout_ref[...], go_full[...].reshape(MODEL, SEQ))
    gas = [grad_att[h * HD : (h + 1) * HD].astype(BF) for h in range(2)]
    gather_finish(x_rest)
    stats.append(chunk_stats(t_far))

    mean = (stats[0][0] + stats[1][0] + stats[2][0] + stats[3][0]) * (1.0 / NT)
    spread = jnp.zeros((1, SEQ), F32)
    for centre, squares in stats:
        spread = spread + squares + COLS * (centre - mean) * (centre - mean)
    rstd = lax.rsqrt(spread * (1.0 / MODEL) + norm_eps)
    for u in range(NT):
        n_low[u] = ((rows_of(u) - mean) * rstd).astype(BF)
    proj = dot(wqkv_ref[...], n_low[...].reshape(MODEL, SEQ))
    for u in range(NT):
        pick(0, u, False)
    n_copies = [remote(out_sel.at[0], mate_sel.at[0], mate)]

    def head_norm(v):
        center = v - jnp.sum(v, axis=0, keepdims=True) * (1.0 / HD)
        var = jnp.sum(center * center, axis=0, keepdims=True) * (1.0 / HD)
        inverse = lax.rsqrt(var + norm_eps)
        return center * inverse, inverse

    def head_back(g, normed, inverse):
        first = jnp.sum(g, axis=0, keepdims=True) * (1.0 / HD)
        second = jnp.sum(g * normed, axis=0, keepdims=True) * (1.0 / HD)
        return inverse * (g - first - normed * second)

    loads[5].wait()
    seg_row = seg_ref[...].astype(F32)
    r, c = grid2(SEQ, SEQ)
    seg_col = jnp.sum(jnp.where(r == c, seg_row, 0.0), axis=-1, keepdims=True)
    same = seg_col == seg_row

    saved = []
    att_parts = []
    for h in range(2):
        q_hat, q_inv = head_norm(proj[h * HD : (h + 1) * HD])
        k_hat, k_inv = head_norm(proj[(2 + h) * HD : (3 + h) * HD])
        v = proj[(4 + h) * HD : (5 + h) * HD].astype(BF)
        q, k = q_hat.astype(BF), k_hat.astype(BF)
        raised = jnp.where(same, jnp.exp(dot(k, q, 0, 0) * score_scale), 0.0)
        weights = raised / jnp.sum(raised, axis=0, keepdims=True)
        weights_low = weights.astype(BF)
        att_parts.append(dot(v, weights_low))
        saved.append((q_hat, q_inv, k_hat, k_inv, q, k, v, weights, weights_low))
    att = jnp.concatenate(att_parts, axis=0).astype(BF)
    gp_buf[3] = att

    def scatter_far(send, rin, make, far, to_right, to_left, cut_at):
        a, b = cut_at
        send[0] = make(far).astype(BF)
        ra = remote(send.at[0, a], rin.at[a], to_right)
        lb = remote(send.at[0, b], rin.at[b], to_left)
        return ra, lb

    def scatter_plain(send, fin, make, right, left, to_right, to_left, cut_at):
        a, b = cut_at
        send[1] = make(right).astype(BF)
        rb = remote(send.at[1, b], fin.at[0, b], to_right)
        send[2] = make(left).astype(BF)
        la = remote(send.at[2, a], fin.at[1, a], to_left)
        return rb, la

    def scatter_relay(send, rin, fin, first, plain, to_right, to_left, cut_at):
        a, b = cut_at
        ra, lb = first
        rb, la = plain
        ra.wait_recv()
        send[1, a] = (send[1, a].astype(F32) + rin[a].astype(F32)).astype(BF)
        fa = remote(send.at[1, a], fin.at[0, a], to_right)
        lb.wait_recv()
        send[2, b] = (send[2, b].astype(F32) + rin[b].astype(F32)).astype(BF)
        fb = remote(send.at[2, b], fin.at[1, b], to_left)
        return rb, la, fa, fb

    cut_y = lo, hi

    def branch(u):
        return dot(wo_t[pl.ds(pl.multiple_of(u * COLS, COLS), COLS), :], att)

    b_send, b_rin, b_fin = rs_send.at[0], rs_rin.at[0], rs_fin.at[0]

    b_far = scatter_far(b_send, b_rin, branch, t_far, y_right, y_left, cut_y)
    gvs = [dot(gas[h], saved[h][8], 1, 1) for h in range(2)]
    gp_buf[2] = jnp.concatenate(gvs, axis=0).astype(BF)
    v_copy = remote(gp_buf.at[pl.ds(2, 2)], gp_mate.at[pl.ds(2, 2)], mate)
    gqs, gks = [], []
    for h in range(2):
        q_hat, q_inv, k_hat, k_inv, q, k, v, weights, weights_low = saved[h]
        gw = dot(v, gas[h], 0, 0)
        inner_sum = jnp.sum(gw * weights, axis=0, keepdims=True)
        gs = (weights * (gw - inner_sum) * score_scale).astype(BF)
        gqs.append(head_back(dot(k, gs), q_hat, q_inv))
        gks.append(head_back(dot(q, gs, 1, 1), k_hat, k_inv))
    gp_buf[0] = jnp.concatenate(gqs, axis=0).astype(BF)
    gp_buf[1] = jnp.concatenate(gks, axis=0).astype(BF)
    qk_copy = remote(gp_buf.at[pl.ds(0, 2)], gp_mate.at[pl.ds(0, 2)], mate)

    def vo_of(n_own, n_mate, go_own, go_mate):
        first = dot(n_own, gp_buf[2], 1, 1) + dot(n_mate, gp_mate[2], 1, 1)
        second = dot(go_own, gp_buf[3], 1, 1) + dot(go_mate, gp_mate[3], 1, 1)
        return jnp.concatenate([first, second], axis=1)

    def qk_of(n_own, n_mate):
        ours = gp_buf[0:2].reshape(2 * QW, SEQ)
        theirs = gp_mate[0:2].reshape(2 * QW, SEQ)
        return dot(n_own, ours, 1, 1) + dot(n_mate, theirs, 1, 1)

    def grad_vo(u):
        return vo_of(own_sel[0, u], mate_sel[0, u], own_sel[1, u], mate_sel[1, u])

    def grad_qk(u):
        return qk_of(own_sel[0, u], mate_sel[0, u])

    cut_x = pl.ds(0, KEPT // 2), pl.ds(KEPT // 2, KEPT // 2)
    order = [x_far, x_right, x_left, xi]
    rest_copy = pick_rest(0)
    for copy in n_copies + go_copies + [v_copy]:
        copy.wait_recv()
    v_send, v_rin, v_fin = xs_send.at[0], xs_rin.at[0], xs_fin.at[0]
    q_send, q_rin, q_fin = xs_send.at[1], xs_rin.at[1], xs_fin.at[1]
    v_far = scatter_far(v_send, v_rin, grad_vo, x_far, px_right, px_left, cut_x)
    v_plain = scatter_plain(
        v_send, v_fin, grad_vo, x_right, x_left, px_right, px_left, cut_x
    )

    gp = gp_buf[0:3].reshape(3 * QW, SEQ)
    gp_wide = gp.astype(F32)
    s1 = jnp.sum(gp_wide * w_sums, axis=0, keepdims=True) * (1.0 / MODEL)
    s2 = jnp.sum(gp_wide * proj, axis=0, keepdims=True) * (1.0 / MODEL)

    def back(u):
        part = dot(w_t[pl.ds(pl.multiple_of(u * COLS, COLS), COLS), :], gp)
        return rstd * (part - s1 - ((rows_of(u) - mean) * rstd) * s2)

    g_send, g_rin, g_fin = rs_send.at[1], rs_rin.at[1], rs_fin.at[1]
    g_far = scatter_far(g_send, g_rin, back, t_far, y_right, y_left, cut_y)
    qk_copy.wait_recv()
    rest_copy.wait_recv()
    rest_q = qk_of(own_rest[0], mate_rest[0])
    rest_v = vo_of(own_rest[0], mate_rest[0], own_rest[1], mate_rest[1])
    for k in range(NZ):
        at = slice(k * REST, (k + 1) * REST)
        rz_send[k] = jnp.concatenate([rest_q[at], rest_v[at]], axis=0).astype(BF)
    rz_copies = [remote(rz_send.at[pz], rz_recv.at[zi], dev) for pz, dev in z_peers]
    g_plain = scatter_plain(g_send, g_fin, back, t_right, t_left, y_right, y_left, cut_y)

    q_far = scatter_far(q_send, q_rin, grad_qk, x_far, px_right, px_left, cut_x)
    q_plain = scatter_plain(
        q_send, q_fin, grad_qk, x_right, x_left, px_right, px_left, cut_x
    )
    g_rest = scatter_relay(g_send, g_rin, g_fin, g_far, g_plain, y_right, y_left, cut_y)
    v_rest = scatter_relay(v_send, v_rin, v_fin, v_far, v_plain, px_right, px_left, cut_x)
    q_rest = scatter_relay(q_send, q_rin, q_fin, q_far, q_plain, px_right, px_left, cut_x)
    b_plain = scatter_plain(b_send, b_fin, branch, t_right, t_left, y_right, y_left, cut_y)
    b_rest = scatter_relay(b_send, b_rin, b_fin, b_far, b_plain, y_right, y_left, cut_y)

    mixed_own = x_full[t].astype(F32) + branch(t)
    gx_own = go_full[t].astype(F32) + back(t)
    v_own = grad_vo(xi)
    q_own = grad_qk(xi)

    for copy in g_rest:
        copy.wait_recv()
    gx = (gx_own + g_fin[0].astype(F32) + g_fin[1].astype(F32)).astype(BF)
    r, c = grid2(SPILL, SEQ)
    bsnd_next[...] = dot(hot(c == r + SEQ - tail), gx, 1, 1).astype(BF)
    bsnd_prev[...] = dot(hot(c == r), gx, 1, 1).astype(BF)
    back_next = remote(bsnd_next, bfrom_prev, dp_next)
    back_prev = remote(bsnd_prev, bfrom_next, dp_prev)

    def along_z(rest, mine, fin, slot):
        for copy in rest:
            copy.wait_recv()
        summed = mine + fin[0].astype(F32) + fin[1].astype(F32)
        z_send[slot] = summed.astype(BF).reshape(NZ, XROWS, COLS)
        return [remote(z_send.at[slot, pz], z_recv.at[slot, zi], dev) for pz, dev in z_peers]

    earlier = list(pending)
    pending.clear()
    vz_copies = along_z(v_rest, v_own, v_fin, 1)
    qz_copies = along_z(q_rest, q_own, q_fin, 0)

    rest = rz_send[zi].astype(F32)
    for copy in rz_copies:
        copy.wait_recv()
    for pz, _ in z_peers:
        rest = rest + rz_recv[pz].astype(F32)
    r, c = grid2(NX * XROWS, 2 * REST)
    mask = c < 0
    for k in range(NX):
        at = r - k * XROWS
        mask = mask | ((at >= 0) & (at < ZROWS) & (c == at + k * ZROWS))
        at = at - 8
        mask = mask | ((at >= 0) & (at < ZROWS) & (c == at + k * ZROWS + REST))
    rest = dot(hot(mask), rest.astype(BF)).astype(BF)
    rx_send[...] = rest.reshape(NX, XROWS, COLS)
    rx_copies = [
        remote(rx_send.at[px], rx_recv.at[xi], (px * 16 + inner, t))
        for px in (x_far, x_right, x_left)
    ]

    length = SEQ + upper - lower
    behind = jnp.maximum(-lower, 0)
    ahead = jnp.maximum(upper, 0)
    r, c = grid2(SEQ, SRC)
    mine = hot((r == c + lower) & (c >= behind) & (c < length - ahead))
    src_rows = dot(gx, mine)
    r, c = grid2(SPILL, SRC)
    pick_prev = hot((c == r) & (c < behind))
    pick_next = hot((r == c - (length - ahead)) & (c >= length - ahead) & (c < length))
    back_next.wait_recv()
    back_prev.wait_recv()
    src_rows = (
        src_rows + dot(bfrom_prev[...], pick_prev, 0, 0) + dot(bfrom_next[...], pick_next, 0, 0)
    )
    gpatch_ref[...] = src_rows.astype(BF)
    gpatch_copy = pltpu.make_async_copy(gpatch_ref, gpatch_out, lsem.at[6])
    gpatch_copy.start()

    for copy in earlier:
        copy.wait_send()
    for copy in b_rest:
        copy.wait_recv()
    mixed_ref[...] = (mixed_own + b_fin[0].astype(F32) + b_fin[1].astype(F32)).astype(BF)
    mixed_copy = pltpu.make_async_copy(mixed_ref, mixed_out, lsem.at[7])
    mixed_copy.start()

    last = rx_send[xi].astype(F32)
    for copy in rx_copies:
        copy.wait_recv()
    for px in (x_far, x_right, x_left):
        last = last + rx_recv[px].astype(F32)
    last = last * total_scale

    def finish(copies, slot):
        total = z_send[slot, zi].astype(F32)
        for copy in copies:
            copy.wait_recv()
        for pz, _ in z_peers:
            total = total + z_recv[slot, pz].astype(F32)
        return total * total_scale

    vo = finish(vz_copies, 1)
    qk = finish(qz_copies, 0)
    gqkv_ref[0, 0:XROWS] = qk[:, 0:QW]
    gqkv_ref[0, XROWS:SHARE] = last[0:ZROWS, 0:QW]
    gqkv_ref[1, 0:XROWS] = qk[:, QW : 2 * QW]
    gqkv_ref[1, XROWS:SHARE] = last[0:ZROWS, QW : 2 * QW]
    gqkv_ref[2, 0:XROWS] = vo[:, 0:QW]
    gqkv_ref[2, XROWS:SHARE] = last[8 : 8 + ZROWS, 0:QW]
    gwout_ref[0:XROWS] = vo[:, QW : 2 * QW]
    gwout_ref[XROWS:SHARE] = last[8 : 8 + ZROWS, QW : 2 * QW]

    for copy in pending:
        copy.wait_send()
    gpatch_copy.wait()
    mixed_copy.wait()


def hand_out(a, b, c, e, a_out, b_out, c_out, e_out):
    a_out[...] = a[...]
    b_out[...] = b[...]
    c_out[...] = c[...]
    e_out[...] = e[...]


COPIES = 88


def body(patches, seg_ids, cut, w_qkv, w_out, grad_out):
    vmem = pl.BlockSpec(memory_space=pltpu.VMEM)
    anym = pl.BlockSpec(memory_space=pl.ANY)
    halo = pltpu.VMEM((SPILL, COLS), BF)
    scratch = [
        pltpu.SMEM((1, 2), jnp.int32),
        pltpu.VMEM((1, SEQ), jnp.int32),
        pltpu.VMEM((COLS, SEQ), BF),
        pltpu.VMEM((COLS, SRC), BF),
        pltpu.VMEM((COLS, SRC), BF),
        pltpu.VMEM((3 * QW, MODEL), BF),
        pltpu.VMEM((QW, MODEL), BF),
        pltpu.VMEM((2, NT, COLS, SEQ), BF),
        pltpu.VMEM((NT, COLS, SEQ), BF),
        pltpu.VMEM((MODEL, 3 * QW), BF),
        pltpu.VMEM((MODEL, QW), BF),
        halo, halo, halo, halo, halo, halo, halo, halo,
        pltpu.VMEM((2, 3, COLS, SEQ), BF),
        pltpu.VMEM((2, COLS, SEQ), BF),
        pltpu.VMEM((2, 2, COLS, SEQ), BF),
        pltpu.VMEM((4, QW, SEQ), BF),
        pltpu.VMEM((4, QW, SEQ), BF),
        pltpu.VMEM((2, NX, KEPT, SEQ), BF),
        pltpu.VMEM((2, NX, KEPT, SEQ), BF),
        pltpu.VMEM((2, NX, KEPT, SEQ), BF),
        pltpu.VMEM((2 * NZ * REST, MODEL), BF),
        pltpu.VMEM((2, NZ * REST, SEQ), BF),
        pltpu.VMEM((2, NZ * REST, SEQ), BF),
        pltpu.VMEM((2, NZ * REST, SEQ), BF),
        pltpu.VMEM((2, 3, KEPT, COLS), BF),
        pltpu.VMEM((2, KEPT, COLS), BF),
        pltpu.VMEM((2, 2, KEPT, COLS), BF),
        pltpu.VMEM((2, NZ, XROWS, COLS), BF),
        pltpu.VMEM((2, NZ, XROWS, COLS), BF),
        pltpu.VMEM((NZ, 2 * REST, COLS), BF),
        pltpu.VMEM((NZ, 2 * REST, COLS), BF),
        pltpu.VMEM((NX, XROWS, COLS), BF),
        pltpu.VMEM((NX, XROWS, COLS), BF),
        pltpu.SemaphoreType.DMA((COPIES,)),
        pltpu.SemaphoreType.DMA((COPIES,)),
        pltpu.SemaphoreType.DMA((8,)),
    ]
    out_shape = (
        jax.ShapeDtypeStruct((COLS, SEQ), BF),
        jax.ShapeDtypeStruct((COLS, SRC), BF),
        jax.ShapeDtypeStruct((3, SHARE, QW), F32),
        jax.ShapeDtypeStruct((SHARE, QW), F32),
    )
    results = pl.pallas_call(
        kernel,
        out_shape=out_shape,
        in_specs=[anym, anym, anym, anym, anym, anym],
        out_specs=(anym, anym, vmem, vmem),
        scratch_shapes=scratch,
        compiler_params=pltpu.CompilerParams(
            collective_id=0, has_side_effects=True, vmem_limit_bytes=56 * 1024 * 1024
        ),
    )(cut, seg_ids.reshape(1, SEQ), patches.T, w_qkv.reshape(3 * QW, MODEL), w_out, grad_out.T)
    mixed, grad_patches, qkv_grad, out_grad = pl.pallas_call(
        hand_out,
        out_shape=out_shape,
        in_specs=[vmem, vmem, vmem, vmem],
        out_specs=(vmem, vmem, vmem, vmem),
    )(*results)
    return mixed.T, grad_patches.T, jnp.swapaxes(qkv_grad, 1, 2), out_grad.T


def solution(mesh):
    in_specs = (
        P("dp", "tensor"),
        P("dp"),
        P("dp", None),
        P(None, "tensor", None),
        P("tensor", None),
        P("dp", "tensor"),
    )
    out_specs = (P("dp", "tensor"), P("dp", "tensor"), P(None, "tensor", "dp"), P("tensor", "dp"))
    return jax.shard_map(body, mesh=mesh, in_specs=in_specs, out_specs=out_specs, check_vma=False)
```
